32 devices in a mesh: wide: 8 (over z, y), narrow: 4 (over x, core).
Axes of the slice: x: 2, y: 2, z: 4, core: 2. Of those that a mesh axis runs over, the one named last changes fastest.
Arguments:
- tokens: bfloat16 [34816, 768], P(('wide', 'narrow')), may hold values from -6 to 6
- cotangent: bfloat16 [34816, 768], P(('wide', 'narrow')), may hold values from -6 to 6
- latents: bfloat16 [34816, 16], P(('wide', 'narrow')), may hold values from -6 to 6
- added_noise: float32 [4, 16, 8192], P(None, None, ('wide', 'narrow')), may hold values from -6 to 6
- timesteps: int32 [4, 8192], P(None, ('wide', 'narrow')), may hold values from 0 to 999
- bucket: int32 [32], replicated, may hold values from 256 to 1024, as said below
- masked: int32 [32, 1088], P(('wide', 'narrow')), may hold values from 0 to 1, as said below
- deal_start: int32 [32], replicated, may hold values from 0 to 7
- first_gain: float32 [768], replicated, may hold values from 0.5 to 1.5
- first_shift: float32 [768], replicated, may hold values from -0.3125 to 0.3125
- joint_weight: bfloat16 [768, 2304], replicated, may hold values from -0.21875 to 0.21875
- query_value_bias: float32 [1536], replicated, may hold values from -0.3125 to 0.3125
- output_weight: bfloat16 [768, 768], replicated, may hold values from -1.5 to 1.5
- output_bias: float32 [768], replicated, may hold values from -0.3125 to 0.3125
- second_gain: float32 [768], replicated, may hold values from 0.5 to 1.5
- second_shift: float32 [768], replicated, may hold values from -0.3125 to 0.3125
- expand_weight: bfloat16 [768, 3072], replicated, may hold values from -0.21875 to 0.21875
- expand_bias: float32 [3072], replicated, may hold values from -1.25 to 1.25
- reduce_weight: bfloat16 [3072, 768], replicated, may hold values from -0.109375 to 0.109375
- reduce_bias: float32 [768], replicated, may hold values from -0.3125 to 0.3125
- input_proj: bfloat16 [1024, 16], replicated, may hold values from -1.5 to 1.5
- cond_proj: bfloat16 [768, 1024], replicated, may hold values from -0.21875 to 0.21875
- time_first: bfloat16 [256, 1024], replicated, may hold values from -0.375 to 0.375
- time_second: bfloat16 [1024, 1024], replicated, may hold values from -0.1875 to 0.1875
- block_mod: bfloat16 [1024, 3072], replicated, may hold values from -0.1875 to 0.1875
- block_expand: bfloat16 [1024, 1024], replicated, may hold values from -0.1875 to 0.1875
- block_reduce: bfloat16 [1024, 1024], replicated, may hold values from -0.1875 to 0.1875
- final_mod: bfloat16 [1024, 2048], replicated, may hold values from -0.1875 to 0.1875
- final_proj: bfloat16 [1024, 16], replicated, may hold values from -0.375 to 0.375
Outputs:
- block_output: bfloat16 [34816, 768], P(('wide', 'narrow'))
- noise_guess: float32 [4, 16, 8192], P(None, None, ('wide', 'narrow'))
- branch_spread: float32 [32, 2], P(('wide', 'narrow'))
- tokens_gradient: float32 [34816, 768], P(('wide', 'narrow'))
- first_gain_gradient: float32 [768], P('wide')
- first_shift_gradient: float32 [768], P('wide')
- joint_weight_gradient: float32 [768, 2304], P('wide')
- query_value_bias_gradient: float32 [1536], P('wide')
- output_weight_gradient: float32 [768, 768], P('wide')
- output_bias_gradient: float32 [768], P('wide')
- second_gain_gradient: float32 [768], P('wide')
- second_shift_gradient: float32 [768], P('wide')
- expand_weight_gradient: float32 [768, 3072], P('wide')
- expand_bias_gradient: float32 [3072], P('wide')
- reduce_weight_gradient: float32 [3072, 768], P('wide')
- reduce_bias_gradient: float32 [768], P('wide')
- input_proj_gradient: float32 [1024, 16], P('wide')
- cond_proj_gradient: float32 [768, 1024], P('wide')
- time_first_gradient: float32 [256, 1024], P('wide')
- time_second_gradient: float32 [1024, 1024], P('wide')
- block_mod_gradient: float32 [1024, 3072], P('wide')
- block_expand_gradient: float32 [1024, 1024], P('wide')
- block_reduce_gradient: float32 [1024, 1024], P('wide')
- final_mod_gradient: float32 [1024, 2048], P('wide')
- final_proj_gradient: float32 [1024, 16], P('wide')
The draws below stay inside these ranges and needn't reach their ends.
Inputs may be any that keep to these rules, and one draw needn't show every extreme that they name: `bucket`: each entry is 256 or 1024; among the images whose index has one remainder modulo 4, at least one has 1024. `masked`: row i has exactly bucket[i] * 256 // 1024 ones, all at positions 64 to 64 + bucket[i] - 1.
All inputs are finite; a program needn't handle non-finite values.
Results may differ from the reference program's by a relative error of at most 0.017.
Values may be sent and summed in bfloat16 or wider, within the bound.
No kernel may reach another device: no remote copies, remote signals or barrier semaphores. Data moves between devices by JAX's collectives and lax.ppermute only.
A program may use at most 320 MiB of HBM per device.

```python
import math
import jax
import jax.numpy as jnp
from jax import lax

D = 768
HEADS = 12
HEAD_DIM = 64
FF = 3072
DIFF_WIDTH = 1024
TOKEN_DIM = 16
BUFFER = 64
FREQ_DIM = 256
IMAGE_MAX = 1024
MASK_MAX = 256
REPEATS = 4
SEQ = 1088
IMAGES = 32
TOKENS = 34816
CAP = 32
SLOTS = 8192
N_WIDE = 8
N_NARROW = 4
DEVICES = 32


def bucket_sizes(key):
    base = jax.random.fold_in(key, 7)
    larger = jax.random.randint(jax.random.fold_in(base, 1), (N_WIDE, N_NARROW), 0, 2)
    picked = jax.random.randint(jax.random.fold_in(base, 2), (N_NARROW,), 0, N_WIDE)
    forced = (jnp.arange(N_WIDE)[:, None] == picked[None, :]).astype(jnp.int32)
    larger = jnp.maximum(larger, forced)
    sizes = IMAGE_MAX // 4 + larger * (IMAGE_MAX - IMAGE_MAX // 4)
    return sizes.reshape(-1).astype(jnp.int32)


def draw_bucket(key, part):
    return bucket_sizes(key)


def draw_masked(key, part):
    sizes = bucket_sizes(key)
    counts = sizes * MASK_MAX // IMAGE_MAX
    position = jnp.arange(SEQ).astype(jnp.int32)
    random_int = jax.random.randint(jax.random.fold_in(key, 23), (IMAGES, SEQ), 0, 2 ** 19)
    inside = (position[None, :] >= BUFFER) & (position[None, :] < BUFFER + sizes[:, None])
    score = jnp.where(inside, random_int * SEQ + position[None, :], 2 ** 30 + position[None, :])
    ranking = jnp.argsort(jnp.argsort(score, axis=1), axis=1)
    return (ranking < counts[:, None]).astype(jnp.int32)


def drawn_field(key, shape):
    return jax.random.truncated_normal(key, -6.0, 6.0, shape, jnp.float32)


def draw_tokens(key, part):
    key = jax.random.fold_in(key, 101)
    values = drawn_field(key, (TOKENS, D))
    return values.astype(jnp.bfloat16)


def draw_latents(key, part):
    key = jax.random.fold_in(key, 103)
    values = drawn_field(key, (TOKENS, TOKEN_DIM))
    return values.astype(jnp.bfloat16)


def draw_added_noise(key, part):
    key = jax.random.fold_in(key, 107)
    values = drawn_field(key, (REPEATS, TOKEN_DIM, SLOTS))
    return values.astype(jnp.float32)


def plant(drawn, stream_key, least, top_value):
    spot = [jax.random.randint(jax.random.fold_in(stream_key, axis), (), 0, length) for axis, length in enumerate(drawn.shape)]
    widest = drawn.shape.index(max(drawn.shape))
    neighbour = spot[:widest] + [(spot[widest] + 1) % drawn.shape[widest]] + spot[widest + 1:]
    return drawn.at[tuple(spot)].set(least).at[tuple(neighbour)].set(top_value)


def level_of(rng, dims, cuts, low, largest):
    def one(axis_at, parts):
        draws = jax.random.uniform(jax.random.fold_in(jax.random.fold_in(rng, 6), axis_at), (parts,), jnp.float32, low / len(cuts), largest / len(cuts))
        return jnp.repeat(jnp.exp(draws), dims[axis_at] // parts).reshape((-1,) + (1,) * (len(dims) - axis_at - 1))

    gain = one(*cuts[0])
    for cut in cuts[1:]:
        gain = gain * one(*cut)
    return gain


def noise(rng, shape, scale, reach, shards=(), dtype=jnp.bfloat16):
    gain = level_of(rng, shape, shards, -0.22, 0.18) if shards else 1.0
    values = jax.random.normal(rng, shape, jnp.float32) * scale * gain
    return jnp.minimum(jnp.maximum(values, -reach), reach).astype(dtype)


def setup_inputs(seed: int = 0) -> dict:
    key_list = jax.random.split(jax.random.key(seed), 30)
    return {
        "tokens": draw_tokens(jax.random.fold_in(key_list[29], 71), 0),
        "cotangent": noise(key_list[1], (TOKENS, D), 1.0, 6.0, ((0, 32),)),
        "latents": draw_latents(jax.random.fold_in(key_list[29], 71), 0),
        "added_noise": draw_added_noise(jax.random.fold_in(key_list[29], 71), 0),
        "timesteps": plant(jax.random.randint(key_list[4], (REPEATS, SLOTS), 0, 1000), jax.random.fold_in(key_list[4], 1), 0, 999).astype(jnp.int32),
        "bucket": draw_bucket(jax.random.fold_in(key_list[29], 71), 0),
        "masked": draw_masked(jax.random.fold_in(key_list[29], 71), 0),
        "deal_start": plant(jax.random.randint(key_list[7], (IMAGES,), 0, N_WIDE), jax.random.fold_in(key_list[7], 1), 0, N_WIDE - 1).astype(jnp.int32),
        "first_gain": jnp.clip(1.0 + 0.1 * jax.random.normal(key_list[8], (D,), jnp.float32), 0.5, 1.5),
        "first_shift": noise(key_list[9], (D,), 0.05, 0.3125, (), jnp.float32),
        "joint_weight": noise(key_list[10], (D, 3 * D), D ** -0.5, 0.21875),
        "query_value_bias": noise(key_list[11], (2 * D,), 0.05, 0.3125, (), jnp.float32),
        "output_weight": noise(key_list[12], (D, D), 16 ** -0.5, 1.5),
        "output_bias": noise(key_list[13], (D,), 0.05, 0.3125, (), jnp.float32),
        "second_gain": jnp.clip(1.0 + 0.1 * jax.random.normal(key_list[14], (D,), jnp.float32), 0.5, 1.5),
        "second_shift": noise(key_list[15], (D,), 0.05, 0.3125, (), jnp.float32),
        "expand_weight": noise(key_list[16], (D, FF), D ** -0.5, 0.21875),
        "expand_bias": noise(key_list[17], (FF,), 0.2, 1.25, (), jnp.float32),
        "reduce_weight": noise(key_list[18], (FF, D), FF ** -0.5, 0.109375),
        "reduce_bias": noise(key_list[19], (D,), 0.05, 0.3125, (), jnp.float32),
        "input_proj": noise(key_list[20], (DIFF_WIDTH, TOKEN_DIM), TOKEN_DIM ** -0.5, 1.5),
        "cond_proj": noise(key_list[21], (D, DIFF_WIDTH), D ** -0.5, 0.21875),
        "time_first": noise(key_list[22], (FREQ_DIM, DIFF_WIDTH), FREQ_DIM ** -0.5, 0.375),
        "time_second": noise(key_list[23], (DIFF_WIDTH, DIFF_WIDTH), DIFF_WIDTH ** -0.5, 0.1875),
        "block_mod": noise(key_list[24], (DIFF_WIDTH, 3 * DIFF_WIDTH), DIFF_WIDTH ** -0.5, 0.1875),
        "block_expand": noise(key_list[25], (DIFF_WIDTH, DIFF_WIDTH), DIFF_WIDTH ** -0.5, 0.1875),
        "block_reduce": noise(key_list[26], (DIFF_WIDTH, DIFF_WIDTH), DIFF_WIDTH ** -0.5, 0.1875),
        "final_mod": noise(key_list[27], (DIFF_WIDTH, 2 * DIFF_WIDTH), DIFF_WIDTH ** -0.5, 0.1875),
        "final_proj": noise(key_list[28], (DIFF_WIDTH, TOKEN_DIM), (DIFF_WIDTH // 4) ** -0.5, 0.375),
    }


@jax.custom_vjp
def low(v):
    return lax.optimization_barrier(v.astype(jnp.bfloat16)).astype(jnp.float32)

@jax.custom_vjp
def low_back(v):
    return v

def low_keep(v):
    return (low(v), None)

def low_pass(kept, grad):
    return (grad,)

def back_keep(v):
    return (v, None)

def back_low(kept, grad):
    return (low(grad),)
low.defvjp(low_keep, low_pass)
low_back.defvjp(back_keep, back_low)
HIGHEST = lax.Precision.HIGHEST
SHIFT_ANGLE = 0.008 / 1.008 * math.pi / 2.0
STEP_ANGLE = math.pi / (2.0 * 1.008 * 1000.0)

def layer_norm(values):
    centre = values - lax.optimization_barrier(jnp.mean(values, axis=-1, keepdims=True))
    spread = lax.optimization_barrier(jnp.mean(centre * centre, axis=-1, keepdims=True))
    return centre * lax.rsqrt(spread + 1e-06)

def product(left, right):
    return jnp.dot(left, right, precision=HIGHEST)

def vit_image(weights, image, length):
    first_gain, first_shift, joint_weight, query_value_bias, output_weight, output_bias, second_gain, second_shift, expand_weight, expand_bias, reduce_weight, reduce_bias = weights
    keep = (jnp.arange(SEQ) < length).astype(jnp.float32)
    first_in = low(layer_norm(image) * first_gain + first_shift)
    joint = product(first_in, joint_weight)
    query = low_back(low(joint[:, :D] + query_value_bias[:D])).reshape(SEQ, HEADS, HEAD_DIM)
    keys = low_back(low(joint[:, D:2 * D])).reshape(SEQ, HEADS, HEAD_DIM)
    values = low_back(low(joint[:, 2 * D:] + query_value_bias[D:])).reshape(SEQ, HEADS, HEAD_DIM)
    scores = low_back(jnp.einsum('qhd,khd->hqk', query, keys, precision=HIGHEST) * HEAD_DIM ** (-0.5))
    scores = jnp.where(keep[None, None, :] > 0.5, scores, -1e+30)
    probs = low(jax.nn.softmax(scores, axis=-1))
    mixed = jnp.einsum('hqk,khd->qhd', probs, values, precision=HIGHEST).reshape(SEQ, D)
    mixed = low_back(low(mixed))
    branch = low_back(product(mixed, output_weight) + output_bias)
    middle = image + branch
    second_in = low(layer_norm(middle) * second_gain + second_shift)
    hidden = low_back(product(second_in, expand_weight) + expand_bias)
    active = low(jax.nn.gelu(hidden, approximate=False))
    feed = low_back(product(active, reduce_weight) + reduce_bias)
    result = (middle + feed) * keep[:, None]
    count = length.astype(jnp.float32) * D
    spread = jnp.stack([jnp.sqrt(jnp.sum(keep[:, None] * branch * branch) / count), jnp.sqrt(jnp.sum(keep[:, None] * feed * feed) / count)])
    return (result, spread)

def diffusion_block(weights, rows, start, noise_part, steps, live):
    input_proj, cond_proj, time_first, time_second, block_mod, block_expand, block_reduce, final_mod, final_proj = weights
    width = DIFF_WIDTH
    rows = low_back(low(rows))
    embed = low_back(product(rows, cond_proj))
    steps_float = steps.astype(jnp.float32)
    half = FREQ_DIM // 2
    freqs = jnp.exp(-math.log(10000.0) * jnp.arange(half).astype(jnp.float32) / half)
    angles = steps_float[:, :, None] * freqs
    sinus = low(jnp.concatenate([jnp.cos(angles), jnp.sin(angles)], axis=-1))
    first = low_back(jnp.einsum('rsf,fw->rsw', sinus, time_first, precision=HIGHEST))
    timed = low_back(jnp.einsum('rsw,wv->rsv', low(jax.nn.silu(first)), time_second, precision=HIGHEST))
    cond_all = embed[None] + timed
    acted = low(jax.nn.silu(cond_all))
    modul = low_back(jnp.einsum('rsw,wv->rsv', acted, block_mod, precision=HIGHEST))
    finmod = low_back(jnp.einsum('rsw,wv->rsv', acted, final_mod, precision=HIGHEST))
    shift_a = modul[..., :width]
    scale_a = modul[..., width:2 * width]
    gate_a = modul[..., 2 * width:]
    shift_b = finmod[..., :width]
    scale_b = finmod[..., width:]
    offset = steps_float * STEP_ANGLE
    keep_sig = jnp.cos(offset + SHIFT_ANGLE) / math.cos(SHIFT_ANGLE)
    drop_sig = jnp.sqrt(jnp.sin(offset) * jnp.sin(offset + 2.0 * SHIFT_ANGLE)) / math.cos(SHIFT_ANGLE)
    noisy = low(keep_sig[:, None, :] * start.T[None] + drop_sig[:, None, :] * noise_part)
    entry = low_back(jnp.einsum('rcs,wc->rsw', noisy, input_proj, precision=HIGHEST))
    inner = low(layer_norm(entry) * (1.0 + scale_a) + shift_a)
    upper = low_back(jnp.einsum('rsw,wv->rsv', inner, block_expand, precision=HIGHEST))
    lifted = low(jax.nn.silu(upper))
    branch = low_back(jnp.einsum('rsw,wv->rsv', lifted, block_reduce, precision=HIGHEST))
    after = entry + gate_a * branch
    last = low(layer_norm(after) * (1.0 + scale_b) + shift_b)
    guess = low_back(jnp.einsum('rsw,wc->rcs', last, final_proj, precision=HIGHEST)) * live[None, None, :]
    miss = guess - noise_part * live[None, None, :]
    return (jnp.sum(miss * miss) / REPEATS, guess)

def reference(tokens, cotangent, latents, added_noise, timesteps, bucket, masked, deal_start, first_gain, first_shift, joint_weight, query_value_bias, output_weight, output_bias, second_gain, second_shift, expand_weight, expand_bias, reduce_weight, reduce_bias, input_proj, cond_proj, time_first, time_second, block_mod, block_expand, block_reduce, final_mod, final_proj):
    floats = tuple((item.astype(jnp.float32) for item in (first_gain, first_shift, joint_weight, query_value_bias, output_weight, output_bias, second_gain, second_shift, expand_weight, expand_bias, reduce_weight, reduce_bias, input_proj, cond_proj, time_first, time_second, block_mod, block_expand, block_reduce, final_mod, final_proj)))
    lengths = (BUFFER + bucket).astype(jnp.int32)
    order = (jnp.cumsum(masked, axis=1) - 1).astype(jnp.int32)
    image_ids = jnp.arange(IMAGES).astype(jnp.int32)
    wide_of = image_ids // N_NARROW
    narrow_of = image_ids % N_NARROW
    target_wide = (deal_start[:, None] + order) % N_WIDE
    target = ((target_wide * N_NARROW + narrow_of[:, None]) * N_WIDE + wide_of[:, None]) * CAP + order // N_WIDE
    target = jnp.where(masked > 0, target, SLOTS).astype(jnp.int32).reshape(-1)
    live = jnp.zeros((SLOTS + 1,), jnp.float32).at[target].set(1.0)[:SLOTS]
    dealt_latent = jnp.zeros((SLOTS + 1, TOKEN_DIM), jnp.float32).at[target].set(latents.astype(jnp.float32).reshape(TOKENS, TOKEN_DIM))[:SLOTS]
    noise_blocks = added_noise.astype(jnp.float32).reshape(REPEATS, TOKEN_DIM, DEVICES, MASK_MAX).transpose(2, 0, 1, 3)
    step_blocks = timesteps.reshape(REPEATS, DEVICES, MASK_MAX).transpose(1, 0, 2)
    cot_float = cotangent.astype(jnp.float32).reshape(TOKENS, D)

    def forward(weights, inputs):
        vit_part = weights[:12]
        head_part = weights[12:]

        def image_step(carry, item):
            image, length = item
            result, spread = jax.checkpoint(vit_image)(vit_part, image, length)
            return (carry, (result, spread))
        unused, (results, spreads) = lax.scan(image_step, None, (inputs.reshape(IMAGES, SEQ, D), lengths))
        flat = results.reshape(TOKENS, D)
        dealt = jnp.zeros((SLOTS + 1, D), jnp.float32).at[target].set(flat)[:SLOTS]

        def head_step(total, item):
            rows, start, noise_part, steps, alive = item
            loss, guess = jax.checkpoint(diffusion_block)(head_part, rows, start, noise_part, steps, alive)
            return (total + loss, guess)
        loss, guesses = lax.scan(head_step, jnp.zeros((), jnp.float32), (dealt.reshape(DEVICES, MASK_MAX, D), dealt_latent.reshape(DEVICES, MASK_MAX, TOKEN_DIM), noise_blocks, step_blocks, live.reshape(DEVICES, MASK_MAX)))
        total = jnp.sum(flat * cot_float) + loss
        return (total, (flat, guesses, spreads))
    total, pullback, extra = jax.vjp(forward, floats, tokens.astype(jnp.float32), has_aux=True)
    weight_grads, token_grad = pullback(jnp.ones_like(total))
    flat, guesses, spreads = extra
    noise_guess = guesses.transpose(1, 2, 0, 3).reshape(REPEATS, TOKEN_DIM, SLOTS)
    g_first_gain, g_first_shift, g_joint, g_qv_bias, g_output, g_output_bias, g_second_gain, g_second_shift, g_expand, g_expand_bias, g_reduce, g_reduce_bias, g_input, g_cond, g_time_first, g_time_second, g_block_mod, g_block_expand, g_block_reduce, g_final_mod, g_final_proj = weight_grads
    return (flat.astype(jnp.bfloat16), noise_guess, spreads, token_grad, g_first_gain, g_first_shift, g_joint, g_qv_bias, g_output, g_output_bias, g_second_gain, g_second_shift, g_expand, g_expand_bias, g_reduce, g_reduce_bias, g_input, g_cond, g_time_first, g_time_second, g_block_mod, g_block_expand, g_block_reduce, g_final_mod, g_final_proj)
```

```python
from functools import partial
import math

import jax
import jax.numpy as jnp
from jax import lax
from jax.experimental import pallas as pl
from jax.experimental.pallas import tpu as pltpu
from jax.sharding import PartitionSpec as P

D = 768
HEADS = 12
HEAD_DIM = 64
TOKEN_DIM = 16
BUFFER = 64
IMAGE_MAX = 1024
MASK_MAX = 256
REPEATS = 4
SEQ = 1088


SHIFT_ANGLE = 0.008 / 1.008 * math.pi / 2.0
STEP_ANGLE = math.pi / (2.0 * 1.008 * 1000.0)


def for_sending(shard):
    return jax.tree.map(lambda a: a.astype(jnp.bfloat16) if a.dtype == jnp.float32 else a, shard)


def matmul(left, right):
    return jnp.dot(left, right, preferred_element_type=jnp.float32)


def contract_rows(left, right):
    return lax.dot_general(
        left, right, (((0,), (0,)), ((), ())), preferred_element_type=jnp.float32
    )


def contract_last(left, right):
    return lax.dot_general(
        left, right, (((1,), (1,)), ((), ())), preferred_element_type=jnp.float32
    )


def normalize(values):
    centre = values - jnp.mean(values, axis=-1, keepdims=True)
    inverse = lax.rsqrt(jnp.mean(centre * centre, axis=-1, keepdims=True) + 1e-06)
    return (centre * inverse, inverse)


def normalize_back(grad_normed, normed, inverse):
    return inverse * (
        grad_normed
        - jnp.mean(grad_normed, axis=-1, keepdims=True)
        - normed * jnp.mean(grad_normed * normed, axis=-1, keepdims=True)
    )


def silu_back(before, grad_after):
    sigma = jax.nn.sigmoid(before)
    return grad_after * sigma * (1.0 + before * (1.0 - sigma))


PAIRS = 6
VM=60*1024*1024

def nt(a,b): return lax.dot_general(a,b,(((1,),(1,)),((),())),preferred_element_type=jnp.float32)
def nn(a,b): return jnp.dot(a,b,preferred_element_type=jnp.float32)
def tn(a,b): return lax.dot_general(a,b,(((0,),(0,)),((),())),preferred_element_type=jnp.float32)

def fwd_kernel(QB, len_ref, q_ref, k_ref, v_ref, o_ref, lse_ref):
    length=len_ref[0]
    low=lax.broadcasted_iota(jnp.int32,(1,128),1)<64
    bias=jnp.where(lax.broadcasted_iota(jnp.int32,(1,SEQ),1)<length,0.0,-1e30).astype(jnp.float32)
    k=k_ref[...]; v=v_ref[...]
    one=jnp.ones((),v.dtype); zero=jnp.zeros((),v.dtype)
    vs=(jnp.where(low,v,one),jnp.where(low,one,v))
    for b in range(SEQ//QB):
        rows=pl.ds(b*QB,QB)
        q=q_ref[rows,:]
        outs=[];lses=[]
        for h in range(2):
            qh=jnp.where(low,q,zero) if h==0 else jnp.where(low,zero,q)
            s=nt(qh,k)+bias
            top=jnp.max(s,axis=1,keepdims=True)
            p=jnp.exp(s-top).astype(jnp.bfloat16)
            o=nn(p,vs[h])
            total=pltpu.roll(o,64,1)
            outs.append(o/total)
            lses.append(top+jnp.log(total))
        o_ref[rows,:]=jnp.where(low,outs[0],outs[1]).astype(jnp.bfloat16)
        lse_ref[rows,:]=jnp.where(low,lses[0],lses[1])

def attend(joint,length,QB=272):
    spec=lambda off: pl.BlockSpec((SEQ,128),lambda i,off=off:(0,i+off))
    return pl.pallas_call(partial(fwd_kernel,QB),
        grid=(PAIRS,),
        in_specs=[pl.BlockSpec(memory_space=pltpu.SMEM),spec(0),spec(6),spec(12)],
        out_specs=[spec(0),spec(0)],
        out_shape=[jax.ShapeDtypeStruct((SEQ,D),jnp.bfloat16),jax.ShapeDtypeStruct((SEQ,D),jnp.float32)],
        compiler_params=pltpu.CompilerParams(vmem_limit_bytes=VM),
        cost_estimate=pl.CostEstimate(flops=4*SEQ*SEQ*D,bytes_accessed=SEQ*D*12,transcendentals=SEQ*SEQ*12),
        name='attend')(length,joint,joint,joint)

def bwd_kernel(KB,MODE,len_ref,q_ref,k_ref,v_ref,do_ref,o_ref,lse_ref,dq_ref,dk_ref,dv_ref,ds_ref):
    length=len_ref[0]
    low=lax.broadcasted_iota(jnp.int32,(1,128),1)<64
    q=q_ref[...]; do=do_ref[...]
    zero=jnp.zeros((),q.dtype)
    prod=do.astype(jnp.float32)*o_ref[...].astype(jnp.float32)
    prodT=prod.T
    lseT=lse_ref[...].T
    deltas=(jnp.sum(prodT[:64],axis=0,keepdims=True),jnp.sum(prodT[64:],axis=0,keepdims=True))
    lses=(lseT[0:1],lseT[64:65])
    for b in range(SEQ//KB):
        rows=pl.ds(b*KB,KB)
        k=k_ref[rows,:]; v=v_ref[rows,:]
        bias=jnp.where(lax.broadcasted_iota(jnp.int32,(KB,1),0)+b*KB<length,0.0,-1e30).astype(jnp.float32)
        dks=[];dvs=[]
        for h in range(2):
            pick=(lambda a: jnp.where(low,a,zero)) if h==0 else (lambda a: jnp.where(low,zero,a))
            s=nt(pick(k),q)+bias
            p=jnp.exp(s-lses[h])
            dp=nt(pick(v),do)
            ds=(p*(dp-deltas[h])).astype(jnp.bfloat16)
            dvs.append(nn(p.astype(jnp.bfloat16),do))
            dks.append(nn(ds,q))
            ds_ref[h,rows,:]=ds
        dk_ref[rows,:]=jnp.where(low,dks[0],dks[1]).astype(jnp.bfloat16)
        dv_ref[rows,:]=jnp.where(low,dvs[0],dvs[1]).astype(jnp.bfloat16)
    if MODE=='tn':
        dq=[tn(ds_ref[h],k_ref[...]) for h in range(2)]
        dq_ref[...]=(jnp.where(low,dq[0],dq[1])*0.125).astype(jnp.bfloat16)
    else:
        kT=k_ref[...].astype(jnp.float32).T.astype(jnp.bfloat16)
        dqT=jnp.concatenate([nn(kT[64*h:64*h+64],ds_ref[h]) for h in range(2)],axis=0)
        dq_ref[...]=(dqT.T*0.125).astype(jnp.bfloat16)

def attend_back(joint,do,o,lse,length,KB=544,MODE='kt'):
    spec=lambda off: pl.BlockSpec((SEQ,128),lambda i,off=off:(0,i+off))
    return pl.pallas_call(partial(bwd_kernel,KB,MODE),
        grid=(PAIRS,),
        in_specs=[pl.BlockSpec(memory_space=pltpu.SMEM),spec(0),spec(6),spec(12),spec(0),spec(0),spec(0)],
        out_specs=[spec(0)]*3,
        out_shape=[jax.ShapeDtypeStruct((SEQ,D),jnp.bfloat16)]*3,
        scratch_shapes=[pltpu.VMEM((2,SEQ,SEQ),jnp.bfloat16)],
        compiler_params=pltpu.CompilerParams(vmem_limit_bytes=VM),
        cost_estimate=pl.CostEstimate(flops=10*SEQ*SEQ*D,bytes_accessed=SEQ*D*18,transcendentals=SEQ*SEQ*12),
        name='attend_back')(length,joint,joint,joint,do,o,lse)


def add_up(terms):
    total = terms[0].astype(jnp.float32)
    for term in terms[1:]:
        total = total + term.astype(jnp.float32)
    return total


def swap(array, axis, mask):
    count = lax.axis_size(axis)
    return lax.ppermute(array, axis, [(i, i ^ mask) for i in range(count)])


def bit(label):
    return lax.axis_index(label[0]) // label[1] % 2


def behind(value, *others):
    return lax.optimization_barrier((value,) + others)[0]


class Flow:
    def __init__(self, whole):
        wide, narrow = lax.axis_size("wide"), lax.axis_size("narrow")
        labels = [("wide", 1 << b) for b in reversed(range(wide.bit_length() - 1))]
        labels += [("narrow", 1 << b) for b in reversed(range(narrow.bit_length() - 1))]
        rows = whole.shape[0] // (wide * narrow)
        first = [("narrow", 1 << b) for b in range(1, narrow.bit_length() - 1)] + [("wide", 1)]
        cut = whole.shape[1] // 256 * 128
        whole = whole.reshape((2,) * len(labels) + (rows,) + whole.shape[1:])
        self.lanes = [
            {"cols": (0, cut), "order": first},
            {"cols": (cut, whole.shape[-1]), "order": first[::-1]},
        ]
        self.labels = labels
        self.terms = [whole]
        self.count = len(first)
        self.steps = self.run()

    def step(self):
        return next(self.steps)

    def take(self, term, labels, picks):
        labels = list(labels)
        for label, value in picks:
            term = lax.dynamic_index_in_dim(term, value, labels.index(label), keepdims=False)
            labels.remove(label)
        return term

    def halve(self, terms, labels, label):
        mine = bit(label)
        sent = add_up([self.take(t, labels, [(label, 1 - mine)]) for t in terms])
        got = swap(sent.astype(jnp.bfloat16), *label)
        kept = [self.take(t, labels, [(label, mine)]) for t in terms]
        return kept + [got], [l for l in labels if l != label], got

    def run(self):
        terms, labels, got = self.halve(self.terms, self.labels, ("narrow", 1))
        yield (got,)
        lanes = []
        for lane in self.lanes:
            lanes.append(([t[..., lane["cols"][0] : lane["cols"][1]] for t in terms], labels))
        for turn in range(self.count):
            arrived = []
            for i, lane in enumerate(self.lanes):
                terms, labels, got = self.halve(*lanes[i], lane["order"][turn])
                lanes[i] = (terms, labels)
                arrived.append(got)
            yield tuple(arrived)
        labels = lanes[0][1]
        axis = labels[0][0]
        arrived = []
        for pick in range(1 << len(labels)):
            mask = sum(label[1] for i, label in enumerate(labels) if pick >> i & 1)
            picks = [(l, (1 - bit(l)) if mask & l[1] else bit(l)) for l in labels]
            part = jnp.concatenate(
                [
                    add_up([self.take(t, labels, picks) for t in terms]).astype(jnp.bfloat16)
                    for terms, labels in lanes
                ],
                axis=-1,
            )
            if mask:
                arrived.append(swap(part, axis, mask))
            else:
                own = part
        yield tuple(arrived)
        share = add_up([own] + arrived).astype(jnp.bfloat16)
        count = lax.axis_size("narrow")
        stack = share[None]
        mask = count // 2
        while mask:
            got = swap(stack, "narrow", mask)
            yield (got,)
            low = bit(("narrow", mask)) == 0
            stack = jnp.concatenate(
                [jnp.where(low, stack, got), jnp.where(low, got, stack)], axis=0
            )
            mask //= 2
        half = int(math.log2(count))
        shape = stack.shape[1:]
        stack = stack.reshape((2,) * half + shape)
        stack = stack.transpose(tuple(reversed(range(half))) + (half, half + 1))
        self.result = stack.reshape((count,) + shape)
        yield ()


def small_sum(rows):
    narrow, wide = lax.axis_size("narrow"), lax.axis_size("wide")
    low = rows.astype(jnp.bfloat16)
    low = add_up([low] + [swap(low, "narrow", m) for m in range(1, narrow)]).astype(jnp.bfloat16)
    place = lax.axis_index("wide")
    parts = [lax.dynamic_index_in_dim(low, place ^ m, 0, keepdims=False) for m in range(wide)]
    return add_up(parts[:1] + [swap(parts[m], "wide", m) for m in range(1, wide)])


def diffusion_pass(rows, latent, noise_part, steps, live, weights):
    (
        input_proj,
        cond_proj,
        time_first,
        time_second,
        block_mod,
        block_expand,
        block_reduce,
        final_mod,
        final_proj,
    ) = weights
    width = cond_proj.shape[1]
    embed = matmul(rows, cond_proj)
    half = time_first.shape[0] // 2
    freqs = jnp.exp(-math.log(10000.0) * jnp.arange(half).astype(jnp.float32) / half)
    angles = steps[:, :, None] * freqs
    sinus = jnp.concatenate([jnp.cos(angles), jnp.sin(angles)], axis=-1).astype(jnp.bfloat16)
    first = jnp.einsum("rsf,fw->rsw", sinus, time_first, preferred_element_type=jnp.float32)
    first_low = jax.nn.silu(first).astype(jnp.bfloat16)
    timed = jnp.einsum("rsw,wv->rsv", first_low, time_second, preferred_element_type=jnp.float32)
    cond_all = embed[None] + timed
    acted = jax.nn.silu(cond_all).astype(jnp.bfloat16)
    modul = jnp.einsum("rsw,wv->rsv", acted, block_mod, preferred_element_type=jnp.float32)
    finmod = jnp.einsum("rsw,wv->rsv", acted, final_mod, preferred_element_type=jnp.float32)
    shift_a = modul[..., :width]
    scale_a = modul[..., width : 2 * width]
    gate_a = modul[..., 2 * width :]
    shift_b = finmod[..., :width]
    scale_b = finmod[..., width:]
    offset = steps * STEP_ANGLE
    keep_sig = jnp.cos(offset + SHIFT_ANGLE) / math.cos(SHIFT_ANGLE)
    drop_sig = jnp.sqrt(jnp.sin(offset) * jnp.sin(offset + 2.0 * SHIFT_ANGLE)) / math.cos(
        SHIFT_ANGLE
    )
    noisy = (
        keep_sig[:, None, :] * latent.astype(jnp.float32).T[None]
        + drop_sig[:, None, :] * noise_part
    ).astype(jnp.bfloat16)
    entry = jnp.einsum("rcs,wc->rsw", noisy, input_proj, preferred_element_type=jnp.float32)
    inner_normed, inner_inverse = normalize(entry)
    inner = (inner_normed * (1.0 + scale_a) + shift_a).astype(jnp.bfloat16)
    upper = jnp.einsum("rsw,wv->rsv", inner, block_expand, preferred_element_type=jnp.float32)
    lifted = jax.nn.silu(upper).astype(jnp.bfloat16)
    branch = jnp.einsum("rsw,wv->rsv", lifted, block_reduce, preferred_element_type=jnp.float32)
    after = entry + gate_a * branch
    last_normed, last_inverse = normalize(after)
    last = (last_normed * (1.0 + scale_b) + shift_b).astype(jnp.bfloat16)
    masking = live[None, None, :]
    guess = (
        jnp.einsum("rsw,wc->rcs", last, final_proj, preferred_element_type=jnp.float32) * masking
    )
    miss = guess - noise_part * masking
    grad_guess = (2.0 / REPEATS * miss * masking).astype(jnp.bfloat16)
    final_proj_grad = jnp.einsum(
        "rsw,rcs->wc", last, grad_guess, preferred_element_type=jnp.float32
    )
    grad_last = jnp.einsum(
        "rcs,wc->rsw", grad_guess, final_proj, preferred_element_type=jnp.float32
    )
    grad_scale_b = grad_last * last_normed
    grad_after = normalize_back(grad_last * (1.0 + scale_b), last_normed, last_inverse)
    grad_gate = grad_after * branch
    grad_branch = (grad_after * gate_a).astype(jnp.bfloat16)
    block_reduce_grad = jnp.einsum(
        "rsw,rsv->wv", lifted, grad_branch, preferred_element_type=jnp.float32
    )
    grad_lifted = jnp.einsum(
        "rsv,wv->rsw", grad_branch, block_reduce, preferred_element_type=jnp.float32
    )
    grad_upper = silu_back(upper, grad_lifted).astype(jnp.bfloat16)
    block_expand_grad = jnp.einsum(
        "rsw,rsv->wv", inner, grad_upper, preferred_element_type=jnp.float32
    )
    grad_inner = jnp.einsum(
        "rsv,wv->rsw", grad_upper, block_expand, preferred_element_type=jnp.float32
    )
    grad_scale_a = grad_inner * inner_normed
    grad_entry = (
        grad_after + normalize_back(grad_inner * (1.0 + scale_a), inner_normed, inner_inverse)
    ).astype(jnp.bfloat16)
    input_proj_grad = jnp.einsum(
        "rsw,rcs->wc", grad_entry, noisy, preferred_element_type=jnp.float32
    )
    grad_modul = jnp.concatenate([grad_inner, grad_scale_a, grad_gate], axis=-1).astype(
        jnp.bfloat16
    )
    grad_finmod = jnp.concatenate([grad_last, grad_scale_b], axis=-1).astype(jnp.bfloat16)
    final_mod_grad = jnp.einsum(
        "rsw,rsv->wv", acted, grad_finmod, preferred_element_type=jnp.float32
    )
    flow_one = Flow(
        jnp.concatenate(
            [g.astype(jnp.bfloat16) for g in (final_mod_grad, block_reduce_grad, block_expand_grad)],
            axis=1,
        )
    )
    grad_modul = behind(grad_modul, *flow_one.step())
    one = flow_one.step()
    grad_acted = jnp.einsum(
        "rsv,wv->rsw", grad_modul, block_mod, preferred_element_type=jnp.float32
    ) + jnp.einsum("rsv,wv->rsw", grad_finmod, final_mod, preferred_element_type=jnp.float32)
    grad_cond = silu_back(cond_all, grad_acted)
    grad_timed = grad_cond.astype(jnp.bfloat16)
    grad_embed = jnp.sum(grad_cond, axis=0).astype(jnp.bfloat16)
    grad_rows = contract_last(grad_embed, cond_proj)
    time_second_grad = jnp.einsum(
        "rsw,rsv->wv", first_low, grad_timed, preferred_element_type=jnp.float32
    )
    grad_first = silu_back(
        first,
        jnp.einsum("rsv,wv->rsw", grad_timed, time_second, preferred_element_type=jnp.float32),
    ).astype(jnp.bfloat16)
    time_first_grad = jnp.einsum(
        "rsf,rsw->fw", sinus, grad_first, preferred_element_type=jnp.float32
    )
    cond_proj_grad = contract_rows(rows, grad_embed)
    acted_later = behind(acted, *one)
    one = flow_one.step()
    block_mod_grad = jnp.einsum(
        "rsw,rsv->wv", acted_later, grad_modul, preferred_element_type=jnp.float32
    )
    total = lax.axis_size("wide") * lax.axis_size("narrow")

    def chunked(grad):
        return grad.astype(jnp.bfloat16).reshape(total, -1, grad.shape[1])

    mixed_rows = jnp.concatenate([chunked(cond_proj_grad), chunked(time_first_grad)], axis=1)
    flow_two = Flow(
        jnp.concatenate(
            [
                block_mod_grad.astype(jnp.bfloat16),
                time_second_grad.astype(jnp.bfloat16),
                mixed_rows.reshape(-1, width),
            ],
            axis=1,
        )
    )
    two = flow_two.step()
    return (guess, grad_rows, (input_proj_grad, final_proj_grad), (flow_one, one), (flow_two, two))


def shards(
    tokens,
    cotangent,
    latents,
    added_noise,
    timesteps,
    bucket,
    masked,
    deal_start,
    first_gain,
    first_shift,
    joint_weight,
    query_value_bias,
    output_weight,
    output_bias,
    second_gain,
    second_shift,
    expand_weight,
    expand_bias,
    reduce_weight,
    reduce_bias,
    input_proj,
    cond_proj,
    time_first,
    time_second,
    block_mod,
    block_expand,
    block_reduce,
    final_mod,
    final_proj,
):
    wide_count = lax.axis_size("wide")
    narrow_count = lax.axis_size("narrow")
    capacity = MASK_MAX // wide_count
    place_wide = lax.axis_index("wide")
    place_narrow = lax.axis_index("narrow")
    image_index = place_wide * narrow_count + place_narrow
    length = BUFFER + bucket[image_index]
    keep_keys = jnp.arange(SEQ) < length
    keep_rows = keep_keys.astype(jnp.float32)[:, None]
    scale = HEAD_DIM ** (-0.5)
    image = tokens.astype(jnp.float32)
    first_normed, first_inverse = normalize(image)
    first_in = (first_normed * first_gain + first_shift).astype(jnp.bfloat16)
    joint = matmul(first_in, joint_weight)
    joint_bias = jnp.concatenate([query_value_bias[:D], jnp.zeros((D,), jnp.float32), query_value_bias[D:]])
    joint_scale = jnp.where(jnp.arange(3 * D) < D, scale, 1.0)
    joint_low = ((joint + joint_bias).astype(jnp.bfloat16) * joint_scale.astype(jnp.bfloat16))
    mixed, logsum = attend(joint_low, length[None])
    branch = matmul(mixed, output_weight) + output_bias
    middle = image + branch
    second_normed, second_inverse = normalize(middle)
    second_in = (second_normed * second_gain + second_shift).astype(jnp.bfloat16)
    hidden = matmul(second_in, expand_weight) + expand_bias
    active, gelu_back = jax.vjp(partial(jax.nn.gelu, approximate=False), hidden)
    active_low = active.astype(jnp.bfloat16)
    feed = matmul(active_low, reduce_weight) + reduce_bias
    result = (middle + feed) * keep_rows
    block_output = result.astype(jnp.bfloat16)
    count = length.astype(jnp.float32) * D
    spread = jnp.stack(
        [
            jnp.sqrt(jnp.sum(keep_rows * branch * branch) / count),
            jnp.sqrt(jnp.sum(keep_rows * feed * feed) / count),
        ]
    )[None, :]
    chosen = masked[0] > 0
    order = jnp.cumsum(masked[0]) - 1
    target = jnp.where(
        chosen,
        (deal_start[image_index] + order) % wide_count * capacity + order // wide_count,
        wide_count * capacity,
    )
    send_rows = (
        jnp.zeros((wide_count * capacity + 1, D), jnp.bfloat16).at[target].set(block_output)[:-1]
    )
    send_latent = (
        jnp.zeros((wide_count * capacity + 1, TOKEN_DIM), jnp.bfloat16).at[target].set(latents)[:-1]
    )
    head_weights = (
        input_proj,
        cond_proj,
        time_first,
        time_second,
        block_mod,
        block_expand,
        block_reduce,
        final_mod,
        final_proj,
    )
    got_rows, got_latent = (
        lax.all_to_all(
            send_rows.reshape(wide_count, capacity, D),
            "wide",
            split_axis=0,
            concat_axis=0,
            tiled=True,
        ),
        lax.all_to_all(
            send_latent.reshape(wide_count, capacity, TOKEN_DIM),
            "wide",
            split_axis=0,
            concat_axis=0,
            tiled=True,
        ),
    )
    sources = jnp.arange(wide_count) * narrow_count + place_narrow
    source_count = bucket[sources] * MASK_MAX // IMAGE_MAX
    first_rank = (place_wide - deal_start[sources]) % wide_count
    arrived = jnp.maximum((source_count - first_rank + wide_count - 1) // wide_count, 0)
    live = (jnp.arange(capacity)[None, :] < arrived[:, None]).astype(jnp.float32).reshape(-1)
    guess, grad_rows, head_smalls, (flow_one, one), (flow_two, two) = diffusion_pass(
        got_rows.reshape(-1, D),
        got_latent.reshape(-1, TOKEN_DIM),
        added_noise,
        timesteps.astype(jnp.float32),
        live,
        head_weights,
    )
    returned = lax.all_to_all(
        grad_rows.astype(jnp.bfloat16).reshape(wide_count, capacity, D),
        "wide",
        split_axis=0,
        concat_axis=0,
        tiled=True,
    ).reshape(-1, D)
    padded = jnp.concatenate([returned, jnp.zeros((1, D), jnp.bfloat16)], axis=0)
    head_to_tokens = padded[target].astype(jnp.float32)
    grad_out = (cotangent.astype(jnp.float32) + head_to_tokens) * keep_rows
    grad_feed = grad_out.astype(jnp.bfloat16)
    grad_feed = behind(grad_feed, *one, *two)
    one = flow_one.step()
    two = flow_two.step()
    reduce_weight_grad = contract_rows(active_low, grad_feed)
    reduce_bias_grad = jnp.sum(grad_feed.astype(jnp.float32), axis=0)
    grad_active = contract_last(grad_feed, reduce_weight)
    grad_hidden = gelu_back(grad_active)[0].astype(jnp.bfloat16)
    grad_hidden = behind(grad_hidden, *one, *two)
    one = flow_one.step()
    two = flow_two.step()
    expand_weight_grad = contract_rows(second_in, grad_hidden)
    total = wide_count * narrow_count

    def low(grad):
        return grad.astype(jnp.bfloat16)

    parts = low(reduce_weight_grad).reshape(total, -1, D)
    piece = D // total
    ratio = parts.shape[1] // piece
    reduce_wide = jnp.concatenate([parts[:, i * piece : (i + 1) * piece] for i in range(ratio)], axis=2)
    flow_feed = Flow(jnp.concatenate([low(expand_weight_grad), reduce_wide.reshape(D, -1)], axis=1))
    expand_bias_grad = jnp.sum(grad_hidden.astype(jnp.float32), axis=0)
    grad_second = contract_last(grad_hidden, expand_weight)
    second_gain_grad = jnp.sum(grad_second * second_normed, axis=0)
    second_shift_grad = jnp.sum(grad_second, axis=0)
    grad_middle = grad_out + normalize_back(
        grad_second * second_gain, second_normed, second_inverse
    )
    grad_branch = grad_middle.astype(jnp.bfloat16)
    grad_branch = behind(grad_branch, *one, *two)
    one = flow_one.step()
    two = flow_two.step()
    feed = flow_feed.step()
    output_weight_grad = contract_rows(mixed, grad_branch)
    output_bias_grad = jnp.sum(grad_branch.astype(jnp.float32), axis=0)
    grad_mixed = contract_last(grad_branch, output_weight).astype(jnp.bfloat16)
    grad_mixed = behind(grad_mixed, *feed)
    feed = flow_feed.step()
    grad_query, grad_keys, grad_values = attend_back(
        joint_low, grad_mixed, mixed, logsum, length[None]
    )
    grad_joint = jnp.concatenate([grad_query, grad_keys, grad_values], axis=1)
    grad_joint = behind(grad_joint, *one, *two, *feed)
    one = flow_one.step()
    two = flow_two.step()
    feed = flow_feed.step()
    joint_weight_grad = contract_rows(first_in, grad_joint)
    flow_last = Flow(jnp.concatenate([low(joint_weight_grad), low(output_weight_grad)], axis=1))
    last = flow_last.step()
    grad_joint = behind(grad_joint, *last)
    last = flow_last.step()
    query_value_bias_grad = jnp.concatenate(
        [
            jnp.sum(grad_query.astype(jnp.float32), axis=0),
            jnp.sum(grad_values.astype(jnp.float32), axis=0),
        ]
    )
    grad_first = contract_last(grad_joint, joint_weight)
    first_gain_grad = jnp.sum(grad_first * first_normed, axis=0)
    first_shift_grad = jnp.sum(grad_first, axis=0)
    tokens_gradient = grad_middle + normalize_back(
        grad_first * first_gain, first_normed, first_inverse
    )
    (input_proj_grad, final_proj_grad) = head_smalls
    width = cond_proj.shape[1]
    flows = (flow_one, flow_two, flow_feed, flow_last)
    for flow in flows:
        for unused in flow.steps:
            pass
    one_sum, two_sum, feed_sum, last_sum = [flow.result for flow in flows]

    def full(rows):
        return rows.reshape(-1, rows.shape[-1]).astype(jnp.float32)

    final_mod_out = full(one_sum[..., : 2 * width])
    block_reduce_out = full(one_sum[..., 2 * width : 3 * width])
    block_expand_out = full(one_sum[..., 3 * width : 4 * width])
    block_mod_out = full(two_sum[..., : 3 * width])
    time_second_out = full(two_sum[..., 3 * width : 4 * width])
    cut = D // total
    cond_out = full(two_sum[:, :cut, 4 * width :])
    time_first_out = full(two_sum[:, cut:, 4 * width :])
    hidden_width = expand_weight.shape[1]
    expand_out = full(feed_sum[..., :hidden_width])
    wide_parts = feed_sum[..., hidden_width:]
    reduce_out = full(
        jnp.concatenate([wide_parts[..., i * D : (i + 1) * D] for i in range(ratio)], axis=1)
    )
    joint_out = full(last_sum[..., : 3 * D])
    output_out = full(last_sum[..., 3 * D :])
    smalls = (
        first_gain_grad,
        first_shift_grad,
        query_value_bias_grad,
        output_bias_grad,
        second_gain_grad,
        second_shift_grad,
        expand_bias_grad,
        reduce_bias_grad,
        input_proj_grad,
        final_proj_grad,
    )
    packed = jnp.concatenate([g.reshape(wide_count, -1) for g in smalls], axis=1)
    small = small_sum(packed)
    outs = []
    at = 0
    for g in smalls:
        size = g.size // wide_count
        outs.append(small[at : at + size].reshape((-1,) + g.shape[1:]))
        at += size
    return (
        block_output,
        guess,
        spread,
        tokens_gradient,
        outs[0],
        outs[1],
        joint_out,
        outs[2],
        output_out,
        outs[3],
        outs[4],
        outs[5],
        expand_out,
        outs[6],
        reduce_out,
        outs[7],
        outs[8],
        cond_out,
        time_first_out,
        time_second_out,
        block_mod_out,
        block_expand_out,
        block_reduce_out,
        final_mod_out,
        outs[9],
    )


def solution(mesh):
    in_specs = (
        P(("wide", "narrow"), None),
        P(("wide", "narrow"), None),
        P(("wide", "narrow"), None),
        P(None, None, ("wide", "narrow")),
        P(None, ("wide", "narrow")),
        P(),
        P(("wide", "narrow"), None),
        P(),
        P(),
        P(),
        P(),
        P(),
        P(),
        P(),
        P(),
        P(),
        P(),
        P(),
        P(),
        P(),
        P(),
        P(),
        P(),
        P(),
        P(),
        P(),
        P(),
        P(),
        P(),
    )
    out_specs = (
        P(("wide", "narrow"), None),
        P(None, None, ("wide", "narrow")),
        P(("wide", "narrow"), None),
        P(("wide", "narrow"), None),
        P("wide"),
        P("wide"),
        P("wide", None),
        P("wide"),
        P("wide", None),
        P("wide"),
        P("wide"),
        P("wide"),
        P("wide", None),
        P("wide"),
        P("wide", None),
        P("wide"),
        P("wide", None),
        P("wide", None),
        P("wide", None),
        P("wide", None),
        P("wide", None),
        P("wide", None),
        P("wide", None),
        P("wide", None),
        P("wide", None),
    )
    return jax.shard_map(shards, mesh=mesh, in_specs=in_specs, out_specs=out_specs, check_vma=False)
```

```python
from functools import partial
import math

import jax
import jax.numpy as jnp
from jax import lax
from jax.experimental import pallas as pl
from jax.experimental.pallas import tpu as pltpu
from jax.sharding import PartitionSpec as P

D = 768
HEADS = 12
HEAD_DIM = 64
TOKEN_DIM = 16
BUFFER = 64
IMAGE_MAX = 1024
MASK_MAX = 256
REPEATS = 4
SEQ = 1088


SHIFT_ANGLE = 0.008 / 1.008 * math.pi / 2.0
STEP_ANGLE = math.pi / (2.0 * 1.008 * 1000.0)
PAIRS = 6
VMEM = 60 * 1024 * 1024


def cost(micros):
    return pl.CostEstimate(flops=0, bytes_accessed=1<<20, transcendentals=0)


OWN = pl.CostEstimate(flops=1<<40, bytes_accessed=1<<20, transcendentals=0)
OTHER = pl.CostEstimate(flops=0, bytes_accessed=1<<20, transcendentals=0)


def nt(a,b): return lax.dot_general(a,b,(((1,),(1,)),((),())),preferred_element_type=jnp.float32)
def nn(a,b): return jnp.dot(a,b,preferred_element_type=jnp.float32)
def tn(a,b): return lax.dot_general(a,b,(((0,),(0,)),((),())),preferred_element_type=jnp.float32)
def normalize(values):
    centre = values - jnp.mean(values, axis=-1, keepdims=True)
    inverse = lax.rsqrt(jnp.mean(centre * centre, axis=-1, keepdims=True) + 1e-06)
    return (centre * inverse, inverse)


def normalize_back(grad_normed, normed, inverse):
    return inverse * (
        grad_normed
        - jnp.mean(grad_normed, axis=-1, keepdims=True)
        - normed * jnp.mean(grad_normed * normed, axis=-1, keepdims=True)
    )


def sigmoid(value):
    return 0.5 * jnp.tanh(0.5 * value) + 0.5


def silu_slope(value, sigma):
    return sigma * (1.0 + value * (1.0 - sigma))


def whole_block(shape):
    zeros = (0,) * len(shape)
    return pl.BlockSpec(shape, lambda *unused: zeros, pipeline_mode=pl.Buffered(1))


def time_kernel(sinus_ref, first_ref, second_ref, low_ref, slope_ref, timed_ref):
    first = nn(sinus_ref[...], first_ref[...])
    sigma = sigmoid(first)
    low = (first * sigma).astype(jnp.bfloat16)
    slope_ref[...] = silu_slope(first, sigma).astype(jnp.bfloat16)
    low_ref[...] = low.T
    timed_ref[...] = nn(low, second_ref[...])


def time_embedding(sinus, time_first, time_second):
    count, freq = sinus.shape
    width = time_first.shape[1]
    rows = count // REPEATS
    by_rows = pl.BlockSpec((rows, width), lambda i: (i, 0))
    return pl.pallas_call(
        time_kernel,
        grid=(REPEATS,),
        in_specs=[
            pl.BlockSpec((rows, freq), lambda i: (i, 0)),
            whole_block(time_first.shape),
            whole_block(time_second.shape),
        ],
        out_specs=[pl.BlockSpec((width, rows), lambda i: (0, i)), by_rows, by_rows],
        out_shape=[
            jax.ShapeDtypeStruct((width, count), jnp.bfloat16),
            jax.ShapeDtypeStruct((count, width), jnp.bfloat16),
            jax.ShapeDtypeStruct((count, width), jnp.float32),
        ],
        compiler_params=pltpu.CompilerParams(vmem_limit_bytes=VMEM),
        cost_estimate=cost(7),
        name="time_embedding",
    )(sinus, time_first, time_second)


def head_kernel(
    dealt_ref,
    timed_ref,
    keep_ref,
    drop_ref,
    noise_ref,
    live_ref,
    input_ref,
    cond_ref,
    mod_ref,
    expand_ref,
    reduce_ref,
    fin_ref,
    final_ref,
    guess_ref,
    left_ref,
    fin_grad_ref,
    branch_grad_ref,
    upper_grad_ref,
    mod_grad_ref,
    timed_grad_ref,
    embed_grad_ref,
    rows_grad_ref,
    input_grad_ref,
    final_grad_ref,
    embed_scratch,
    total_scratch,
):
    turn = pl.program_id(0)
    width = timed_ref.shape[1]

    @pl.when(turn == 0)
    def _():
        embed_scratch[...] = nn(dealt_ref[:, :D], cond_ref[...])
        total_scratch[...] = jnp.zeros_like(total_scratch)
        input_grad_ref[...] = jnp.zeros_like(input_grad_ref)
        final_grad_ref[...] = jnp.zeros_like(final_grad_ref)

    cond = embed_scratch[...] + timed_ref[...]
    acted = (cond * sigmoid(cond)).astype(jnp.bfloat16)
    left_ref[0] = acted.T
    start = dealt_ref[:, D:].astype(jnp.float32).T[:TOKEN_DIM]
    noise = noise_ref[0]
    noisy = (keep_ref[0] * start + drop_ref[0] * noise).astype(jnp.bfloat16)
    entry = tn(noisy, input_ref[...])
    inner_normed, inner_inverse = normalize(entry)
    shift_a = nn(acted, mod_ref[:, :width])
    scale_a = nn(acted, mod_ref[:, width : 2 * width])
    gate_a = nn(acted, mod_ref[:, 2 * width :])
    inner = (inner_normed * (1.0 + scale_a) + shift_a).astype(jnp.bfloat16)
    left_ref[2] = inner.T
    upper = nn(inner, expand_ref[...])
    upper_sigma = sigmoid(upper)
    lifted = (upper * upper_sigma).astype(jnp.bfloat16)
    left_ref[1] = lifted.T
    branch = nn(lifted, reduce_ref[...])
    shift_b = nn(acted, fin_ref[:, :width])
    scale_b = nn(acted, fin_ref[:, width:])
    last_normed, last_inverse = normalize(entry + gate_a * branch)
    last = (last_normed * (1.0 + scale_b) + shift_b).astype(jnp.bfloat16)
    live = live_ref[...]
    guess = nt(final_ref[...], last) * live
    guess_ref[0] = guess
    guess_grad = (2.0 / REPEATS * (guess - noise * live) * live).astype(jnp.bfloat16)
    final_grad_ref[...] += nn(guess_grad, last)
    last_grad = tn(guess_grad, final_ref[...])
    fin_grad = jnp.concatenate([last_grad, last_grad * last_normed], axis=1).astype(jnp.bfloat16)
    fin_grad_ref[...] = fin_grad
    after_grad = normalize_back(last_grad * (1.0 + scale_b), last_normed, last_inverse)
    branch_grad = (after_grad * gate_a).astype(jnp.bfloat16)
    branch_grad_ref[...] = branch_grad
    lifted_grad = nt(branch_grad, reduce_ref[...])
    upper_grad = (lifted_grad * silu_slope(upper, upper_sigma)).astype(jnp.bfloat16)
    upper_grad_ref[...] = upper_grad
    inner_grad = nt(upper_grad, expand_ref[...])
    entry_grad = (
        after_grad + normalize_back(inner_grad * (1.0 + scale_a), inner_normed, inner_inverse)
    ).astype(jnp.bfloat16)
    input_grad_ref[...] += nn(noisy, entry_grad)
    mod_grad = jnp.concatenate(
        [inner_grad, inner_grad * inner_normed, after_grad * branch], axis=1
    ).astype(jnp.bfloat16)
    mod_grad_ref[...] = mod_grad
    acted_grad = nt(mod_grad, mod_ref[...]) + nt(fin_grad, fin_ref[...])
    cond = embed_scratch[...] + timed_ref[...]
    cond_grad = acted_grad * silu_slope(cond, sigmoid(cond))
    timed_grad_ref[...] = cond_grad.astype(jnp.bfloat16)
    total_scratch[...] += cond_grad

    @pl.when(turn == REPEATS - 1)
    def _():
        embed_grad = total_scratch[...].astype(jnp.bfloat16)
        embed_grad_ref[...] = embed_grad
        rows_grad_ref[...] = nt(embed_grad, cond_ref[...]).astype(jnp.bfloat16)


def head_pass(dealt, timed, keep_sig, drop_sig, noise, live, weights):
    input_proj, cond_proj, block_mod, block_expand, block_reduce, final_mod, final_proj = weights
    slots = dealt.shape[0]
    width = cond_proj.shape[1]
    count = REPEATS * slots
    by_rows = lambda n: pl.BlockSpec((slots, n), lambda i: (i, 0))
    by_turn = lambda a: pl.BlockSpec((1,) + a, lambda i: (i, 0, 0))
    low = lambda *s: jax.ShapeDtypeStruct(s, jnp.bfloat16)
    full = lambda *s: jax.ShapeDtypeStruct(s, jnp.float32)
    operands = (
        dealt,
        timed,
        keep_sig,
        drop_sig,
        noise,
        live,
        input_proj,
        cond_proj,
        block_mod,
        block_expand,
        block_reduce,
        final_mod,
        final_proj,
    )
    return pl.pallas_call(
        head_kernel,
        grid=(REPEATS,),
        in_specs=[
            whole_block(dealt.shape),
            by_rows(width),
            by_turn((1, slots)),
            by_turn((1, slots)),
            by_turn((TOKEN_DIM, slots)),
        ]
        + [whole_block(a.shape) for a in operands[5:]],
        out_specs=[
            by_turn((TOKEN_DIM, slots)),
            pl.BlockSpec((3, width, slots), lambda i: (0, 0, i)),
            by_rows(2 * width),
            by_rows(width),
            by_rows(width),
            by_rows(3 * width),
            by_rows(width),
            whole_block((slots, width)),
            whole_block((slots, D)),
            whole_block((TOKEN_DIM, width)),
            whole_block((TOKEN_DIM, width)),
        ],
        out_shape=[
            full(REPEATS, TOKEN_DIM, slots),
            low(3, width, count),
            low(count, 2 * width),
            low(count, width),
            low(count, width),
            low(count, 3 * width),
            low(count, width),
            low(slots, width),
            low(slots, D),
            full(TOKEN_DIM, width),
            full(TOKEN_DIM, width),
        ],
        scratch_shapes=[pltpu.VMEM((slots, width), jnp.float32)] * 2,
        compiler_params=pltpu.CompilerParams(vmem_limit_bytes=VMEM),
        cost_estimate=cost(50),
        name="head_pass",
    )(*operands)


MARK = jax.ShapeDtypeStruct((8, 128), jnp.float32)


def head_grads_one_kernel(half_ref, left_ref, fin_ref, branch_ref, upper_ref, out_ref, mark_ref):
    tile = half_ref[0] * 4 + pl.program_id(0)

    mark_ref[...] = jnp.zeros_like(mark_ref)

    def put(grad):
        out_ref[0] = grad.astype(jnp.bfloat16)

    @pl.when(tile < 4)
    def _():
        put(nn(left_ref[0], fin_ref[...]))

    @pl.when((tile >= 4) & (tile < 6))
    def _():
        put(nn(left_ref[0], branch_ref[...]))

    @pl.when(tile >= 6)
    def _():
        put(nn(left_ref[0], upper_ref[...]))


def head_grads_one(est, half, left, fin_grad, branch_grad, upper_grad):
    width, count = left.shape[1:]
    cols = width // 2

    def at(first, tiles):
        return lambda i, half: (0, jnp.clip(half[0] * 4 + i - first, 0, tiles - 1))

    def which(i, half):
        tile = half[0] * 4 + i
        return (jnp.where(tile < 4, 0, jnp.where(tile < 6, 1, 2)), 0, 0)

    return pl.pallas_call(
        head_grads_one_kernel,
        grid_spec=pltpu.PrefetchScalarGridSpec(
            num_scalar_prefetch=1,
            grid=(4,),
            in_specs=[
                pl.BlockSpec((1, width, count), which),
                pl.BlockSpec((count, cols), at(0, 4)),
                pl.BlockSpec((count, cols), at(4, 2)),
                pl.BlockSpec((count, cols), at(6, 2)),
            ],
            out_specs=[pl.BlockSpec((1, width, cols), lambda i, half: (i, 0, 0)), whole_block((8, 128))],
        ),
        out_shape=[jax.ShapeDtypeStruct((4, width, cols), jnp.bfloat16), MARK],
        compiler_params=pltpu.CompilerParams(vmem_limit_bytes=VMEM),
        cost_estimate=est,
        name="head_grads_one",
    )(half, left, fin_grad, branch_grad, upper_grad)


def time_back_kernel(grad_ref, weight_ref, slope_ref, out_ref):
    grad = nt(grad_ref[...], weight_ref[...])
    out_ref[...] = (grad * slope_ref[...].astype(jnp.float32)).astype(jnp.bfloat16)


def time_back(timed_grad, weight, slope):
    count, width = timed_grad.shape
    by_rows = pl.BlockSpec((count // 4, width), lambda i: (i, 0))
    return pl.pallas_call(
        time_back_kernel,
        grid=(4,),
        in_specs=[by_rows, whole_block(weight.shape), by_rows],
        out_specs=by_rows,
        out_shape=jax.ShapeDtypeStruct((count, width), jnp.bfloat16),
        compiler_params=pltpu.CompilerParams(vmem_limit_bytes=VMEM),
        cost_estimate=cost(6),
        name="time_back",
    )(timed_grad, weight, slope)


def head_grads_two_kernel(
    wide, half_ref, acted_ref, low_ref, mod_ref, timed_ref, rows_ref, embed_ref, sinus_ref, first_ref, out_ref, mark_ref
):
    tile = half_ref[0] * 10 + pl.program_id(0)

    mark_ref[...] = jnp.zeros_like(mark_ref)

    def put(grad):
        out_ref[0] = grad.astype(jnp.bfloat16)

    @pl.when(tile < 12)
    def _():
        put(nn(acted_ref[0], mod_ref[...]))

    @pl.when((tile >= 12) & (tile < 16))
    def _():
        put(nn(low_ref[...], timed_ref[...]))

    @pl.when(tile >= 16)
    def _():
        cond = tn(rows_ref[:, :D], embed_ref[...])
        time = tn(sinus_ref[...], first_ref[...])
        cols = cond.shape[1]
        both = jnp.concatenate(
            [cond.reshape(wide, -1, cols), time.reshape(wide, -1, cols)], axis=1
        )
        put(both.reshape(-1, cols))


def head_grads_two(est, half, left, low, mod_grad, timed_grad, dealt, embed_grad, sinus, first_grad, wide):
    width, count = left.shape[1:]
    slots = dealt.shape[0]
    cols = width // 4

    def at(first, tiles):
        return lambda i, half: (0, jnp.clip(half[0] * 10 + i - first, 0, tiles - 1))

    return pl.pallas_call(
        partial(head_grads_two_kernel, wide),
        grid_spec=pltpu.PrefetchScalarGridSpec(
            num_scalar_prefetch=1,
            grid=(10,),
            in_specs=[
                whole_block((1, width, count)),
                whole_block((width, count)),
                pl.BlockSpec((count, cols), at(0, 12)),
                pl.BlockSpec((count, cols), at(12, 4)),
                whole_block(dealt.shape),
                pl.BlockSpec((slots, cols), at(16, 4)),
                whole_block(sinus.shape),
                pl.BlockSpec((count, cols), at(16, 4)),
            ],
            out_specs=[pl.BlockSpec((1, width, cols), lambda i, half: (i, 0, 0)), whole_block((8, 128))],
        ),
        out_shape=[jax.ShapeDtypeStruct((10, width, cols), jnp.bfloat16), MARK],
        compiler_params=pltpu.CompilerParams(vmem_limit_bytes=VMEM),
        cost_estimate=est,
        name="head_grads_two",
    )(half, left, low, mod_grad, timed_grad, dealt, embed_grad, sinus, first_grad)


def attend_kernel(QB, at_ref, bucket_ref, q_ref, k_ref, v_ref, o_ref, lse_ref):
    length=BUFFER + bucket_ref[at_ref[0]]
    low=lax.broadcasted_iota(jnp.int32,(1,128),1)<64
    bias=jnp.where(lax.broadcasted_iota(jnp.int32,(1,SEQ),1)<length,0.0,-1e30).astype(jnp.float32)
    k=k_ref[...]; v=v_ref[...]
    one=jnp.ones((),v.dtype); zero=jnp.zeros((),v.dtype)
    vs=(jnp.where(low,v,one),jnp.where(low,one,v))
    for b in range(SEQ//QB):
        rows=pl.ds(b*QB,QB)
        q=q_ref[rows,:]
        outs=[];lses=[]
        for h in range(2):
            qh=jnp.where(low,q,zero) if h==0 else jnp.where(low,zero,q)
            s=nt(qh,k)+bias
            top=jnp.max(s,axis=1,keepdims=True)
            p=jnp.exp(s-top).astype(jnp.bfloat16)
            o=nn(p,vs[h])
            total=pltpu.roll(o,64,1)
            outs.append(o/total)
            lses.append(top+jnp.log(total))
        o_ref[rows,:]=jnp.where(low,outs[0],outs[1]).astype(jnp.bfloat16)
        lse_ref[rows,:]=jnp.where(low,lses[0],lses[1])

def attend(at,bucket,joint,QB=272):
    spec=lambda off: pl.BlockSpec((SEQ,128),lambda i,off=off:(0,i+off))
    return pl.pallas_call(partial(attend_kernel,QB),
        grid=(PAIRS,),
        in_specs=[smem(),smem(),spec(0),spec(6),spec(12)],
        out_specs=[spec(0),spec(0)],
        out_shape=[jax.ShapeDtypeStruct((SEQ,D),jnp.bfloat16),jax.ShapeDtypeStruct((SEQ,D),jnp.float32)],
        compiler_params=pltpu.CompilerParams(vmem_limit_bytes=VMEM),
        cost_estimate=cost(26),
        name='attend')(at,bucket,joint,joint,joint)

def attend_back_kernel(KB, at_ref, bucket_ref,q_ref,k_ref,v_ref,do_ref,o_ref,lse_ref,dq_ref,dk_ref,dv_ref,ds_ref):
    length=BUFFER + bucket_ref[at_ref[0]]
    low=lax.broadcasted_iota(jnp.int32,(1,128),1)<64
    q=q_ref[...]; do=do_ref[...]
    zero=jnp.zeros((),q.dtype)
    prod=do.astype(jnp.float32)*o_ref[...].astype(jnp.float32)
    prodT=prod.T
    lseT=lse_ref[...].T
    deltas=(jnp.sum(prodT[:64],axis=0,keepdims=True),jnp.sum(prodT[64:],axis=0,keepdims=True))
    lses=(lseT[0:1],lseT[64:65])
    for b in range(SEQ//KB):
        rows=pl.ds(b*KB,KB)
        k=k_ref[rows,:]; v=v_ref[rows,:]
        bias=jnp.where(lax.broadcasted_iota(jnp.int32,(KB,1),0)+b*KB<length,0.0,-1e30).astype(jnp.float32)
        dks=[];dvs=[]
        for h in range(2):
            pick=(lambda a: jnp.where(low,a,zero)) if h==0 else (lambda a: jnp.where(low,zero,a))
            s=nt(pick(k),q)+bias
            p=jnp.exp(s-lses[h])
            dp=nt(pick(v),do)
            ds=(p*(dp-deltas[h])).astype(jnp.bfloat16)
            dvs.append(nn(p.astype(jnp.bfloat16),do))
            dks.append(nn(ds,q))
            ds_ref[h,rows,:]=ds
        dk_ref[rows,:]=jnp.where(low,dks[0],dks[1]).astype(jnp.bfloat16)
        dv_ref[rows,:]=jnp.where(low,dvs[0],dvs[1]).astype(jnp.bfloat16)
    kT=k_ref[...].astype(jnp.float32).T.astype(jnp.bfloat16)
    dqT=jnp.concatenate([nn(kT[64*h:64*h+64],ds_ref[h]) for h in range(2)],axis=0)
    dq_ref[...]=(dqT.T*0.125).astype(jnp.bfloat16)

def attend_back(first,count,at,bucket,joint,do,o,lse,KB=544):
    spec=lambda off: pl.BlockSpec((SEQ,128),lambda i,off=off:(0,i+off))
    return pl.pallas_call(partial(attend_back_kernel,KB),
        grid=(count,),
        in_specs=[smem(),smem(),spec(first),spec(6+first),spec(12+first),spec(first),spec(first),spec(first)],
        out_specs=[spec(0)]*3,
        out_shape=[jax.ShapeDtypeStruct((SEQ,count*128),jnp.bfloat16)]*3,
        scratch_shapes=[pltpu.VMEM((2,SEQ,SEQ),jnp.bfloat16)],
        compiler_params=pltpu.CompilerParams(vmem_limit_bytes=VMEM),
        cost_estimate=cost(21),
        name='attend_back')(at,bucket,joint,joint,joint,do,o,lse)


def line(ref):
    return ref[...].reshape(1, ref.shape[0])


def smem():
    return pl.BlockSpec(memory_space=pltpu.SMEM)


def place_kernel(wide, at_ref, bucket_ref, start_ref, chosen_ref, spot_ref, live_ref):
    image, place_wide, place_narrow, narrow = at_ref[0], at_ref[1], at_ref[2], at_ref[3]
    seq = chosen_ref.shape[1]
    slots = live_ref.shape[1]
    shift = wide.bit_length() - 1
    deep = slots // wide
    deep_shift = deep.bit_length() - 1
    row = lax.broadcasted_iota(jnp.int32, (seq, seq), 0)
    column = lax.broadcasted_iota(jnp.int32, (seq, seq), 1)
    lower = (column <= row).astype(jnp.float32).astype(jnp.bfloat16)
    chosen = jnp.broadcast_to(chosen_ref[...], (8, seq)).astype(jnp.float32).astype(jnp.bfloat16)
    counted = nt(lower, chosen)
    first_row = lax.broadcasted_iota(jnp.int32, counted.shape, 0) == 0
    before = jnp.where(first_row, 0.0, pltpu.roll(counted, 1, 0))
    is_chosen = (counted - before)[:, :1] > 0.5
    order = counted[:, :1].astype(jnp.int32) - 1
    target = ((start_ref[image] + order) & (wide - 1)) * deep + (order >> shift)
    target = jnp.where(is_chosen, target, -1)
    slot = lax.broadcasted_iota(jnp.int32, (seq, slots), 1)
    spot_ref[...] = (slot == target).astype(jnp.float32).astype(jnp.bfloat16)
    lane = lax.broadcasted_iota(jnp.int32, (1, slots), 1)
    live = jnp.zeros((1, slots), jnp.float32)
    for source in range(wide):
        other = source * narrow + place_narrow
        count = bucket_ref[other] * MASK_MAX // IMAGE_MAX
        rank = (place_wide - start_ref[other]) & (wide - 1)
        arrived = jnp.maximum((count - rank + wide - 1) >> shift, 0)
        inside = ((lane >> deep_shift) == source) & ((lane & (deep - 1)) < arrived)
        live = jnp.where(inside, 1.0, live)
    live_ref[...] = live


def places(at, bucket, deal_start, masked, wide):
    seq = masked.shape[1]
    return pl.pallas_call(
        partial(place_kernel, wide),
        in_specs=[smem(), smem(), smem(), whole_block((1, seq))],
        out_specs=[whole_block((seq, MASK_MAX)), whole_block((1, MASK_MAX))],
        grid=(1,),
        out_shape=[
            jax.ShapeDtypeStruct((seq, MASK_MAX), jnp.bfloat16),
            jax.ShapeDtypeStruct((1, MASK_MAX), jnp.float32),
        ],
        compiler_params=pltpu.CompilerParams(vmem_limit_bytes=VMEM),
        cost_estimate=cost(3),
        name="places",
    )(at, bucket, deal_start, masked)


def joint_kernel(tokens_ref, gain_ref, shift_ref, weight_ref, bias_ref, first_ref, joint_ref):
    normed, unused = normalize(tokens_ref[...].astype(jnp.float32))
    first = (normed * line(gain_ref) + line(shift_ref)).astype(jnp.bfloat16)
    first_ref[...] = first
    for part in range(3):
        cols = slice(part * D, (part + 1) * D)
        out = nn(first, weight_ref[:, cols])
        if part != 1:
            out = out + line(bias_ref)[:, part // 2 * D : part // 2 * D + D]
        out = out.astype(jnp.bfloat16)
        if part == 0:
            out = out * jnp.bfloat16(HEAD_DIM ** (-0.5))
        joint_ref[:, cols] = out


ROWS = 272


def by_block(columns):
    return pl.BlockSpec((ROWS, columns), lambda i: (i, 0))


def joint_pass(tokens, gain, shift, weight, bias):
    seq = tokens.shape[0]
    return pl.pallas_call(
        joint_kernel,
        grid=(seq // ROWS,),
        in_specs=[by_block(D)] + [whole_block(a.shape) for a in (gain, shift, weight, bias)],
        out_specs=[by_block(D), by_block(3 * D)],
        out_shape=[
            jax.ShapeDtypeStruct((seq, D), jnp.bfloat16),
            jax.ShapeDtypeStruct((seq, 3 * D), jnp.bfloat16),
        ],
        compiler_params=pltpu.CompilerParams(vmem_limit_bytes=VMEM),
        cost_estimate=cost(9),
        name="joint_pass",
    )(tokens, gain, shift, weight, bias)


def gelu_parts(value):
    size = jnp.abs(value)
    bell = jnp.exp(-0.5 * value * value)
    step = 1.0 / (1.0 + (0.3275911 * math.sqrt(0.5)) * size)
    tail = 0.5 * 1.061405429 * step - 0.5 * 1.453152027
    tail = tail * step + 0.5 * 1.421413741
    tail = tail * step - 0.5 * 0.284496736
    tail = tail * step + 0.5 * 0.254829592
    tail = tail * step * bell
    return jnp.where(value < 0.0, tail, 1.0 - tail), bell * (1.0 / math.sqrt(2.0 * math.pi))


def keep_column(at_ref, bucket_ref, rows):
    position = lax.broadcasted_iota(jnp.int32, (rows, 1), 0) + pl.program_id(0) * rows
    return (position < BUFFER + bucket_ref[at_ref[0]]).astype(jnp.float32)


def feed_kernel(
    at_ref,
    bucket_ref,
    mixed_ref,
    tokens_ref,
    latent_ref,
    spot_ref,
    out_w_ref,
    out_b_ref,
    gain_ref,
    shift_ref,
    expand_ref,
    expand_b_ref,
    reduce_ref,
    reduce_b_ref,
    output_ref,
    middle_ref,
    second_ref,
    active_ref,
    slope_ref,
    dealt_ref,
    spread_ref,
    dealt_scratch,
    spread_scratch,
):
    step = pl.program_id(0)

    @pl.when(step == 0)
    def _():
        dealt_scratch[...] = jnp.zeros_like(dealt_scratch)
        spread_scratch[...] = jnp.zeros_like(spread_scratch)

    keep = keep_column(at_ref, bucket_ref, mixed_ref.shape[0])
    branch = nn(mixed_ref[...], out_w_ref[...]) + line(out_b_ref)
    middle = tokens_ref[...].astype(jnp.float32) + branch
    middle_ref[...] = middle
    normed, unused = normalize(middle)
    second = (normed * line(gain_ref) + line(shift_ref)).astype(jnp.bfloat16)
    second_ref[...] = second
    hidden_width = expand_ref.shape[1]
    expand_b = line(expand_b_ref)
    feed = line(reduce_b_ref)
    for part in range(hidden_width // D):
        cols = slice(part * D, (part + 1) * D)
        hidden = nn(second, expand_ref[:, cols]) + expand_b[:, cols]
        phi, density = gelu_parts(hidden)
        active = (hidden * phi).astype(jnp.bfloat16)
        active_ref[:, cols] = active
        slope_ref[:, cols] = (phi + hidden * density).astype(jnp.bfloat16)
        feed = feed + nn(active, reduce_ref[cols, :])
    output = ((middle + feed) * keep).astype(jnp.bfloat16)
    output_ref[...] = output
    spread_scratch[0:1, :] += jnp.sum(keep * branch * branch, axis=0, keepdims=True)
    spread_scratch[1:2, :] += jnp.sum(keep * feed * feed, axis=0, keepdims=True)
    spot = spot_ref[...]
    dealt_scratch[:, :D] += tn(spot, output)
    dealt_scratch[:, D : D + TOKEN_DIM] += tn(spot, latent_ref[...])

    @pl.when(step == pl.num_programs(0) - 1)
    def _():
        dealt_ref[...] = dealt_scratch[...].astype(jnp.bfloat16)
        count = (BUFFER + bucket_ref[at_ref[0]]).astype(jnp.float32) * D
        total = jnp.sum(spread_scratch[...], axis=1, keepdims=True)
        spread_ref[...] = jnp.sqrt(jnp.broadcast_to(total, spread_ref.shape) / count)


def feed_pass(at, bucket, mixed, tokens, latents, spot, weights):
    seq = tokens.shape[0]
    slots = spot.shape[1]
    hidden = weights[4].shape[1]
    low = lambda *s: jax.ShapeDtypeStruct(s, jnp.bfloat16)
    full = lambda *s: jax.ShapeDtypeStruct(s, jnp.float32)
    return pl.pallas_call(
        feed_kernel,
        grid=(seq // ROWS,),
        in_specs=[smem(), smem(), by_block(D), by_block(D), by_block(TOKEN_DIM), by_block(slots)]
        + [whole_block(a.shape) for a in weights],
        out_specs=[
            by_block(D),
            by_block(D),
            by_block(D),
            by_block(hidden),
            by_block(hidden),
            whole_block((slots, D + 128)),
            whole_block((8, 128)),
        ],
        out_shape=[
            low(seq, D),
            full(seq, D),
            low(seq, D),
            low(seq, hidden),
            low(seq, hidden),
            low(slots, D + 128),
            full(8, 128),
        ],
        scratch_shapes=[pltpu.VMEM((slots, D + 128), jnp.float32), pltpu.VMEM((8, D), jnp.float32)],
        compiler_params=pltpu.CompilerParams(vmem_limit_bytes=VMEM),
        cost_estimate=cost(30),
        name="feed_pass",
    )(at, bucket, mixed, tokens, latents, spot, *weights)


def feed_back_kernel(
    at_ref,
    bucket_ref,
    cot_ref,
    spot_ref,
    middle_ref,
    slope_ref,
    returned_ref,
    out_w_ref,
    gain_ref,
    expand_ref,
    reduce_ref,
    feed_grad_ref,
    hidden_grad_ref,
    middle_grad_ref,
    branch_grad_ref,
    mixed_grad_ref,
    sums_ref,
    wide_sum_ref,
):
    @pl.when(pl.program_id(0) == 0)
    def _():
        sums_ref[...] = jnp.zeros_like(sums_ref)
        wide_sum_ref[...] = jnp.zeros_like(wide_sum_ref)

    def add_sum(row, value):
        sums_ref[row : row + 1, :] += jnp.sum(value, axis=0, keepdims=True)

    keep = keep_column(at_ref, bucket_ref, cot_ref.shape[0])
    grad = (cot_ref[...].astype(jnp.float32) + nn(spot_ref[...], returned_ref[...])) * keep
    feed_grad = grad.astype(jnp.bfloat16)
    feed_grad_ref[...] = feed_grad
    add_sum(0, feed_grad.astype(jnp.float32))
    second_grad = jnp.zeros(grad.shape, jnp.float32)
    for part in range(expand_ref.shape[1] // D):
        cols = slice(part * D, (part + 1) * D)
        active_grad = nt(feed_grad, reduce_ref[cols, :])
        hidden_grad = (active_grad * slope_ref[:, cols].astype(jnp.float32)).astype(jnp.bfloat16)
        hidden_grad_ref[:, cols] = hidden_grad
        wide_sum_ref[:, cols] += jnp.sum(hidden_grad.astype(jnp.float32), axis=0, keepdims=True)
        second_grad = second_grad + nt(hidden_grad, expand_ref[:, cols])
    normed, inverse = normalize(middle_ref[...])
    add_sum(1, second_grad * normed)
    add_sum(2, second_grad)
    middle_grad = grad + normalize_back(second_grad * line(gain_ref), normed, inverse)
    middle_grad_ref[...] = middle_grad
    branch_grad = middle_grad.astype(jnp.bfloat16)
    branch_grad_ref[...] = branch_grad
    add_sum(3, branch_grad.astype(jnp.float32))
    mixed_grad_ref[...] = nt(branch_grad, out_w_ref[...]).astype(jnp.bfloat16)


def feed_back(at, bucket, cotangent, spot, middle, slope, returned, weights):
    seq = cotangent.shape[0]
    slots = spot.shape[1]
    hidden = slope.shape[1]
    low = lambda *s: jax.ShapeDtypeStruct(s, jnp.bfloat16)
    full = lambda *s: jax.ShapeDtypeStruct(s, jnp.float32)
    return pl.pallas_call(
        feed_back_kernel,
        grid=(seq // ROWS,),
        in_specs=[smem(), smem(), by_block(D), by_block(slots), by_block(D), by_block(hidden)]
        + [whole_block(a.shape) for a in (returned,) + weights],
        out_specs=[
            by_block(D),
            by_block(hidden),
            by_block(D),
            by_block(D),
            by_block(D),
            whole_block((8, D)),
            whole_block((1, hidden)),
        ],
        out_shape=[
            low(seq, D),
            low(seq, hidden),
            full(seq, D),
            low(seq, D),
            low(seq, D),
            full(8, D),
            full(1, hidden),
        ],
        compiler_params=pltpu.CompilerParams(vmem_limit_bytes=VMEM),
        cost_estimate=cost(22),
        name="feed_back",
    )(at, bucket, cotangent, spot, middle, slope, returned, *weights)


def feed_grads_kernel(wide, half_ref, second_ref, hidden_ref, active_ref, grad_ref, out_ref, mark_ref):
    step = pl.program_id(0)
    mark_ref[...] = jnp.zeros_like(mark_ref)

    @pl.when(step == 0)
    def _():
        out_ref[0] = tn(second_ref[...], hidden_ref[...]).astype(jnp.bfloat16)

    @pl.when(step == 1)
    def _():
        out_ref[1] = tn(second_ref[...], hidden_ref[...]).astype(jnp.bfloat16)

    @pl.when(step == 2)
    def _():
        whole = tn(active_ref[...], grad_ref[...])
        pieces = whole.shape[0] // D
        whole = whole.reshape(wide, pieces, D // wide, D // 2)
        for piece in range(pieces):
            out_ref[2 + piece // 2, :, piece % 2 * (D // 2) : (piece % 2 + 1) * (D // 2)] = (
                whole[:, piece].reshape(D, D // 2).astype(jnp.bfloat16)
            )


def feed_grads(est, half, second, hidden_grad, active, feed_grad, wide):
    seq, hidden = active.shape
    return pl.pallas_call(
        partial(feed_grads_kernel, wide),
        grid_spec=pltpu.PrefetchScalarGridSpec(
            num_scalar_prefetch=1,
            grid=(3,),
            in_specs=[
                whole_block((seq, D)),
                pl.BlockSpec((seq, D), lambda i, half: (0, half[0] * 2 + jnp.minimum(i, 1))),
                whole_block((seq, hidden)),
                pl.BlockSpec((seq, D // 2), lambda i, half: (0, half[0])),
            ],
            out_specs=[whole_block((4, D, D)), whole_block((8, 128))],
        ),
        out_shape=[jax.ShapeDtypeStruct((4, D, D), jnp.bfloat16), MARK],
        compiler_params=pltpu.CompilerParams(vmem_limit_bytes=VMEM),
        cost_estimate=est,
        name="feed_grads",
    )(half, second, hidden_grad, active, feed_grad)


def last_grads_kernel(half_ref, first_ref, mixed_ref, *refs):
    out_ref, mark_ref = refs[-2:]
    mark_ref[...] = jnp.zeros_like(mark_ref)

    def put(at, left, right):
        out_ref[at] = tn(left[...], right[...]).astype(jnp.bfloat16)

    @pl.when(half_ref[0] == 0)
    def _():
        for i in range(4):
            put(i, first_ref, refs[i])

    @pl.when(half_ref[0] == 1)
    def _():
        put(0, first_ref, refs[4])
        put(1, first_ref, refs[5])
        whole = tn(mixed_ref[...], refs[6][...]).astype(jnp.bfloat16)
        out_ref[2] = whole[:, : D // 2]
        out_ref[3] = whole[:, D // 2 :]


def last_grads(est, half, *operands):
    return pl.pallas_call(
        last_grads_kernel,
        in_specs=[smem()] + [whole_block(a.shape) for a in operands],
        out_specs=[whole_block((4, D, D // 2)), whole_block((8, 128))],
        grid=(1,),
        out_shape=[jax.ShapeDtypeStruct((4, D, D // 2), jnp.bfloat16), MARK],
        compiler_params=pltpu.CompilerParams(vmem_limit_bytes=VMEM),
        cost_estimate=est,
        name="last_grads",
    )(half, *operands)


def tokens_back_kernel(
    tokens_ref, q1_ref, q2_ref, k1_ref, k2_ref, v1_ref, v2_ref, middle_ref, gain_ref, weight_ref, out_ref, packed_ref, sums_ref
):
    @pl.when(pl.program_id(0) == 0)
    def _():
        sums_ref[...] = jnp.zeros_like(sums_ref)

    def add_sum(row, value):
        sums_ref[row : row + 1, :] += jnp.sum(value, axis=0, keepdims=True)

    query = jnp.concatenate([q1_ref[...], q2_ref[...]], axis=1)
    value = jnp.concatenate([v1_ref[...], v2_ref[...]], axis=1)
    grad = nt(query, weight_ref[:, :D])
    grad = grad + nt(jnp.concatenate([k1_ref[...], k2_ref[...]], axis=1), weight_ref[:, D : 2 * D])
    grad = grad + nt(value, weight_ref[:, 2 * D :])
    normed, inverse = normalize(tokens_ref[...].astype(jnp.float32))
    add_sum(0, grad * normed)
    add_sum(1, grad)
    add_sum(2, query.astype(jnp.float32))
    add_sum(3, value.astype(jnp.float32))
    out_ref[...] = middle_ref[...] + normalize_back(grad * line(gain_ref), normed, inverse)

    @pl.when(pl.program_id(0) == pl.num_programs(0) - 1)
    def _():
        wide = packed_ref.shape[0]
        part = D // wide
        for w in range(wide):
            packed_ref[w : w + 1, :part] = sums_ref[0:1, w * part : (w + 1) * part]
            packed_ref[w : w + 1, part : 2 * part] = sums_ref[1:2, w * part : (w + 1) * part]
            bias_row = 2 + w * 2 // wide
            at = w % (wide // 2) * 2 * part
            packed_ref[w : w + 1, 2 * part :] = sums_ref[bias_row : bias_row + 1, at : at + 2 * part]


def tokens_back(tokens, parts, middle_grad, gain, weight, wide):
    seq = tokens.shape[0]
    return pl.pallas_call(
        tokens_back_kernel,
        grid=(seq // ROWS,),
        in_specs=[by_block(D)] + [by_block(D // 2)] * 6 + [by_block(D)] + [whole_block(gain.shape), whole_block(weight.shape)],
        out_specs=[by_block(D), whole_block((wide, 4 * D // wide))],
        out_shape=[
            jax.ShapeDtypeStruct((seq, D), jnp.float32),
            jax.ShapeDtypeStruct((wide, 4 * D // wide), jnp.float32),
        ],
        scratch_shapes=[pltpu.VMEM((8, D), jnp.float32)],
        compiler_params=pltpu.CompilerParams(vmem_limit_bytes=VMEM),
        cost_estimate=cost(11),
        name="tokens_back",
    )(tokens, *parts, middle_grad, gain, weight)


def pack_kernel(feed_ref, hidden_ref, input_ref, final_ref, token_ref, *refs):
    out_ref = refs[-1]
    out_ref[...] = jnp.zeros_like(out_ref)
    wide, rows, cols = out_ref.shape
    part = D // wide
    block = input_ref.shape[1] // wide
    for w in range(wide):
        out_ref[w, :TOKEN_DIM, :block] = input_ref[:, w * block : (w + 1) * block]
        out_ref[w, :TOKEN_DIM, block : 2 * block] = final_ref[:, w * block : (w + 1) * block]
        out_ref[w, TOKEN_DIM : TOKEN_DIM + 1, :] = hidden_ref[:, w * cols : (w + 1) * cols]
        out_ref[w, TOKEN_DIM + 2 : TOKEN_DIM + 3, :] = token_ref[w : w + 1, :]
        for i in range(4):
            out_ref[w, TOKEN_DIM + 1 : TOKEN_DIM + 2, i * part : (i + 1) * part] = feed_ref[
                i : i + 1, w * part : (w + 1) * part
            ]


def pack(feed_sums, hidden_sum, input_grad, final_grad, token_packed, marks):
    operands = (feed_sums, hidden_sum, input_grad, final_grad, token_packed)
    wide = token_packed.shape[0]
    shape = (wide, TOKEN_DIM + 8, hidden_sum.shape[1] // wide)
    return pl.pallas_call(
        pack_kernel,
        grid=(1,),
        in_specs=[whole_block(a.shape) for a in operands] + [pl.BlockSpec(memory_space=pl.ANY)] * len(marks),
        out_specs=whole_block(shape),
        out_shape=jax.ShapeDtypeStruct(shape, jnp.float32),
        cost_estimate=cost(2),
        name="pack",
    )(*operands, *marks)


def add_up(terms):
    total = terms[0].astype(jnp.float32)
    for term in terms[1:]:
        total = total + term.astype(jnp.float32)
    return total


def swap(array, axis, mask):
    count = lax.axis_size(axis)
    return lax.ppermute(array, axis, [(i, i ^ mask) for i in range(count)])


def bit(axis, mask):
    return lax.axis_index(axis) // mask % 2


def pick(array, index, axis):
    return lax.dynamic_index_in_dim(array, index, axis, keepdims=False)


class Order:
    def __init__(self):
        self.mark = ()
        self.marks = ()

    def __call__(self, *values):
        out = lax.optimization_barrier(values + self.mark)[: len(values)]
        return out if len(values) > 1 else out[0]

    def at(self, *values):
        self.mark = values


class Flow:
    def __init__(self, order, sent):
        self.order = order
        sent, mark = sent
        self.got = (swap(sent, "narrow", 1),)
        order.at(mark)
        order.marks += (mark,)

    def own(self, own):
        self.last = lax.axis_size("wide").bit_length() - 2
        dims = (2,) * (self.last + 1)
        own, mark = own
        self.mine = own.reshape((2, own.shape[0] // 2) + dims + (-1, own.shape[2]))
        self.order.at(mark)
        self.order.marks += (mark,)
        self.steps = self.run()

    def step(self):
        next(self.steps)

    def take(self):
        got = self.order(*self.got)
        return got if isinstance(got, (tuple, list)) else (got,)

    def send(self, *sends):
        self.got = tuple(swap(*s) for s in sends)
        self.order.at(*[s[0] for s in sends])

    def halve(self, terms, axis, mask, dim):
        mine = bit(axis, mask)
        sent = add_up([pick(t, 1 - mine, dim) for t in terms]).astype(jnp.bfloat16)
        return [pick(t, mine, dim) for t in terms], (sent, axis, mask)

    def lane(self, terms, first, count, axis, mask, dim):
        mine = bit(axis, mask)

        def part(term, at):
            starts = [0] * term.ndim
            sizes = list(term.shape)
            starts[1], sizes[1] = first, count
            starts[dim], sizes[dim] = at, 1
            return lax.dynamic_slice(term, starts, sizes).squeeze(dim)

        sent = add_up([part(t, 1 - mine) for t in terms]).astype(jnp.bfloat16)
        return [part(t, mine) for t in terms], (sent, axis, mask)

    def run(self):
        last = self.last
        tiles = self.mine.shape[1]
        cut = tiles // 2
        terms = [self.mine, self.take()[0].reshape(self.mine.shape)]
        one, send_one = self.lane(terms, 0, cut, "narrow", 2, 0)
        two, send_two = self.lane(terms, cut, tiles - cut, "wide", 1, 2 + last)
        self.send(send_one, send_two)
        yield
        got = self.take()
        one, send_one = self.halve(one + [got[0]], "wide", 1, 1 + last)
        two, send_two = self.halve(two + [got[1]], "narrow", 2, 0)
        self.send(send_one, send_two)
        yield
        got = self.take()
        one, two = one + [got[0]], two + [got[1]]
        both = []
        for b in reversed(range(last)):
            mask = 2 << b
            one, send_one = self.halve(one, "wide", mask, 1)
            two, send_two = self.halve(two, "wide", mask, 1)
            if both:
                sent = add_up([jnp.concatenate([send_one[0], send_two[0]], axis=0)] + [pick(t, 1 - bit("wide", mask), 1) for t in both])
                both = [pick(t, bit("wide", mask), 1) for t in both]
            else:
                sent = jnp.concatenate([send_one[0], send_two[0]], axis=0)
            self.send((sent.astype(jnp.bfloat16), "wide", mask))
            yield
            both.append(self.take()[0])
        own = jnp.concatenate([add_up(one), add_up(two)], axis=0)
        share = add_up([own] + both).astype(jnp.bfloat16)
        self.send((share, "narrow", 2))
        yield
        (got,) = self.take()
        low = bit("narrow", 2) == 0
        pair = jnp.concatenate([jnp.where(low, share, got), jnp.where(low, got, share)], axis=0)
        self.send((pair, "narrow", 1))
        yield
        (got,) = self.take()
        low = bit("narrow", 1) == 0
        self.result = jnp.concatenate([jnp.where(low, pair, got), jnp.where(low, got, pair)], axis=0)
        yield

    def finish(self):
        for unused in self.steps:
            pass
        return self.result


def columns(tiles):
    return jnp.concatenate([tiles[i] for i in range(tiles.shape[0])], axis=1).astype(jnp.float32)


def small_sum(rows):
    low = rows.astype(jnp.bfloat16)
    for mask in (1, 2):
        low = (low.astype(jnp.float32) + swap(low, "narrow", mask).astype(jnp.float32)).astype(
            jnp.bfloat16
        )
    wide = lax.axis_size("wide")
    low = low.reshape((wide // 2, 2) + low.shape[1:])
    mine = bit("wide", 1)
    low = add_up([pick(low, mine, 1), swap(pick(low, 1 - mine, 1), "wide", 1)]).astype(jnp.bfloat16)
    place = lax.axis_index("wide") // 2
    return add_up(
        [pick(low, place, 0)]
        + [swap(pick(low, place ^ (m // 2), 0), "wide", m) for m in range(2, wide, 2)]
    )


def shards(
    tokens,
    cotangent,
    latents,
    added_noise,
    timesteps,
    bucket,
    masked,
    deal_start,
    first_gain,
    first_shift,
    joint_weight,
    query_value_bias,
    output_weight,
    output_bias,
    second_gain,
    second_shift,
    expand_weight,
    expand_bias,
    reduce_weight,
    reduce_bias,
    input_proj,
    cond_proj,
    time_first,
    time_second,
    block_mod,
    block_expand,
    block_reduce,
    final_mod,
    final_proj,
):
    wide = lax.axis_size("wide")
    narrow = lax.axis_size("narrow")
    place_wide = lax.axis_index("wide")
    place_narrow = lax.axis_index("narrow")
    core = bit("narrow", 1)
    mine, other = core[None], (1 - core)[None]
    image_index = place_wide * narrow + place_narrow
    at = jnp.stack([image_index, place_wide, place_narrow, jnp.int32(narrow)]).astype(jnp.int32)

    spot, live = places(at, bucket, deal_start, masked, wide)
    slots = spot.shape[1]
    steps = timesteps.astype(jnp.float32)
    half = time_first.shape[0] // 2
    freqs = jnp.exp(-math.log(10000.0) * jnp.arange(half).astype(jnp.float32) / half)
    angles = steps.reshape(-1, 1) * freqs
    sinus = jnp.concatenate([jnp.cos(angles), jnp.sin(angles)], axis=-1).astype(jnp.bfloat16)
    offset = steps * STEP_ANGLE
    keep_sig = jnp.cos(offset + SHIFT_ANGLE) / math.cos(SHIFT_ANGLE)
    drop_sig = jnp.sqrt(jnp.sin(offset) * jnp.sin(offset + 2.0 * SHIFT_ANGLE)) / math.cos(SHIFT_ANGLE)
    input_turned = input_proj.T
    final_turned = final_proj.T

    first_in, joint = joint_pass(
        tokens, first_gain, first_shift, joint_weight, query_value_bias
    )
    mixed, logsum = attend(at, bucket, joint)
    block_output, middle, second_in, active, slope, dealt, spread = feed_pass(
        at,
        bucket,
        mixed,
        tokens,
        latents,
        spot,
        (
            output_weight,
            output_bias,
            second_gain,
            second_shift,
            expand_weight,
            expand_bias,
            reduce_weight,
            reduce_bias,
        ),
    )

    def deal(array):
        shape = array.shape
        return lax.all_to_all(
            array.reshape(wide, -1, shape[1]), "wide", split_axis=0, concat_axis=0, tiled=True
        ).reshape(shape)

    dealt = deal(dealt)
    low_turned, time_slope, timed = time_embedding(sinus, time_first, time_second)
    (
        guess,
        left,
        fin_grad,
        branch_grad,
        upper_grad,
        mod_grad,
        timed_grad,
        embed_grad,
        rows_grad,
        input_grad,
        final_grad,
    ) = head_pass(
        dealt,
        timed,
        keep_sig[:, None, :],
        drop_sig[:, None, :],
        added_noise,
        live,
        (input_turned, cond_proj, block_mod, block_expand, block_reduce, final_mod, final_turned),
    )
    order = Order()
    order.at(rows_grad)
    one_args = (left, fin_grad, branch_grad, upper_grad)
    returned = deal(rows_grad)
    one = Flow(order, head_grads_one(OTHER, other, *one_args))
    one.own(head_grads_one(OWN, mine, order(left), *one_args[1:]))
    one.step()
    first_grad = time_back(order(timed_grad), time_second, time_slope)
    order.at(first_grad)
    two_args = (mod_grad, timed_grad, dealt, embed_grad, sinus, first_grad, wide)
    returned = order(returned)
    order.at(returned, first_grad)
    two = Flow(order, head_grads_two(OTHER, other, left, order(low_turned), *two_args))
    two.own(head_grads_two(OWN, mine, left, order(low_turned), *two_args))
    one.step()
    feed_grad, hidden_grad, middle_grad, out_grad, mixed_grad, feed_sums, hidden_sum = feed_back(
        at,
        bucket,
        order(cotangent),
        spot,
        middle,
        slope,
        returned,
        (output_weight, second_gain, expand_weight, reduce_weight),
    )
    order.at(mixed_grad)
    two.step()
    one.step()
    feed_args = (hidden_grad, active, feed_grad, wide)
    feed = Flow(order, feed_grads(OTHER, other, order(second_in), *feed_args))
    feed.own(feed_grads(OWN, mine, order(second_in), *feed_args))
    two.step()
    one.step()
    back_args = (at, bucket, joint)
    first_part = attend_back(0, PAIRS // 2, *back_args, order(mixed_grad), mixed, logsum)
    order.at(first_part[0])
    feed.step()
    two.step()
    one.step()
    second_part = attend_back(PAIRS // 2, PAIRS // 2, *back_args, order(mixed_grad), mixed, logsum)
    order.at(second_part[0])
    feed.step()
    one.step()
    qkv = tuple(a for pair in zip(first_part, second_part) for a in pair)
    last_args = (mixed,) + qkv + (out_grad,)
    last = Flow(order, last_grads(OTHER, other, order(first_in), *last_args))
    two.step()
    last.own(last_grads(OWN, mine, order(first_in), *last_args))
    feed.step()
    two.step()
    tokens_gradient, token_packed = tokens_back(
        order(tokens), qkv, middle_grad, first_gain, joint_weight, wide
    )
    order.at(token_packed)
    last.step()
    packed = pack(feed_sums, hidden_sum, input_grad, final_grad, order(token_packed), order.marks)
    order.at(packed)
    small = small_sum(packed)
    two.step()
    feed.step()
    last.step()
    feed.step()
    last.step()
    feed.step()
    one, two, feed, last = [flow.finish() for flow in (one, two, feed, last)]
    part = D // wide
    block = input_grad.shape[1] // wide
    vectors = [small[TOKEN_DIM + 1, i * part : (i + 1) * part] for i in range(4)]
    input_out = small[:TOKEN_DIM, :block].T
    final_out = small[:TOKEN_DIM, block : 2 * block].T
    late = small[TOKEN_DIM + 2]
    outs = [
        late[:part],
        late[part : 2 * part],
        late[2 * part :],
        vectors[3],
        vectors[1],
        vectors[2],
        small[TOKEN_DIM],
        vectors[0],
        input_out,
        final_out,
    ]
    final_mod_out = columns(one[:4])
    block_reduce_out = columns(one[4:6])
    block_expand_out = columns(one[6:])
    block_mod_out = columns(two[:12])
    time_second_out = columns(two[12:16])
    cut = cond_proj.shape[0] // wide
    cond_out = columns(two[16:, :cut])
    time_first_out = columns(two[16:, cut:])
    expand_out = columns(jnp.stack([feed[0], feed[1], feed[4], feed[5]]))
    pieces = jnp.stack([feed[2], feed[3], feed[6], feed[7]])
    rows = pieces.shape[1]
    pieces = pieces.reshape(2, 2, rows, 2, D // 2).transpose(1, 3, 2, 0, 4)
    reduce_out = pieces.reshape(4 * rows, D).astype(jnp.float32)
    joint_out = columns(last[:6])
    output_out = columns(last[6:])
    return (
        block_output,
        guess,
        spread[:2, 0].reshape(1, 2),
        tokens_gradient,
        outs[0],
        outs[1],
        joint_out,
        outs[2],
        output_out,
        outs[3],
        outs[4],
        outs[5],
        expand_out,
        outs[6],
        reduce_out,
        outs[7],
        outs[8],
        cond_out,
        time_first_out,
        time_second_out,
        block_mod_out,
        block_expand_out,
        block_reduce_out,
        final_mod_out,
        outs[9],
    )


def solution(mesh):
    in_specs = (
        P(("wide", "narrow"), None),
        P(("wide", "narrow"), None),
        P(("wide", "narrow"), None),
        P(None, None, ("wide", "narrow")),
        P(None, ("wide", "narrow")),
        P(),
        P(("wide", "narrow"), None),
        P(),
        P(),
        P(),
        P(),
        P(),
        P(),
        P(),
        P(),
        P(),
        P(),
        P(),
        P(),
        P(),
        P(),
        P(),
        P(),
        P(),
        P(),
        P(),
        P(),
        P(),
        P(),
    )
    out_specs = (
        P(("wide", "narrow"), None),
        P(None, None, ("wide", "narrow")),
        P(("wide", "narrow"), None),
        P(("wide", "narrow"), None),
        P("wide"),
        P("wide"),
        P("wide", None),
        P("wide"),
        P("wide", None),
        P("wide"),
        P("wide"),
        P("wide"),
        P("wide", None),
        P("wide"),
        P("wide", None),
        P("wide"),
        P("wide", None),
        P("wide", None),
        P("wide", None),
        P("wide", None),
        P("wide", None),
        P("wide", None),
        P("wide", None),
        P("wide", None),
        P("wide", None),
    )
    return jax.shard_map(shards, mesh=mesh, in_specs=in_specs, out_specs=out_specs, check_vma=False)
```

```python
from functools import partial
import math

import jax
import jax.numpy as jnp
from jax import lax
from jax.experimental import pallas as pl
from jax.experimental.pallas import tpu as pltpu
from jax.sharding import PartitionSpec as P

D = 768
HEADS = 12
HEAD_DIM = 64
TOKEN_DIM = 16
BUFFER = 64
IMAGE_MAX = 1024
MASK_MAX = 256
REPEATS = 4
SEQ = 1088


SHIFT_ANGLE = 0.008 / 1.008 * math.pi / 2.0
STEP_ANGLE = math.pi / (2.0 * 1.008 * 1000.0)
PAIRS = 6
VMEM = 60 * 1024 * 1024

OWN = pl.CostEstimate(flops=1 << 40, bytes_accessed=1 << 20, transcendentals=0)
OTHER = pl.CostEstimate(flops=0, bytes_accessed=1 << 20, transcendentals=0)


def nt(a,b): return lax.dot_general(a,b,(((1,),(1,)),((),())),preferred_element_type=jnp.float32)
def nn(a,b): return jnp.dot(a,b,preferred_element_type=jnp.float32)
def tn(a,b): return lax.dot_general(a,b,(((0,),(0,)),((),())),preferred_element_type=jnp.float32)
def normalize(values):
    centre = values - jnp.mean(values, axis=-1, keepdims=True)
    inverse = lax.rsqrt(jnp.mean(centre * centre, axis=-1, keepdims=True) + 1e-06)
    return (centre * inverse, inverse)


def normalize_back(grad_normed, normed, inverse):
    return inverse * (
        grad_normed
        - jnp.mean(grad_normed, axis=-1, keepdims=True)
        - normed * jnp.mean(grad_normed * normed, axis=-1, keepdims=True)
    )


def sigmoid(value):
    return 0.5 * jnp.tanh(0.5 * value) + 0.5


def silu_slope(value, sigma):
    return sigma * (1.0 + value * (1.0 - sigma))


def whole_block(shape):
    zeros = (0,) * len(shape)
    return pl.BlockSpec(shape, lambda *unused: zeros, pipeline_mode=pl.Buffered(1))


def time_kernel(sinus_ref, first_ref, second_ref, low_ref, slope_ref, timed_ref):
    first = nn(sinus_ref[...], first_ref[...])
    sigma = sigmoid(first)
    low = (first * sigma).astype(jnp.bfloat16)
    slope_ref[...] = silu_slope(first, sigma).astype(jnp.bfloat16)
    low_ref[...] = low.T
    timed_ref[...] = nn(low, second_ref[...])


def time_embedding(sinus, time_first, time_second):
    count, freq = sinus.shape
    width = time_first.shape[1]
    rows = count // REPEATS
    by_rows = pl.BlockSpec((rows, width), lambda i: (i, 0))
    return pl.pallas_call(
        time_kernel,
        grid=(REPEATS,),
        in_specs=[
            pl.BlockSpec((rows, freq), lambda i: (i, 0)),
            whole_block(time_first.shape),
            whole_block(time_second.shape),
        ],
        out_specs=[pl.BlockSpec((width, rows), lambda i: (0, i)), by_rows, by_rows],
        out_shape=[
            jax.ShapeDtypeStruct((width, count), jnp.bfloat16),
            jax.ShapeDtypeStruct((count, width), jnp.bfloat16),
            jax.ShapeDtypeStruct((count, width), jnp.float32),
        ],
        compiler_params=pltpu.CompilerParams(vmem_limit_bytes=VMEM),
        cost_estimate=OTHER,
        name="time_embedding",
    )(sinus, time_first, time_second)


def head_kernel(
    dealt_ref,
    timed_ref,
    keep_ref,
    drop_ref,
    noise_ref,
    live_ref,
    input_ref,
    cond_ref,
    mod_ref,
    expand_ref,
    reduce_ref,
    fin_ref,
    final_ref,
    guess_ref,
    left_ref,
    fin_grad_ref,
    branch_grad_ref,
    upper_grad_ref,
    mod_grad_ref,
    timed_grad_ref,
    embed_grad_ref,
    rows_grad_ref,
    input_grad_ref,
    final_grad_ref,
    embed_scratch,
    total_scratch,
):
    turn = pl.program_id(0)
    width = timed_ref.shape[1]

    @pl.when(turn == 0)
    def _():
        embed_scratch[...] = nn(dealt_ref[:, :D], cond_ref[...])
        total_scratch[...] = jnp.zeros_like(total_scratch)
        input_grad_ref[...] = jnp.zeros_like(input_grad_ref)
        final_grad_ref[...] = jnp.zeros_like(final_grad_ref)

    cond = embed_scratch[...] + timed_ref[...]
    acted = (cond * sigmoid(cond)).astype(jnp.bfloat16)
    left_ref[0] = acted.T
    start = dealt_ref[:, D:].astype(jnp.float32).T[:TOKEN_DIM]
    noise = noise_ref[0]
    noisy = (keep_ref[0] * start + drop_ref[0] * noise).astype(jnp.bfloat16)
    entry = tn(noisy, input_ref[...])
    inner_normed, inner_inverse = normalize(entry)
    shift_a = nn(acted, mod_ref[:, :width])
    scale_a = nn(acted, mod_ref[:, width : 2 * width])
    gate_a = nn(acted, mod_ref[:, 2 * width :])
    inner = (inner_normed * (1.0 + scale_a) + shift_a).astype(jnp.bfloat16)
    left_ref[2] = inner.T
    upper = nn(inner, expand_ref[...])
    upper_sigma = sigmoid(upper)
    lifted = (upper * upper_sigma).astype(jnp.bfloat16)
    left_ref[1] = lifted.T
    branch = nn(lifted, reduce_ref[...])
    shift_b = nn(acted, fin_ref[:, :width])
    scale_b = nn(acted, fin_ref[:, width:])
    last_normed, last_inverse = normalize(entry + gate_a * branch)
    last = (last_normed * (1.0 + scale_b) + shift_b).astype(jnp.bfloat16)
    live = live_ref[...]
    guess = nt(final_ref[...], last) * live
    guess_ref[0] = guess
    guess_grad = (2.0 / REPEATS * (guess - noise * live) * live).astype(jnp.bfloat16)
    final_grad_ref[...] += nn(guess_grad, last)
    last_grad = tn(guess_grad, final_ref[...])
    fin_grad = jnp.concatenate([last_grad, last_grad * last_normed], axis=1).astype(jnp.bfloat16)
    fin_grad_ref[...] = fin_grad
    after_grad = normalize_back(last_grad * (1.0 + scale_b), last_normed, last_inverse)
    branch_grad = (after_grad * gate_a).astype(jnp.bfloat16)
    branch_grad_ref[...] = branch_grad
    lifted_grad = nt(branch_grad, reduce_ref[...])
    upper_grad = (lifted_grad * silu_slope(upper, upper_sigma)).astype(jnp.bfloat16)
    upper_grad_ref[...] = upper_grad
    inner_grad = nt(upper_grad, expand_ref[...])
    entry_grad = (
        after_grad + normalize_back(inner_grad * (1.0 + scale_a), inner_normed, inner_inverse)
    ).astype(jnp.bfloat16)
    input_grad_ref[...] += nn(noisy, entry_grad)
    mod_grad = jnp.concatenate(
        [inner_grad, inner_grad * inner_normed, after_grad * branch], axis=1
    ).astype(jnp.bfloat16)
    mod_grad_ref[...] = mod_grad
    acted_grad = nt(mod_grad, mod_ref[...]) + nt(fin_grad, fin_ref[...])
    cond = embed_scratch[...] + timed_ref[...]
    cond_grad = acted_grad * silu_slope(cond, sigmoid(cond))
    timed_grad_ref[...] = cond_grad.astype(jnp.bfloat16)
    total_scratch[...] += cond_grad

    @pl.when(turn == REPEATS - 1)
    def _():
        embed_grad = total_scratch[...].astype(jnp.bfloat16)
        embed_grad_ref[...] = embed_grad
        rows_grad_ref[...] = nt(embed_grad, cond_ref[...]).astype(jnp.bfloat16)


def head_pass(dealt, timed, keep_sig, drop_sig, noise, live, weights):
    input_proj, cond_proj, block_mod, block_expand, block_reduce, final_mod, final_proj = weights
    slots = dealt.shape[0]
    width = cond_proj.shape[1]
    count = REPEATS * slots
    by_rows = lambda n: pl.BlockSpec((slots, n), lambda i: (i, 0))
    by_turn = lambda a: pl.BlockSpec((1,) + a, lambda i: (i, 0, 0))
    low = lambda *s: jax.ShapeDtypeStruct(s, jnp.bfloat16)
    full = lambda *s: jax.ShapeDtypeStruct(s, jnp.float32)
    operands = (
        dealt,
        timed,
        keep_sig,
        drop_sig,
        noise,
        live,
        input_proj,
        cond_proj,
        block_mod,
        block_expand,
        block_reduce,
        final_mod,
        final_proj,
    )
    return pl.pallas_call(
        head_kernel,
        grid=(REPEATS,),
        in_specs=[
            whole_block(dealt.shape),
            by_rows(width),
            by_turn((1, slots)),
            by_turn((1, slots)),
            by_turn((TOKEN_DIM, slots)),
        ]
        + [whole_block(a.shape) for a in operands[5:]],
        out_specs=[
            by_turn((TOKEN_DIM, slots)),
            pl.BlockSpec((3, width, slots), lambda i: (0, 0, i)),
            by_rows(2 * width),
            by_rows(width),
            by_rows(width),
            by_rows(3 * width),
            by_rows(width),
            whole_block((slots, width)),
            whole_block((slots, D)),
            whole_block((TOKEN_DIM, width)),
            whole_block((TOKEN_DIM, width)),
        ],
        out_shape=[
            full(REPEATS, TOKEN_DIM, slots),
            low(3, width, count),
            low(count, 2 * width),
            low(count, width),
            low(count, width),
            low(count, 3 * width),
            low(count, width),
            low(slots, width),
            low(slots, D),
            full(TOKEN_DIM, width),
            full(TOKEN_DIM, width),
        ],
        scratch_shapes=[pltpu.VMEM((slots, width), jnp.float32)] * 2,
        compiler_params=pltpu.CompilerParams(vmem_limit_bytes=VMEM),
        cost_estimate=OTHER,
        name="head_pass",
    )(*operands)


MARK = jax.ShapeDtypeStruct((8, 128), jnp.float32)


def head_grads_one_kernel(half_ref, left_ref, fin_ref, branch_ref, upper_ref, *refs):
    turn = pl.program_id(0)
    tile = head_one_tile(turn, half_ref)

    def put(grad):
        if len(refs) == 2:
            out_ref, mark_ref = refs
            out_ref[0] = grad.astype(jnp.bfloat16)
        else:
            got_ref, sent_ref, kept_ref, mark_ref = refs
            grad = (grad + got_ref[0].astype(jnp.float32)).astype(jnp.bfloat16)

            @pl.when(turn < 2)
            def _():
                sent_ref[0] = grad

            @pl.when(turn >= 2)
            def _():
                kept_ref[0] = grad

        mark_ref[...] = jnp.zeros_like(mark_ref)

    @pl.when(tile < 4)
    def _():
        put(nn(left_ref[0], fin_ref[...]))

    @pl.when((tile >= 4) & (tile < 6))
    def _():
        put(nn(left_ref[0], branch_ref[...]))

    @pl.when(tile >= 6)
    def _():
        put(nn(left_ref[0], upper_ref[...]))


def head_one_tile(turn, half):
    return half[0] * 4 + (turn ^ (2 - 2 * half[1]))


def head_grads_one(half, left, fin_grad, branch_grad, upper_grad, got=None):
    width, count = left.shape[1:]
    cols = width // 2

    def at(first, tiles):
        return lambda i, half: (0, jnp.clip(head_one_tile(i, half) - first, 0, tiles - 1))

    def which(i, half):
        tile = head_one_tile(i, half)
        return (jnp.where(tile < 4, 0, jnp.where(tile < 6, 1, 2)), 0, 0)

    tiles = lambda n: jax.ShapeDtypeStruct((n, width, cols), jnp.bfloat16)
    block = lambda where: pl.BlockSpec((1, width, cols), where)
    if got is None:
        more = ()
        outs = [(block(lambda i, half: (i ^ (2 - 2 * half[1]), 0, 0)), tiles(4))]
    else:
        more = (got,)
        outs = [
            (block(lambda i, half: (jnp.minimum(i, 1), 0, 0)), tiles(2)),
            (block(lambda i, half: (jnp.maximum(i - 2, 0), 0, 0)), tiles(2)),
        ]
    outs.append((whole_block((8, 128)), MARK))
    return pl.pallas_call(
        head_grads_one_kernel,
        grid_spec=pltpu.PrefetchScalarGridSpec(
            num_scalar_prefetch=1,
            grid=(4,),
            in_specs=[
                pl.BlockSpec((1, width, count), which),
                pl.BlockSpec((count, cols), at(0, 4)),
                pl.BlockSpec((count, cols), at(4, 2)),
                pl.BlockSpec((count, cols), at(6, 2)),
            ]
            + [block(lambda i, half: (i ^ (2 - 2 * half[1]), 0, 0))] * len(more),
            out_specs=[o[0] for o in outs],
        ),
        out_shape=[o[1] for o in outs],
        compiler_params=pltpu.CompilerParams(vmem_limit_bytes=VMEM),
        cost_estimate=OTHER if got is None else OWN,
        name="head_grads_one",
    )(half, left, fin_grad, branch_grad, upper_grad, *more)


def time_back_kernel(grad_ref, weight_ref, slope_ref, out_ref):
    grad = nt(grad_ref[...], weight_ref[...])
    out_ref[...] = (grad * slope_ref[...].astype(jnp.float32)).astype(jnp.bfloat16)


def time_back(timed_grad, weight, slope):
    count, width = timed_grad.shape
    by_rows = pl.BlockSpec((count // 4, width), lambda i: (i, 0))
    return pl.pallas_call(
        time_back_kernel,
        grid=(4,),
        in_specs=[by_rows, whole_block(weight.shape), by_rows],
        out_specs=by_rows,
        out_shape=jax.ShapeDtypeStruct((count, width), jnp.bfloat16),
        compiler_params=pltpu.CompilerParams(vmem_limit_bytes=VMEM),
        cost_estimate=OTHER,
        name="time_back",
    )(timed_grad, weight, slope)


def split_rows(grad, wide, y):
    grad = grad.reshape((wide // 2, 2, -1) + grad.shape[1:])
    own, other = jnp.where(y == 0, grad[:, 0], grad[:, 1]), jnp.where(y == 0, grad[:, 1], grad[:, 0])
    flat = lambda a: a.reshape((-1,) + a.shape[2:]).astype(jnp.bfloat16)
    return flat(other), flat(own)


def head_grads_two_kernel(
    wide, half_ref, acted_ref, low_ref, mod_ref, timed_ref, rows_ref, embed_ref, sinus_ref, first_ref, *refs
):
    turn = pl.program_id(0)
    tile = half_ref[0] * 10 + head_two_tile(turn, half_ref)

    def put(grad):
        refs[-1][...] = jnp.zeros_like(refs[-1])
        if len(refs) == 2:
            refs[0][0] = grad.astype(jnp.bfloat16)
            return
        got_ref, sent_one, kept_one, sent_two, kept_two, unused = refs
        grad = grad + got_ref[0].astype(jnp.float32)

        @pl.when(turn < 2)
        def _():
            sent_one[0] = grad.astype(jnp.bfloat16)

        @pl.when((turn >= 5) & (turn < 7))
        def _():
            kept_one[0] = grad.astype(jnp.bfloat16)

        @pl.when(turn % 5 >= 2)
        def _():
            sent_two[0], kept_two[0] = split_rows(grad, wide, half_ref[2])

    @pl.when(tile < 12)
    def _():
        put(nn(acted_ref[0], mod_ref[...]))

    @pl.when((tile >= 12) & (tile < 16))
    def _():
        put(nn(low_ref[...], timed_ref[...]))

    @pl.when(tile >= 16)
    def _():
        cond = tn(rows_ref[:, :D], embed_ref[...])
        time = tn(sinus_ref[...], first_ref[...])
        cols = cond.shape[1]
        both = jnp.concatenate(
            [cond.reshape(wide, -1, cols), time.reshape(wide, -1, cols)], axis=1
        )
        put(both.reshape(-1, cols))


def head_two_tile(turn, half):
    return (turn // 5 ^ (1 - half[1])) * 5 + turn % 5


def head_grads_two(half, left, low, mod_grad, timed_grad, dealt, embed_grad, sinus, first_grad, wide, got=None):
    width, count = left.shape[1:]
    slots = dealt.shape[0]
    cols = width // 4

    def at(first, tiles):
        return lambda i, half: (0, jnp.clip(half[0] * 10 + head_two_tile(i, half) - first, 0, tiles - 1))

    whole = pl.BlockSpec((1, width, cols), lambda i, half: (head_two_tile(i, half), 0, 0))
    like = lambda n, rows: jax.ShapeDtypeStruct((n, rows, cols), jnp.bfloat16)
    if got is None:
        more = ()
        outs = [(whole, like(10, width))]
    else:
        more = (got,)
        block = lambda rows, where: pl.BlockSpec((1, rows, cols), where)

        def second(i, half):
            return ((i // 5 ^ (1 - half[1])) * 3 + jnp.maximum(i % 5 - 2, 0), 0, 0)

        outs = [
            (block(width, lambda i, half: (jnp.minimum(i, 1), 0, 0)), like(2, width)),
            (block(width, lambda i, half: (jnp.clip(i - 5, 0, 1), 0, 0)), like(2, width)),
            (block(width // 2, second), like(6, width // 2)),
            (block(width // 2, second), like(6, width // 2)),
        ]
    outs.append((whole_block((8, 128)), MARK))
    return pl.pallas_call(
        partial(head_grads_two_kernel, wide),
        grid_spec=pltpu.PrefetchScalarGridSpec(
            num_scalar_prefetch=1,
            grid=(10,),
            in_specs=[
                whole_block((1, width, count)),
                whole_block((width, count)),
                pl.BlockSpec((count, cols), at(0, 12)),
                pl.BlockSpec((count, cols), at(12, 4)),
                whole_block(dealt.shape),
                pl.BlockSpec((slots, cols), at(16, 4)),
                whole_block(sinus.shape),
                pl.BlockSpec((count, cols), at(16, 4)),
            ]
            + [whole] * len(more),
            out_specs=[o[0] for o in outs],
        ),
        out_shape=[o[1] for o in outs],
        compiler_params=pltpu.CompilerParams(vmem_limit_bytes=VMEM),
        cost_estimate=OTHER if got is None else OWN,
        name="head_grads_two",
    )(half, left, low, mod_grad, timed_grad, dealt, embed_grad, sinus, first_grad, *more)


def attend_kernel(QB, at_ref, bucket_ref, q_ref, k_ref, v_ref, o_ref, lse_ref):
    length=BUFFER + bucket_ref[at_ref[0]]
    low=lax.broadcasted_iota(jnp.int32,(1,128),1)<64
    bias=jnp.where(lax.broadcasted_iota(jnp.int32,(1,SEQ),1)<length,0.0,-1e30).astype(jnp.float32)
    k=k_ref[...]; v=v_ref[...]
    one=jnp.ones((),v.dtype); zero=jnp.zeros((),v.dtype)
    vs=(jnp.where(low,v,one),jnp.where(low,one,v))
    for b in range(SEQ//QB):
        rows=pl.ds(b*QB,QB)
        q=q_ref[rows,:]
        outs=[];lses=[]
        for h in range(2):
            qh=jnp.where(low,q,zero) if h==0 else jnp.where(low,zero,q)
            s=nt(qh,k)+bias
            top=jnp.max(s,axis=1,keepdims=True)
            p=jnp.exp(s-top).astype(jnp.bfloat16)
            o=nn(p,vs[h])
            total=pltpu.roll(o,64,1)
            outs.append(o/total)
            lses.append(top+jnp.log(total))
        o_ref[rows,:]=jnp.where(low,outs[0],outs[1]).astype(jnp.bfloat16)
        lse_ref[rows,:]=jnp.where(low,lses[0],lses[1])

def attend(at,bucket,joint,QB=272):
    spec=lambda off: pl.BlockSpec((SEQ,128),lambda i,off=off:(0,i+off))
    return pl.pallas_call(partial(attend_kernel,QB),
        grid=(PAIRS,),
        in_specs=[smem(),smem(),spec(0),spec(6),spec(12)],
        out_specs=[spec(0),spec(0)],
        out_shape=[jax.ShapeDtypeStruct((SEQ,D),jnp.bfloat16),jax.ShapeDtypeStruct((SEQ,D),jnp.float32)],
        compiler_params=pltpu.CompilerParams(vmem_limit_bytes=VMEM),
        cost_estimate=OTHER,
        name='attend')(at,bucket,joint,joint,joint)

def attend_back_kernel(KB, at_ref, bucket_ref,q_ref,k_ref,v_ref,do_ref,o_ref,lse_ref,grads_ref,ds_ref):
    length=BUFFER + bucket_ref[at_ref[0]]
    low=lax.broadcasted_iota(jnp.int32,(1,128),1)<64
    q=q_ref[...]; do=do_ref[...]
    zero=jnp.zeros((),q.dtype)
    prod=do.astype(jnp.float32)*o_ref[...].astype(jnp.float32)
    prodT=prod.T
    lseT=lse_ref[...].T
    deltas=(jnp.sum(prodT[:64],axis=0,keepdims=True),jnp.sum(prodT[64:],axis=0,keepdims=True))
    lses=(lseT[0:1],lseT[64:65])
    for b in range(SEQ//KB):
        rows=pl.ds(b*KB,KB)
        k=k_ref[rows,:]; v=v_ref[rows,:]
        bias=jnp.where(lax.broadcasted_iota(jnp.int32,(KB,1),0)+b*KB<length,0.0,-1e30).astype(jnp.float32)
        dks=[];dvs=[]
        for h in range(2):
            pick=(lambda a: jnp.where(low,a,zero)) if h==0 else (lambda a: jnp.where(low,zero,a))
            s=nt(pick(k),q)+bias
            p=jnp.exp(s-lses[h])
            dp=nt(pick(v),do)
            ds=(p*(dp-deltas[h])).astype(jnp.bfloat16)
            dvs.append(nn(p.astype(jnp.bfloat16),do))
            dks.append(nn(ds,q))
            ds_ref[h,rows,:]=ds
        grads_ref[1,rows,:]=jnp.where(low,dks[0],dks[1]).astype(jnp.bfloat16)
        grads_ref[2,rows,:]=jnp.where(low,dvs[0],dvs[1]).astype(jnp.bfloat16)
    kT=k_ref[...].astype(jnp.float32).T.astype(jnp.bfloat16)
    dqT=jnp.concatenate([nn(kT[64*h:64*h+64],ds_ref[h]) for h in range(2)],axis=0)
    grads_ref[0]=(dqT.T*0.125).astype(jnp.bfloat16)

def attend_back(first,count,at,bucket,joint,do,o,lse,KB=544):
    spec=lambda off: pl.BlockSpec((SEQ,128),lambda i,off=off:(0,i+off))
    return pl.pallas_call(partial(attend_back_kernel,KB),
        grid=(count,),
        in_specs=[smem(),smem(),spec(first),spec(6+first),spec(12+first),spec(first),spec(first),spec(first)],
        out_specs=pl.BlockSpec((3,SEQ,128),lambda i:(0,0,i)),
        out_shape=jax.ShapeDtypeStruct((3,SEQ,count*128),jnp.bfloat16),
        scratch_shapes=[pltpu.VMEM((2,SEQ,SEQ),jnp.bfloat16)],
        compiler_params=pltpu.CompilerParams(vmem_limit_bytes=VMEM),
        cost_estimate=OWN,
        name="attend_back")(at,bucket,joint,joint,joint,do,o,lse)


def line(ref):
    return ref[...].reshape(1, ref.shape[0])


def smem():
    return pl.BlockSpec(memory_space=pltpu.SMEM)


def place_kernel(wide, at_ref, bucket_ref, start_ref, chosen_ref, spot_ref, live_ref):
    image, place_wide, place_narrow, narrow = at_ref[0], at_ref[1], at_ref[2], at_ref[3]
    seq = chosen_ref.shape[1]
    slots = live_ref.shape[1]
    shift = wide.bit_length() - 1
    deep = slots // wide
    deep_shift = deep.bit_length() - 1
    row = lax.broadcasted_iota(jnp.int32, (seq, seq), 0)
    column = lax.broadcasted_iota(jnp.int32, (seq, seq), 1)
    lower = (column <= row).astype(jnp.float32).astype(jnp.bfloat16)
    chosen = jnp.broadcast_to(chosen_ref[...], (8, seq)).astype(jnp.float32).astype(jnp.bfloat16)
    counted = nt(lower, chosen)
    first_row = lax.broadcasted_iota(jnp.int32, counted.shape, 0) == 0
    before = jnp.where(first_row, 0.0, pltpu.roll(counted, 1, 0))
    is_chosen = (counted - before)[:, :1] > 0.5
    order = counted[:, :1].astype(jnp.int32) - 1
    target = ((start_ref[image] + order) & (wide - 1)) * deep + (order >> shift)
    target = jnp.where(is_chosen, target, -1)
    slot = lax.broadcasted_iota(jnp.int32, (seq, slots), 1)
    spot_ref[...] = (slot == target).astype(jnp.float32).astype(jnp.bfloat16)
    lane = lax.broadcasted_iota(jnp.int32, (1, slots), 1)
    live = jnp.zeros((1, slots), jnp.float32)
    for source in range(wide):
        other = source * narrow + place_narrow
        count = bucket_ref[other] * MASK_MAX // IMAGE_MAX
        rank = (place_wide - start_ref[other]) & (wide - 1)
        arrived = jnp.maximum((count - rank + wide - 1) >> shift, 0)
        inside = ((lane >> deep_shift) == source) & ((lane & (deep - 1)) < arrived)
        live = jnp.where(inside, 1.0, live)
    live_ref[...] = live


def places(at, bucket, deal_start, masked, wide):
    seq = masked.shape[1]
    return pl.pallas_call(
        partial(place_kernel, wide),
        in_specs=[smem(), smem(), smem(), whole_block((1, seq))],
        out_specs=[whole_block((seq, MASK_MAX)), whole_block((1, MASK_MAX))],
        grid=(1,),
        out_shape=[
            jax.ShapeDtypeStruct((seq, MASK_MAX), jnp.bfloat16),
            jax.ShapeDtypeStruct((1, MASK_MAX), jnp.float32),
        ],
        compiler_params=pltpu.CompilerParams(vmem_limit_bytes=VMEM),
        cost_estimate=OTHER,
        name="places",
    )(at, bucket, deal_start, masked)


def joint_kernel(tokens_ref, gain_ref, shift_ref, weight_ref, bias_ref, first_ref, joint_ref):
    normed, unused = normalize(tokens_ref[...].astype(jnp.float32))
    first = (normed * line(gain_ref) + line(shift_ref)).astype(jnp.bfloat16)
    first_ref[...] = first
    for part in range(3):
        cols = slice(part * D, (part + 1) * D)
        out = nn(first, weight_ref[:, cols])
        if part != 1:
            out = out + line(bias_ref)[:, part // 2 * D : part // 2 * D + D]
        out = out.astype(jnp.bfloat16)
        if part == 0:
            out = out * jnp.bfloat16(HEAD_DIM ** (-0.5))
        joint_ref[:, cols] = out


ROWS = 272


def by_block(columns):
    return pl.BlockSpec((ROWS, columns), lambda i: (i, 0))


def joint_pass(tokens, gain, shift, weight, bias):
    seq = tokens.shape[0]
    return pl.pallas_call(
        joint_kernel,
        grid=(seq // ROWS,),
        in_specs=[by_block(D)] + [whole_block(a.shape) for a in (gain, shift, weight, bias)],
        out_specs=[by_block(D), by_block(3 * D)],
        out_shape=[
            jax.ShapeDtypeStruct((seq, D), jnp.bfloat16),
            jax.ShapeDtypeStruct((seq, 3 * D), jnp.bfloat16),
        ],
        compiler_params=pltpu.CompilerParams(vmem_limit_bytes=VMEM),
        cost_estimate=OTHER,
        name="joint_pass",
    )(tokens, gain, shift, weight, bias)


def gelu_parts(value):
    size = jnp.abs(value)
    bell = jnp.exp(-0.5 * value * value)
    step = 1.0 / (1.0 + (0.3275911 * math.sqrt(0.5)) * size)
    tail = 0.5 * 1.061405429 * step - 0.5 * 1.453152027
    tail = tail * step + 0.5 * 1.421413741
    tail = tail * step - 0.5 * 0.284496736
    tail = tail * step + 0.5 * 0.254829592
    tail = tail * step * bell
    return jnp.where(value < 0.0, tail, 1.0 - tail), bell * (1.0 / math.sqrt(2.0 * math.pi))


def keep_column(at_ref, bucket_ref, rows):
    position = lax.broadcasted_iota(jnp.int32, (rows, 1), 0) + pl.program_id(0) * rows
    return (position < BUFFER + bucket_ref[at_ref[0]]).astype(jnp.float32)


def feed_kernel(
    at_ref,
    bucket_ref,
    mixed_ref,
    tokens_ref,
    latent_ref,
    spot_ref,
    out_w_ref,
    out_b_ref,
    gain_ref,
    shift_ref,
    expand_ref,
    expand_b_ref,
    reduce_ref,
    reduce_b_ref,
    output_ref,
    middle_ref,
    second_ref,
    active_ref,
    slope_ref,
    dealt_ref,
    spread_ref,
    dealt_scratch,
    spread_scratch,
):
    step = pl.program_id(0)

    @pl.when(step == 0)
    def _():
        dealt_scratch[...] = jnp.zeros_like(dealt_scratch)
        spread_scratch[...] = jnp.zeros_like(spread_scratch)

    keep = keep_column(at_ref, bucket_ref, mixed_ref.shape[0])
    branch = nn(mixed_ref[...], out_w_ref[...]) + line(out_b_ref)
    middle = tokens_ref[...].astype(jnp.float32) + branch
    middle_ref[...] = middle
    normed, unused = normalize(middle)
    second = (normed * line(gain_ref) + line(shift_ref)).astype(jnp.bfloat16)
    second_ref[...] = second
    hidden_width = expand_ref.shape[1]
    expand_b = line(expand_b_ref)
    feed = line(reduce_b_ref)
    for part in range(hidden_width // D):
        cols = slice(part * D, (part + 1) * D)
        hidden = nn(second, expand_ref[:, cols]) + expand_b[:, cols]
        phi, density = gelu_parts(hidden)
        active = (hidden * phi).astype(jnp.bfloat16)
        active_ref[:, cols] = active
        slope_ref[:, cols] = (phi + hidden * density).astype(jnp.bfloat16)
        feed = feed + nn(active, reduce_ref[cols, :])
    output = ((middle + feed) * keep).astype(jnp.bfloat16)
    output_ref[...] = output
    spread_scratch[0:1, :] += jnp.sum(keep * branch * branch, axis=0, keepdims=True)
    spread_scratch[1:2, :] += jnp.sum(keep * feed * feed, axis=0, keepdims=True)
    spot = spot_ref[...]
    dealt_scratch[:, :D] += tn(spot, output)
    dealt_scratch[:, D : D + TOKEN_DIM] += tn(spot, latent_ref[...])

    @pl.when(step == pl.num_programs(0) - 1)
    def _():
        dealt_ref[...] = dealt_scratch[...].astype(jnp.bfloat16)
        count = (BUFFER + bucket_ref[at_ref[0]]).astype(jnp.float32) * D
        total = jnp.sum(spread_scratch[...], axis=1, keepdims=True)
        spread_ref[...] = jnp.sqrt(jnp.broadcast_to(total, spread_ref.shape) / count)


def feed_pass(at, bucket, mixed, tokens, latents, spot, weights):
    seq = tokens.shape[0]
    slots = spot.shape[1]
    hidden = weights[4].shape[1]
    low = lambda *s: jax.ShapeDtypeStruct(s, jnp.bfloat16)
    full = lambda *s: jax.ShapeDtypeStruct(s, jnp.float32)
    return pl.pallas_call(
        feed_kernel,
        grid=(seq // ROWS,),
        in_specs=[smem(), smem(), by_block(D), by_block(D), by_block(TOKEN_DIM), by_block(slots)]
        + [whole_block(a.shape) for a in weights],
        out_specs=[
            by_block(D),
            by_block(D),
            by_block(D),
            by_block(hidden),
            by_block(hidden),
            whole_block((slots, D + 128)),
            whole_block((8, 128)),
        ],
        out_shape=[
            low(seq, D),
            full(seq, D),
            low(seq, D),
            low(seq, hidden),
            low(seq, hidden),
            low(slots, D + 128),
            full(8, 128),
        ],
        scratch_shapes=[pltpu.VMEM((slots, D + 128), jnp.float32), pltpu.VMEM((8, D), jnp.float32)],
        compiler_params=pltpu.CompilerParams(vmem_limit_bytes=VMEM),
        cost_estimate=OTHER,
        name="feed_pass",
    )(at, bucket, mixed, tokens, latents, spot, *weights)


def feed_back_kernel(
    at_ref,
    bucket_ref,
    cot_ref,
    spot_ref,
    middle_ref,
    slope_ref,
    returned_ref,
    out_w_ref,
    gain_ref,
    expand_ref,
    reduce_ref,
    feed_grad_ref,
    hidden_grad_ref,
    middle_grad_ref,
    branch_grad_ref,
    mixed_grad_ref,
    sums_ref,
    wide_sum_ref,
):
    @pl.when(pl.program_id(0) == 0)
    def _():
        sums_ref[...] = jnp.zeros_like(sums_ref)
        wide_sum_ref[...] = jnp.zeros_like(wide_sum_ref)

    def add_sum(row, value):
        sums_ref[row : row + 1, :] += jnp.sum(value, axis=0, keepdims=True)

    keep = keep_column(at_ref, bucket_ref, cot_ref.shape[0])
    grad = (cot_ref[...].astype(jnp.float32) + nn(spot_ref[...], returned_ref[...])) * keep
    feed_grad = grad.astype(jnp.bfloat16)
    feed_grad_ref[...] = feed_grad
    add_sum(0, feed_grad.astype(jnp.float32))
    second_grad = jnp.zeros(grad.shape, jnp.float32)
    for part in range(expand_ref.shape[1] // D):
        cols = slice(part * D, (part + 1) * D)
        active_grad = nt(feed_grad, reduce_ref[cols, :])
        hidden_grad = (active_grad * slope_ref[:, cols].astype(jnp.float32)).astype(jnp.bfloat16)
        hidden_grad_ref[:, cols] = hidden_grad
        wide_sum_ref[:, cols] += jnp.sum(hidden_grad.astype(jnp.float32), axis=0, keepdims=True)
        second_grad = second_grad + nt(hidden_grad, expand_ref[:, cols])
    normed, inverse = normalize(middle_ref[...])
    add_sum(1, second_grad * normed)
    add_sum(2, second_grad)
    middle_grad = grad + normalize_back(second_grad * line(gain_ref), normed, inverse)
    middle_grad_ref[...] = middle_grad
    branch_grad = middle_grad.astype(jnp.bfloat16)
    branch_grad_ref[...] = branch_grad
    add_sum(3, branch_grad.astype(jnp.float32))
    mixed_grad_ref[...] = nt(branch_grad, out_w_ref[...]).astype(jnp.bfloat16)


def feed_back(at, bucket, cotangent, spot, middle, slope, returned, weights):
    seq = cotangent.shape[0]
    slots = spot.shape[1]
    hidden = slope.shape[1]
    low = lambda *s: jax.ShapeDtypeStruct(s, jnp.bfloat16)
    full = lambda *s: jax.ShapeDtypeStruct(s, jnp.float32)
    return pl.pallas_call(
        feed_back_kernel,
        grid=(seq // ROWS,),
        in_specs=[smem(), smem(), by_block(D), by_block(slots), by_block(D), by_block(hidden)]
        + [whole_block(a.shape) for a in (returned,) + weights],
        out_specs=[
            by_block(D),
            by_block(hidden),
            by_block(D),
            by_block(D),
            by_block(D),
            whole_block((8, D)),
            whole_block((1, hidden)),
        ],
        out_shape=[
            low(seq, D),
            low(seq, hidden),
            full(seq, D),
            low(seq, D),
            low(seq, D),
            full(8, D),
            full(1, hidden),
        ],
        compiler_params=pltpu.CompilerParams(vmem_limit_bytes=VMEM),
        cost_estimate=OTHER,
        name="feed_back",
    )(at, bucket, cotangent, spot, middle, slope, returned, *weights)


def feed_grads_kernel(wide, half_ref, second_ref, hidden_ref, active_ref, grad_ref, *refs):
    step = pl.program_id(0)
    refs[-1][...] = jnp.zeros_like(refs[-1])

    @pl.when(step < 2)
    def _():
        grad = tn(second_ref[...], hidden_ref[...])
        if len(refs) == 3:
            refs[0][0] = grad.astype(jnp.bfloat16)
        else:
            grad = (grad + refs[0][0].astype(jnp.float32)).astype(jnp.bfloat16)

            @pl.when(step == 0)
            def _():
                refs[2][...] = grad[None]

            @pl.when(step == 1)
            def _():
                refs[3][...] = grad[None]

    @pl.when(step >= 2)
    def _():
        whole = tn(active_ref[...], grad_ref[...])
        pieces = 4
        rows = D // wide
        places = whole.shape[0] // (pieces * rows)
        whole = whole.reshape(places, pieces, rows, D // 2)
        for piece in range(pieces):
            at = (piece // 2, slice(None), slice(piece % 2 * (D // 2), (piece % 2 + 1) * (D // 2)))
            part = whole[:, piece].reshape(places * rows, D // 2)
            if len(refs) == 3:
                refs[1][at] = part.astype(jnp.bfloat16)
            else:
                part = part + refs[1][at].astype(jnp.float32)
                refs[4][at], refs[5][at] = split_rows(part, places, half_ref[2])


def feed_grads(half, second, hidden_grad, active, feed_grad, wide, got=None):
    seq, hidden = active.shape
    chunk = lambda i: jnp.maximum(i - 2, 0)
    turned = lambda i, half: jnp.minimum(i, 1) ^ (1 - half[1])
    low = lambda *s: jax.ShapeDtypeStruct(s, jnp.bfloat16)
    expand_tile = pl.BlockSpec((1, D, D), lambda i, half: (turned(i, half), 0, 0))
    rows_of = lambda rows: pl.BlockSpec((2, rows, D), lambda i, half: (0, chunk(i), 0))
    if got is None:
        more = ()
        outs = [(expand_tile, low(2, D, D)), (rows_of(D // 4), low(2, D, D))]
    else:
        more = tuple(got)
        outs = [(whole_block((1, D, D)), low(1, D, D))] * 2
        outs += [(rows_of(D // 8), low(2, D // 2, D))] * 2
    outs.append((whole_block((8, 128)), MARK))
    return pl.pallas_call(
        partial(feed_grads_kernel, wide),
        grid_spec=pltpu.PrefetchScalarGridSpec(
            num_scalar_prefetch=1,
            grid=(6,),
            in_specs=[
                whole_block((seq, D)),
                pl.BlockSpec((seq, D), lambda i, half: (0, half[0] * 2 + turned(i, half))),
                pl.BlockSpec((seq, D), lambda i, half: (0, chunk(i))),
                pl.BlockSpec((seq, D // 2), lambda i, half: (0, half[0])),
            ]
            + [expand_tile, rows_of(D // 4)][: len(more)],
            out_specs=[o[0] for o in outs],
        ),
        out_shape=[o[1] for o in outs],
        compiler_params=pltpu.CompilerParams(vmem_limit_bytes=VMEM),
        cost_estimate=OTHER if got is None else OWN,
        name="feed_grads",
    )(half, second, hidden_grad, active, feed_grad, *more)


def last_grads_kernel(half_ref, first_ref, mixed_ref, a_ref, b_ref, c_ref, branch_ref, out_ref, mark_ref):
    kind = half_ref[0] * 2 + pl.program_id(0)
    mark_ref[...] = jnp.zeros_like(mark_ref)

    def put(whole):
        for i in range(6):
            out_ref[i] = whole[:, i * 128 : (i + 1) * 128].astype(jnp.bfloat16)

    @pl.when(kind < 3)
    def _():
        put(tn(first_ref[...], jnp.concatenate([a_ref[0], b_ref[0], c_ref[0]], axis=1)))

    @pl.when(kind == 3)
    def _():
        put(tn(mixed_ref[...], branch_ref[...]))


def last_grads(half, first_in, mixed, parts, branch_grad):
    seq = mixed.shape[0]
    part = lambda a: pl.BlockSpec(
        (1,) + a.shape[1:], lambda i, half: (jnp.minimum(half[0] * 2 + i, 2), 0, 0)
    )
    return pl.pallas_call(
        last_grads_kernel,
        grid_spec=pltpu.PrefetchScalarGridSpec(
            num_scalar_prefetch=1,
            grid=(2,),
            in_specs=[whole_block((seq, D)), whole_block((seq, D))]
            + [part(a) for a in parts]
            + [whole_block((seq, D))],
            out_specs=[pl.BlockSpec((6, D, 128), lambda i, half: (i, 0, 0)), whole_block((8, 128))],
        ),
        out_shape=[jax.ShapeDtypeStruct((12, D, 128), jnp.bfloat16), MARK],
        compiler_params=pltpu.CompilerParams(vmem_limit_bytes=VMEM),
        cost_estimate=OTHER,
        name="last_grads",
    )(half, first_in, mixed, *parts, branch_grad)


def tokens_back_kernel(
    tokens_ref, a_ref, b_ref, c_ref, middle_ref, gain_ref, weight_ref, out_ref, packed_ref, sums_ref
):
    @pl.when(pl.program_id(0) == 0)
    def _():
        sums_ref[...] = jnp.zeros_like(sums_ref)

    def add_sum(row, value):
        sums_ref[row : row + 1, :] += jnp.sum(value, axis=0, keepdims=True)

    query, keys, value = [
        jnp.concatenate([a_ref[i], b_ref[i], c_ref[i]], axis=1) for i in range(3)
    ]
    grad = nt(query, weight_ref[:, :D])
    grad = grad + nt(keys, weight_ref[:, D : 2 * D])
    grad = grad + nt(value, weight_ref[:, 2 * D :])
    normed, inverse = normalize(tokens_ref[...].astype(jnp.float32))
    add_sum(0, grad * normed)
    add_sum(1, grad)
    add_sum(2, query.astype(jnp.float32))
    add_sum(3, value.astype(jnp.float32))
    out_ref[...] = middle_ref[...] + normalize_back(grad * line(gain_ref), normed, inverse)

    @pl.when(pl.program_id(0) == pl.num_programs(0) - 1)
    def _():
        wide = packed_ref.shape[0]
        part = D // wide
        for w in range(wide):
            packed_ref[w : w + 1, :part] = sums_ref[0:1, w * part : (w + 1) * part]
            packed_ref[w : w + 1, part : 2 * part] = sums_ref[1:2, w * part : (w + 1) * part]
            bias_row = 2 + w * 2 // wide
            at = w % (wide // 2) * 2 * part
            packed_ref[w : w + 1, 2 * part :] = sums_ref[bias_row : bias_row + 1, at : at + 2 * part]


def tokens_back(tokens, parts, middle_grad, gain, weight, wide):
    seq = tokens.shape[0]
    return pl.pallas_call(
        tokens_back_kernel,
        grid=(seq // ROWS,),
        in_specs=[by_block(D)]
        + [pl.BlockSpec((3, ROWS, a.shape[2]), lambda i: (0, i, 0)) for a in parts]
        + [by_block(D)] + [whole_block(gain.shape), whole_block(weight.shape)],
        out_specs=[by_block(D), whole_block((wide, 4 * D // wide))],
        out_shape=[
            jax.ShapeDtypeStruct((seq, D), jnp.float32),
            jax.ShapeDtypeStruct((wide, 4 * D // wide), jnp.float32),
        ],
        scratch_shapes=[pltpu.VMEM((8, D), jnp.float32)],
        compiler_params=pltpu.CompilerParams(vmem_limit_bytes=VMEM),
        cost_estimate=OTHER,
        name="tokens_back",
    )(tokens, *parts, middle_grad, gain, weight)


def pack_kernel(feed_ref, hidden_ref, input_ref, final_ref, token_ref, *refs):
    out_ref = refs[-1]
    out_ref[...] = jnp.zeros_like(out_ref)
    wide, rows, cols = out_ref.shape
    part = D // wide
    block = input_ref.shape[1] // wide
    for w in range(wide):
        out_ref[w, :TOKEN_DIM, :block] = input_ref[:, w * block : (w + 1) * block]
        out_ref[w, :TOKEN_DIM, block : 2 * block] = final_ref[:, w * block : (w + 1) * block]
        out_ref[w, TOKEN_DIM : TOKEN_DIM + 1, :] = hidden_ref[:, w * cols : (w + 1) * cols]
        out_ref[w, TOKEN_DIM + 2 : TOKEN_DIM + 3, :] = token_ref[w : w + 1, :]
        for i in range(4):
            out_ref[w, TOKEN_DIM + 1 : TOKEN_DIM + 2, i * part : (i + 1) * part] = feed_ref[
                i : i + 1, w * part : (w + 1) * part
            ]


def pack(feed_sums, hidden_sum, input_grad, final_grad, token_packed, marks):
    operands = (feed_sums, hidden_sum, input_grad, final_grad, token_packed)
    wide = token_packed.shape[0]
    shape = (wide, TOKEN_DIM + 8, hidden_sum.shape[1] // wide)
    return pl.pallas_call(
        pack_kernel,
        grid=(1,),
        in_specs=[whole_block(a.shape) for a in operands] + [pl.BlockSpec(memory_space=pl.ANY)] * len(marks),
        out_specs=whole_block(shape),
        out_shape=jax.ShapeDtypeStruct(shape, jnp.float32),
        cost_estimate=OTHER,
        name="pack",
    )(*operands, *marks)


def add_up(terms):
    total = terms[0].astype(jnp.float32)
    for term in terms[1:]:
        total = total + term.astype(jnp.float32)
    return total


def swap(array, axis, mask):
    count = lax.axis_size(axis)
    return lax.ppermute(array, axis, [(i, i ^ mask) for i in range(count)])


def bit(axis, mask):
    return lax.axis_index(axis) // mask % 2


def pick(array, index, axis):
    return lax.dynamic_index_in_dim(array, index, axis, keepdims=False)


class Order:
    def __init__(self):
        self.mark = ()
        self.marks = ()

    def __call__(self, *values):
        out = lax.optimization_barrier(values + self.mark)[: len(values)]
        return out if len(values) > 1 else out[0]

    def at(self, *values):
        self.mark = values


def bits():
    return jnp.stack([bit("narrow", 1), bit("narrow", 2), bit("wide", 1)]).astype(jnp.int32)


class Flow:
    AXES = {"x": ("narrow", 2), "y": ("wide", 1)}

    def __init__(self, order, lanes, sends=None):
        self.order = order
        self.wide = lax.axis_size("wide").bit_length() - 1
        self.lanes = [[list(terms), tuple(left)] for terms, left in lanes]
        self.steps = self.run(sends)

    def step(self):
        next(self.steps)

    def take(self):
        got = self.order(*self.got)
        return got if isinstance(got, (tuple, list)) else (got,)

    def send(self, *sends):
        self.got = tuple(swap(*s) for s in sends)
        self.order.at(*[s[0] for s in sends])

    def shaped(self, array, left):
        dims = (2,) * (self.wide - ("y" not in left))
        if "x" in left:
            return array.reshape((2, array.shape[0] // 2) + dims + (-1, array.shape[2]))
        return array.reshape((array.shape[0],) + dims + (-1, array.shape[2]))

    def exchange(self, lane, goal):
        terms, left = lane
        dim = 0 if goal == "x" else self.wide + ("x" in left)
        mine = bit(*self.AXES[goal])
        sent = add_up([pick(t, 1 - mine, dim) for t in terms]).astype(jnp.bfloat16)
        lane[0] = [pick(t, mine, dim) for t in terms]
        lane[1] = tuple(n for n in left if n != goal)
        return (sent,) + self.AXES[goal]

    def run(self, sends):
        if sends is not None:
            shapes = [lane[0][0].shape for lane in self.lanes]
            self.send(*sends)
            yield
            got = self.take()
            for lane, g, shape in zip(self.lanes, got, shapes):
                lane[0].append(g.reshape(shape))
        while any(lane[1] for lane in self.lanes):
            self.send(*[self.exchange(lane, lane[1][0]) for lane in self.lanes])
            yield
            for lane, got in zip(self.lanes, self.take()):
                lane[0].append(got)
        parts = [lane[0] for lane in self.lanes]
        both = []
        for b in reversed(range(1, self.wide)):
            mask = 1 << b
            mine = bit("wide", mask)
            sent = [add_up([pick(t, 1 - mine, 1) for t in terms]) for terms in parts]
            sent = [jnp.concatenate(sent, axis=0)] + [pick(t, 1 - mine, 1) for t in both]
            parts = [[pick(t, mine, 1) for t in terms] for terms in parts]
            both = [pick(t, mine, 1) for t in both]
            self.send((add_up(sent).astype(jnp.bfloat16), "wide", mask))
            yield
            both.append(self.take()[0])
        own = jnp.concatenate([add_up(terms) for terms in parts], axis=0)
        share = add_up([own] + both).astype(jnp.bfloat16)
        self.send((share, "narrow", 2))
        yield
        (other,) = self.take()
        self.send((share, "narrow", 1), (other, "narrow", 1))
        yield
        self.result = (share, other) + tuple(self.take())
        yield

    def finish(self):
        for unused in self.steps:
            pass
        return self.result


class Halves:
    def __init__(self, order, sent):
        *sent, mark = sent
        self.order = order
        self.flight = tuple(swap(a, "narrow", 1) for a in sent)
        order.at(mark)
        order.marks += (mark,)

    def got(self):
        got = self.order(*self.flight)
        return tuple(got) if isinstance(got, (tuple, list)) else (got,)


def unpack_kernel(put, bits_ref, *refs):
    shares, outs = refs[:4], refs[4:]
    core, x = bits_ref[0], bits_ref[1]
    for c in range(2):
        for k in range(2):
            same_x, same_core = x == k, core == c
            for t in range(shares[0].shape[0]):
                one, two, three, four = [s[t].astype(jnp.float32) for s in shares]
                near = jnp.where(same_x, one, two)
                far = jnp.where(same_x, three, four)
                put(outs, c, k, t, jnp.where(same_core, near, far))


def unpack(put, shares, shapes):
    return pl.pallas_call(
        partial(unpack_kernel, put),
        grid=(1,),
        in_specs=[smem()] + [whole_block(a.shape) for a in shares],
        out_specs=[whole_block(s) for s in shapes],
        out_shape=[jax.ShapeDtypeStruct(s, jnp.float32) for s in shapes],
        compiler_params=pltpu.CompilerParams(vmem_limit_bytes=VMEM),
        cost_estimate=OTHER,
        name="unpack",
    )(bits(), *shares)


def put_columns(spans, tiles):
    def put(outs, c, x, t, value):
        column = (c * 2 + x) * tiles + t
        for out_ref, (first, stop) in zip(outs, spans):
            if first <= column < stop:
                at = (column - first) * value.shape[1]
                out_ref[:, at : at + value.shape[1]] = value

    return put


def small_steps(order, rows):
    def send(*sends):
        order.at(*[s[0] for s in sends])
        return [swap(*s) for s in sends]

    wide = lax.axis_size("wide")
    low = rows.astype(jnp.bfloat16)
    for mask in (1, 2):
        (got,) = send((low, "narrow", mask))
        yield
        low = add_up([low, order(got)]).astype(jnp.bfloat16)
    low = low.reshape((wide // 2, 2) + low.shape[1:])
    mine = bit("wide", 1)
    (got,) = send((pick(low, 1 - mine, 1), "wide", 1))
    yield
    low = add_up([pick(low, mine, 1), order(got)]).astype(jnp.bfloat16)
    place = lax.axis_index("wide") // 2
    got = send(*[(pick(low, place ^ (m // 2), 0), "wide", m) for m in range(2, wide, 2)])
    yield
    yield add_up([pick(low, place, 0)] + list(order(*got)))


def shards(
    tokens,
    cotangent,
    latents,
    added_noise,
    timesteps,
    bucket,
    masked,
    deal_start,
    first_gain,
    first_shift,
    joint_weight,
    query_value_bias,
    output_weight,
    output_bias,
    second_gain,
    second_shift,
    expand_weight,
    expand_bias,
    reduce_weight,
    reduce_bias,
    input_proj,
    cond_proj,
    time_first,
    time_second,
    block_mod,
    block_expand,
    block_reduce,
    final_mod,
    final_proj,
):
    wide = lax.axis_size("wide")
    narrow = lax.axis_size("narrow")
    place_wide = lax.axis_index("wide")
    place_narrow = lax.axis_index("narrow")
    mine = bits()
    other = mine.at[0].set(1 - mine[0])
    image_index = place_wide * narrow + place_narrow
    at = jnp.stack([image_index, place_wide, place_narrow, jnp.int32(narrow)]).astype(jnp.int32)

    spot, live = places(at, bucket, deal_start, masked, wide)
    slots = spot.shape[1]
    steps = timesteps.astype(jnp.float32)
    half = time_first.shape[0] // 2
    freqs = jnp.exp(-math.log(10000.0) * jnp.arange(half).astype(jnp.float32) / half)
    angles = steps.reshape(-1, 1) * freqs
    sinus = jnp.concatenate([jnp.cos(angles), jnp.sin(angles)], axis=-1).astype(jnp.bfloat16)
    offset = steps * STEP_ANGLE
    keep_sig = jnp.cos(offset + SHIFT_ANGLE) / math.cos(SHIFT_ANGLE)
    drop_sig = jnp.sqrt(jnp.sin(offset) * jnp.sin(offset + 2.0 * SHIFT_ANGLE)) / math.cos(SHIFT_ANGLE)
    input_turned = input_proj.T
    final_turned = final_proj.T

    first_in, joint = joint_pass(
        tokens, first_gain, first_shift, joint_weight, query_value_bias
    )
    mixed, logsum = attend(at, bucket, joint)
    block_output, middle, second_in, active, slope, dealt, spread = feed_pass(
        at,
        bucket,
        mixed,
        tokens,
        latents,
        spot,
        (
            output_weight,
            output_bias,
            second_gain,
            second_shift,
            expand_weight,
            expand_bias,
            reduce_weight,
            reduce_bias,
        ),
    )

    def deal(array):
        shape = array.shape
        return lax.all_to_all(
            array.reshape(wide, -1, shape[1]), "wide", split_axis=0, concat_axis=0, tiled=True
        ).reshape(shape)

    dealt = deal(dealt)
    low_turned, time_slope, timed = time_embedding(sinus, time_first, time_second)
    (
        guess,
        left,
        fin_grad,
        branch_grad,
        upper_grad,
        mod_grad,
        timed_grad,
        embed_grad,
        rows_grad,
        input_grad,
        final_grad,
    ) = head_pass(
        dealt,
        timed,
        keep_sig[:, None, :],
        drop_sig[:, None, :],
        added_noise,
        live,
        (input_turned, cond_proj, block_mod, block_expand, block_reduce, final_mod, final_turned),
    )
    order = Order()
    order.at(rows_grad)
    returned = deal(rows_grad)
    first_grad = time_back(order(timed_grad), time_second, time_slope)
    order.at(first_grad)
    one_args = (fin_grad, branch_grad, upper_grad)
    halves_one = Halves(order, head_grads_one(other, order(left), *one_args))
    two_args = (mod_grad, timed_grad, dealt, embed_grad, sinus, first_grad, wide)
    halves_two = Halves(order, head_grads_two(other, left, order(low_turned), *two_args))
    returned = order(returned)
    order.at(returned, *order.mark)

    def note(mark):
        order.marks += (mark,)
        order.at(mark)

    sent, kept, mark = head_grads_one(mine, order(left), *one_args, *halves_one.got())
    note(mark)
    shape = lambda a: a.reshape((a.shape[0],) + (2,) * (wide.bit_length() - 1) + (-1, a.shape[2]))
    half_shape = lambda a: a.reshape(
        (2, a.shape[0] // 2) + (2,) * (wide.bit_length() - 2) + (-1, a.shape[2])
    )
    one = Flow(order, [([shape(kept)], ("y",))], [(sent, "narrow", 2)])
    one.step()
    order.at(mark)
    sent_a, kept_a, sent_b, kept_b, mark = head_grads_two(
        mine, left, order(low_turned), *two_args, *halves_two.got()
    )
    note(mark)
    two = Flow(
        order,
        [([shape(kept_a)], ("y",)), ([half_shape(kept_b)], ("x",))],
        [(sent_a, "narrow", 2), (sent_b, "wide", 1)],
    )
    two.step()
    order.at(mark)
    feed_grad, hidden_grad, middle_grad, out_grad, mixed_grad, feed_sums, hidden_sum = feed_back(
        at,
        bucket,
        order(cotangent),
        spot,
        middle,
        slope,
        returned,
        (output_weight, second_gain, expand_weight, reduce_weight),
    )
    order.at(mixed_grad)
    feed_args = (hidden_grad, active, feed_grad, wide)
    halves_feed = Halves(order, feed_grads(other, order(second_in), *feed_args))
    one.step()
    parts = []

    def attend_back_part(i):
        grads = attend_back(2 * i, 2, at, bucket, joint, order(mixed_grad), mixed, logsum)
        order.at(grads)
        parts.append(grads)

    attend_back_part(0)
    two.step()
    sent_e, kept_e, sent_r, kept_r, mark = feed_grads(
        mine, order(second_in), *feed_args, halves_feed.got()
    )
    note(mark)
    feed = Flow(
        order,
        [([shape(kept_e)], ("y",)), ([half_shape(kept_r)], ("x",))],
        [(sent_e, "narrow", 2), (sent_r, "wide", 1)],
    )
    feed.step()
    order.at(mark)
    one.step()
    attend_back_part(1)
    feed.step()
    two.step()
    one.step()
    attend_back_part(2)
    feed.step()
    two.step()
    one.step()
    last_args = (mixed, parts, out_grad)
    halves_last = Halves(order, last_grads(other, order(first_in), *last_args))
    one.step()
    own, mark = last_grads(mine, order(first_in), *last_args)
    note(mark)
    terms = [
        a.reshape((2, 6) + (2,) * (wide.bit_length() - 1) + (-1, 128)) for a in (own,) + halves_last.got()
    ]
    last = Flow(
        order, [([a[:, :3] for a in terms], ("x", "y")), ([a[:, 3:] for a in terms], ("y", "x"))]
    )
    last.step()
    two.step()
    tokens_gradient, token_packed = tokens_back(
        order(tokens), parts, middle_grad, first_gain, joint_weight, wide
    )
    order.at(token_packed)
    width = cond_proj.shape[1]
    rows = width // wide
    cut = cond_proj.shape[0] // wide

    def hold(outs):
        order.at(*outs)
        return outs

    last.step()
    feed.step()
    two.step()
    packed = pack(feed_sums, hidden_sum, input_grad, final_grad, order(token_packed), order.marks)
    order.at(packed)
    small = small_steps(order, packed)
    next(small)
    one = one.finish()
    final_mod_out, block_reduce_out, block_expand_out = hold(
        unpack(
            put_columns(((0, 4), (4, 6), (6, 8)), 2),
            (order(one[0]),) + one[1:],
            ((rows, 2 * width), (rows, width), (rows, width)),
        )
    )
    last.step()
    next(small)
    feed.step()
    two = two.finish()

    def put_two(outs, c, x, t, value):
        column = (c * 2 + x) * 5 + t
        if column < 16:
            put_columns(((0, 12), (12, 16)), 5)(outs, c, x, t, value)
        else:
            cols = slice((column - 16) * 256, (column - 15) * 256)
            outs[2][:, cols] = value[:cut]
            outs[3][:, cols] = value[cut:]

    block_mod_out, time_second_out, cond_out, time_first_out = hold(
        unpack(
            put_two,
            (order(two[0]),) + two[1:],
            ((rows, 3 * width), (rows, width), (cut, width), (rows - cut, width)),
        )
    )
    last.step()
    next(small)
    feed.step()
    feed = feed.finish()

    def put_feed(outs, c, x, t, value):
        if t == 0:
            at = (c * 2 + x) * D
            outs[0][:, at : at + D] = value
        else:
            for i in range(2):
                piece = x * 2 + i
                outs[1][piece * cut : (piece + 1) * cut, c * (D // 2) : (c + 1) * (D // 2)] = value[
                    :, i * (D // 2) : (i + 1) * (D // 2)
                ]

    last.step()
    next(small)
    expand_out, reduce_out = hold(
        unpack(put_feed, (order(feed[0]),) + feed[1:], ((cut, 4 * D), (4 * cut, D)))
    )
    last.step()
    small = next(small)
    last = last.finish()
    joint_out, output_out = unpack(
        put_columns(((0, 18), (18, 24)), 6), last, ((cut, 3 * D), (cut, D))
    )
    part = D // wide
    block = input_grad.shape[1] // wide
    vectors = [small[TOKEN_DIM + 1, i * part : (i + 1) * part] for i in range(4)]
    input_out = small[:TOKEN_DIM, :block].T
    final_out = small[:TOKEN_DIM, block : 2 * block].T
    late = small[TOKEN_DIM + 2]
    outs = [
        late[:part],
        late[part : 2 * part],
        late[2 * part :],
        vectors[3],
        vectors[1],
        vectors[2],
        small[TOKEN_DIM],
        vectors[0],
        input_out,
        final_out,
    ]
    return (
        block_output,
        guess,
        spread[:2, 0].reshape(1, 2),
        tokens_gradient,
        outs[0],
        outs[1],
        joint_out,
        outs[2],
        output_out,
        outs[3],
        outs[4],
        outs[5],
        expand_out,
        outs[6],
        reduce_out,
        outs[7],
        outs[8],
        cond_out,
        time_first_out,
        time_second_out,
        block_mod_out,
        block_expand_out,
        block_reduce_out,
        final_mod_out,
        outs[9],
    )


def solution(mesh):
    in_specs = (
        P(("wide", "narrow"), None),
        P(("wide", "narrow"), None),
        P(("wide", "narrow"), None),
        P(None, None, ("wide", "narrow")),
        P(None, ("wide", "narrow")),
        P(),
        P(("wide", "narrow"), None),
        P(),
        P(),
        P(),
        P(),
        P(),
        P(),
        P(),
        P(),
        P(),
        P(),
        P(),
        P(),
        P(),
        P(),
        P(),
        P(),
        P(),
        P(),
        P(),
        P(),
        P(),
        P(),
    )
    out_specs = (
        P(("wide", "narrow"), None),
        P(None, None, ("wide", "narrow")),
        P(("wide", "narrow"), None),
        P(("wide", "narrow"), None),
        P("wide"),
        P("wide"),
        P("wide", None),
        P("wide"),
        P("wide", None),
        P("wide"),
        P("wide"),
        P("wide"),
        P("wide", None),
        P("wide"),
        P("wide", None),
        P("wide"),
        P("wide", None),
        P("wide", None),
        P("wide", None),
        P("wide", None),
        P("wide", None),
        P("wide", None),
        P("wide", None),
        P("wide", None),
        P("wide", None),
    )
    return jax.shard_map(shards, mesh=mesh, in_specs=in_specs, out_specs=out_specs, check_vma=False)
```

```python
from functools import partial
import math

import jax
import jax.numpy as jnp
from jax import lax
from jax.experimental import pallas as pl
from jax.experimental.pallas import tpu as pltpu
from jax.sharding import PartitionSpec as P

D = 768
HEADS = 12
HEAD_DIM = 64
TOKEN_DIM = 16
BUFFER = 64
IMAGE_MAX = 1024
MASK_MAX = 256
REPEATS = 4
SEQ = 1088


SHIFT_ANGLE = 0.008 / 1.008 * math.pi / 2.0
STEP_ANGLE = math.pi / (2.0 * 1.008 * 1000.0)
PAIRS = 6
VMEM = 60 * 1024 * 1024

OWN = pl.CostEstimate(flops=1 << 40, bytes_accessed=1 << 20, transcendentals=0)
OTHER = pl.CostEstimate(flops=0, bytes_accessed=1 << 20, transcendentals=0)


def nt(a,b): return lax.dot_general(a,b,(((1,),(1,)),((),())),preferred_element_type=jnp.float32)
def nn(a,b): return jnp.dot(a,b,preferred_element_type=jnp.float32)
def tn(a,b): return lax.dot_general(a,b,(((0,),(0,)),((),())),preferred_element_type=jnp.float32)
def normalize(values):
    centre = values - jnp.mean(values, axis=-1, keepdims=True)
    inverse = lax.rsqrt(jnp.mean(centre * centre, axis=-1, keepdims=True) + 1e-06)
    return (centre * inverse, inverse)


def normalize_back(grad_normed, normed, inverse):
    return inverse * (
        grad_normed
        - jnp.mean(grad_normed, axis=-1, keepdims=True)
        - normed * jnp.mean(grad_normed * normed, axis=-1, keepdims=True)
    )


def sigmoid(value):
    return 0.5 * jnp.tanh(0.5 * value) + 0.5


def silu_slope(value, sigma):
    return sigma * (1.0 + value * (1.0 - sigma))


def whole_block(shape):
    zeros = (0,) * len(shape)
    return pl.BlockSpec(shape, lambda *unused: zeros, pipeline_mode=pl.Buffered(1))


def time_kernel(sinus_ref, first_ref, second_ref, low_ref, slope_ref, timed_ref):
    first = nn(sinus_ref[...], first_ref[...])
    sigma = sigmoid(first)
    low = (first * sigma).astype(jnp.bfloat16)
    slope_ref[...] = silu_slope(first, sigma).astype(jnp.bfloat16)
    low_ref[...] = low.T
    timed_ref[...] = nn(low, second_ref[...])


def time_embedding(sinus, time_first, time_second):
    count, freq = sinus.shape
    width = time_first.shape[1]
    rows = count // REPEATS
    by_rows = pl.BlockSpec((rows, width), lambda i: (i, 0))
    return pl.pallas_call(
        time_kernel,
        grid=(REPEATS,),
        in_specs=[
            pl.BlockSpec((rows, freq), lambda i: (i, 0)),
            whole_block(time_first.shape),
            whole_block(time_second.shape),
        ],
        out_specs=[pl.BlockSpec((width, rows), lambda i: (0, i)), by_rows, by_rows],
        out_shape=[
            jax.ShapeDtypeStruct((width, count), jnp.bfloat16),
            jax.ShapeDtypeStruct((count, width), jnp.bfloat16),
            jax.ShapeDtypeStruct((count, width), jnp.float32),
        ],
        compiler_params=pltpu.CompilerParams(vmem_limit_bytes=VMEM),
        cost_estimate=OTHER,
        name="time_embedding",
    )(sinus, time_first, time_second)


def head_kernel(
    dealt_ref,
    timed_ref,
    keep_ref,
    drop_ref,
    noise_ref,
    live_ref,
    input_ref,
    cond_ref,
    mod_ref,
    expand_ref,
    reduce_ref,
    fin_ref,
    final_ref,
    guess_ref,
    left_ref,
    fin_grad_ref,
    branch_grad_ref,
    upper_grad_ref,
    mod_grad_ref,
    timed_grad_ref,
    embed_grad_ref,
    rows_grad_ref,
    input_grad_ref,
    final_grad_ref,
    embed_scratch,
    total_scratch,
):
    turn = pl.program_id(0)
    width = timed_ref.shape[1]

    @pl.when(turn == 0)
    def _():
        embed_scratch[...] = nn(dealt_ref[:, :D], cond_ref[...])
        total_scratch[...] = jnp.zeros_like(total_scratch)
        input_grad_ref[...] = jnp.zeros_like(input_grad_ref)
        final_grad_ref[...] = jnp.zeros_like(final_grad_ref)

    cond = embed_scratch[...] + timed_ref[...]
    acted = (cond * sigmoid(cond)).astype(jnp.bfloat16)
    left_ref[0] = acted.T
    start = dealt_ref[:, D:].astype(jnp.float32).T[:TOKEN_DIM]
    noise = noise_ref[0]
    noisy = (keep_ref[0] * start + drop_ref[0] * noise).astype(jnp.bfloat16)
    entry = tn(noisy, input_ref[...])
    inner_normed, inner_inverse = normalize(entry)
    shift_a = nn(acted, mod_ref[:, :width])
    scale_a = nn(acted, mod_ref[:, width : 2 * width])
    gate_a = nn(acted, mod_ref[:, 2 * width :])
    inner = (inner_normed * (1.0 + scale_a) + shift_a).astype(jnp.bfloat16)
    left_ref[2] = inner.T
    upper = nn(inner, expand_ref[...])
    upper_sigma = sigmoid(upper)
    lifted = (upper * upper_sigma).astype(jnp.bfloat16)
    left_ref[1] = lifted.T
    branch = nn(lifted, reduce_ref[...])
    shift_b = nn(acted, fin_ref[:, :width])
    scale_b = nn(acted, fin_ref[:, width:])
    last_normed, last_inverse = normalize(entry + gate_a * branch)
    last = (last_normed * (1.0 + scale_b) + shift_b).astype(jnp.bfloat16)
    live = live_ref[...]
    guess = nt(final_ref[...], last) * live
    guess_ref[0] = guess
    guess_grad = (2.0 / REPEATS * (guess - noise * live) * live).astype(jnp.bfloat16)
    final_grad_ref[...] += nn(guess_grad, last)
    last_grad = tn(guess_grad, final_ref[...])
    fin_grad = jnp.concatenate([last_grad, last_grad * last_normed], axis=1).astype(jnp.bfloat16)
    fin_grad_ref[...] = fin_grad
    after_grad = normalize_back(last_grad * (1.0 + scale_b), last_normed, last_inverse)
    branch_grad = (after_grad * gate_a).astype(jnp.bfloat16)
    branch_grad_ref[...] = branch_grad
    lifted_grad = nt(branch_grad, reduce_ref[...])
    upper_grad = (lifted_grad * silu_slope(upper, upper_sigma)).astype(jnp.bfloat16)
    upper_grad_ref[...] = upper_grad
    inner_grad = nt(upper_grad, expand_ref[...])
    entry_grad = (
        after_grad + normalize_back(inner_grad * (1.0 + scale_a), inner_normed, inner_inverse)
    ).astype(jnp.bfloat16)
    input_grad_ref[...] += nn(noisy, entry_grad)
    mod_grad = jnp.concatenate(
        [inner_grad, inner_grad * inner_normed, after_grad * branch], axis=1
    ).astype(jnp.bfloat16)
    mod_grad_ref[...] = mod_grad
    acted_grad = nt(mod_grad, mod_ref[...]) + nt(fin_grad, fin_ref[...])
    cond = embed_scratch[...] + timed_ref[...]
    cond_grad = acted_grad * silu_slope(cond, sigmoid(cond))
    timed_grad_ref[...] = cond_grad.astype(jnp.bfloat16)
    total_scratch[...] += cond_grad

    @pl.when(turn == REPEATS - 1)
    def _():
        embed_grad = total_scratch[...].astype(jnp.bfloat16)
        embed_grad_ref[...] = embed_grad
        rows_grad_ref[...] = nt(embed_grad, cond_ref[...]).astype(jnp.bfloat16)


def head_pass(dealt, timed, keep_sig, drop_sig, noise, live, weights):
    input_proj, cond_proj, block_mod, block_expand, block_reduce, final_mod, final_proj = weights
    slots = dealt.shape[0]
    width = cond_proj.shape[1]
    count = REPEATS * slots
    by_rows = lambda n: pl.BlockSpec((slots, n), lambda i: (i, 0))
    by_turn = lambda a: pl.BlockSpec((1,) + a, lambda i: (i, 0, 0))
    low = lambda *s: jax.ShapeDtypeStruct(s, jnp.bfloat16)
    full = lambda *s: jax.ShapeDtypeStruct(s, jnp.float32)
    operands = (
        dealt,
        timed,
        keep_sig,
        drop_sig,
        noise,
        live,
        input_proj,
        cond_proj,
        block_mod,
        block_expand,
        block_reduce,
        final_mod,
        final_proj,
    )
    return pl.pallas_call(
        head_kernel,
        grid=(REPEATS,),
        in_specs=[
            whole_block(dealt.shape),
            by_rows(width),
            by_turn((1, slots)),
            by_turn((1, slots)),
            by_turn((TOKEN_DIM, slots)),
        ]
        + [whole_block(a.shape) for a in operands[5:]],
        out_specs=[
            by_turn((TOKEN_DIM, slots)),
            pl.BlockSpec((3, width, slots), lambda i: (0, 0, i)),
            by_rows(2 * width),
            by_rows(width),
            by_rows(width),
            by_rows(3 * width),
            by_rows(width),
            whole_block((slots, width)),
            whole_block((slots, D)),
            whole_block((TOKEN_DIM, width)),
            whole_block((TOKEN_DIM, width)),
        ],
        out_shape=[
            full(REPEATS, TOKEN_DIM, slots),
            low(3, width, count),
            low(count, 2 * width),
            low(count, width),
            low(count, width),
            low(count, 3 * width),
            low(count, width),
            low(slots, width),
            low(slots, D),
            full(TOKEN_DIM, width),
            full(TOKEN_DIM, width),
        ],
        scratch_shapes=[pltpu.VMEM((slots, width), jnp.float32)] * 2,
        compiler_params=pltpu.CompilerParams(vmem_limit_bytes=VMEM),
        cost_estimate=OTHER,
        name="head_pass",
    )(*operands)


MARK = jax.ShapeDtypeStruct((8, 128), jnp.float32)


def head_grads_one_kernel(half_ref, left_ref, fin_ref, branch_ref, upper_ref, *refs):
    turn = pl.program_id(0)
    tile = head_one_tile(turn, half_ref)

    def put(grad):
        if len(refs) == 2:
            out_ref, mark_ref = refs
            out_ref[0] = grad.astype(jnp.bfloat16)
        else:
            got_ref, sent_ref, kept_ref, mark_ref = refs
            grad = (grad + got_ref[0].astype(jnp.float32)).astype(jnp.bfloat16)

            @pl.when(turn < 2)
            def _():
                sent_ref[0] = grad

            @pl.when(turn >= 2)
            def _():
                kept_ref[0] = grad

        mark_ref[...] = jnp.zeros_like(mark_ref)

    @pl.when(tile < 4)
    def _():
        put(nn(left_ref[0], fin_ref[...]))

    @pl.when((tile >= 4) & (tile < 6))
    def _():
        put(nn(left_ref[0], branch_ref[...]))

    @pl.when(tile >= 6)
    def _():
        put(nn(left_ref[0], upper_ref[...]))


def head_one_tile(turn, half):
    return half[0] * 4 + (turn ^ (2 - 2 * half[1]))


def head_grads_one(half, left, fin_grad, branch_grad, upper_grad, got=None):
    width, count = left.shape[1:]
    cols = width // 2

    def at(first, tiles):
        return lambda i, half: (0, jnp.clip(head_one_tile(i, half) - first, 0, tiles - 1))

    def which(i, half):
        tile = head_one_tile(i, half)
        return (jnp.where(tile < 4, 0, jnp.where(tile < 6, 1, 2)), 0, 0)

    tiles = lambda n: jax.ShapeDtypeStruct((n, width, cols), jnp.bfloat16)
    block = lambda where: pl.BlockSpec((1, width, cols), where)
    if got is None:
        more = ()
        outs = [(block(lambda i, half: (i ^ (2 - 2 * half[1]), 0, 0)), tiles(4))]
    else:
        more = (got,)
        outs = [
            (block(lambda i, half: (jnp.minimum(i, 1), 0, 0)), tiles(2)),
            (block(lambda i, half: (jnp.maximum(i - 2, 0), 0, 0)), tiles(2)),
        ]
    outs.append((whole_block((8, 128)), MARK))
    return pl.pallas_call(
        head_grads_one_kernel,
        grid_spec=pltpu.PrefetchScalarGridSpec(
            num_scalar_prefetch=1,
            grid=(4,),
            in_specs=[
                pl.BlockSpec((1, width, count), which),
                pl.BlockSpec((count, cols), at(0, 4)),
                pl.BlockSpec((count, cols), at(4, 2)),
                pl.BlockSpec((count, cols), at(6, 2)),
            ]
            + [block(lambda i, half: (i ^ (2 - 2 * half[1]), 0, 0))] * len(more),
            out_specs=[o[0] for o in outs],
        ),
        out_shape=[o[1] for o in outs],
        compiler_params=pltpu.CompilerParams(vmem_limit_bytes=VMEM),
        cost_estimate=OTHER if got is None else OWN,
        name="head_grads_one",
    )(half, left, fin_grad, branch_grad, upper_grad, *more)


def time_back_kernel(grad_ref, weight_ref, slope_ref, out_ref):
    grad = nt(grad_ref[...], weight_ref[...])
    out_ref[...] = (grad * slope_ref[...].astype(jnp.float32)).astype(jnp.bfloat16)


def time_back(timed_grad, weight, slope):
    count, width = timed_grad.shape
    by_rows = pl.BlockSpec((count // 4, width), lambda i: (i, 0))
    return pl.pallas_call(
        time_back_kernel,
        grid=(4,),
        in_specs=[by_rows, whole_block(weight.shape), by_rows],
        out_specs=by_rows,
        out_shape=jax.ShapeDtypeStruct((count, width), jnp.bfloat16),
        compiler_params=pltpu.CompilerParams(vmem_limit_bytes=VMEM),
        cost_estimate=OTHER,
        name="time_back",
    )(timed_grad, weight, slope)


def split_rows(grad, wide, y):
    grad = grad.reshape((wide // 2, 2, -1) + grad.shape[1:])
    own, other = jnp.where(y == 0, grad[:, 0], grad[:, 1]), jnp.where(y == 0, grad[:, 1], grad[:, 0])
    flat = lambda a: a.reshape((-1,) + a.shape[2:]).astype(jnp.bfloat16)
    return flat(other), flat(own)


def head_grads_two_kernel(
    wide, half_ref, acted_ref, low_ref, mod_ref, timed_ref, rows_ref, embed_ref, sinus_ref, first_ref, *refs
):
    turn = pl.program_id(0)
    tile = half_ref[0] * 10 + head_two_tile(turn, half_ref)

    def put(grad):
        refs[-1][...] = jnp.zeros_like(refs[-1])
        if len(refs) == 2:
            refs[0][0] = grad.astype(jnp.bfloat16)
            return
        got_ref, sent_one, kept_one, sent_two, kept_two, unused = refs
        grad = grad + got_ref[0].astype(jnp.float32)

        @pl.when(turn < 2)
        def _():
            sent_one[0] = grad.astype(jnp.bfloat16)

        @pl.when((turn >= 5) & (turn < 7))
        def _():
            kept_one[0] = grad.astype(jnp.bfloat16)

        @pl.when(turn % 5 >= 2)
        def _():
            sent_two[0], kept_two[0] = split_rows(grad, wide, half_ref[2])

    @pl.when(tile < 12)
    def _():
        put(nn(acted_ref[0], mod_ref[...]))

    @pl.when((tile >= 12) & (tile < 16))
    def _():
        put(nn(low_ref[...], timed_ref[...]))

    @pl.when(tile >= 16)
    def _():
        cond = tn(rows_ref[:, :D], embed_ref[...])
        time = tn(sinus_ref[...], first_ref[...])
        cols = cond.shape[1]
        both = jnp.concatenate(
            [cond.reshape(wide, -1, cols), time.reshape(wide, -1, cols)], axis=1
        )
        put(both.reshape(-1, cols))


def head_two_tile(turn, half):
    return (turn // 5 ^ (1 - half[1])) * 5 + turn % 5


def head_grads_two(half, left, low, mod_grad, timed_grad, dealt, embed_grad, sinus, first_grad, wide, got=None):
    width, count = left.shape[1:]
    slots = dealt.shape[0]
    cols = width // 4

    def at(first, tiles):
        return lambda i, half: (0, jnp.clip(half[0] * 10 + head_two_tile(i, half) - first, 0, tiles - 1))

    whole = pl.BlockSpec((1, width, cols), lambda i, half: (head_two_tile(i, half), 0, 0))
    like = lambda n, rows: jax.ShapeDtypeStruct((n, rows, cols), jnp.bfloat16)
    if got is None:
        more = ()
        outs = [(whole, like(10, width))]
    else:
        more = (got,)
        block = lambda rows, where: pl.BlockSpec((1, rows, cols), where)

        def second(i, half):
            return ((i // 5 ^ (1 - half[1])) * 3 + jnp.maximum(i % 5 - 2, 0), 0, 0)

        outs = [
            (block(width, lambda i, half: (jnp.minimum(i, 1), 0, 0)), like(2, width)),
            (block(width, lambda i, half: (jnp.clip(i - 5, 0, 1), 0, 0)), like(2, width)),
            (block(width // 2, second), like(6, width // 2)),
            (block(width // 2, second), like(6, width // 2)),
        ]
    outs.append((whole_block((8, 128)), MARK))
    return pl.pallas_call(
        partial(head_grads_two_kernel, wide),
        grid_spec=pltpu.PrefetchScalarGridSpec(
            num_scalar_prefetch=1,
            grid=(10,),
            in_specs=[
                whole_block((1, width, count)),
                whole_block((width, count)),
                pl.BlockSpec((count, cols), at(0, 12)),
                pl.BlockSpec((count, cols), at(12, 4)),
                whole_block(dealt.shape),
                pl.BlockSpec((slots, cols), at(16, 4)),
                whole_block(sinus.shape),
                pl.BlockSpec((count, cols), at(16, 4)),
            ]
            + [whole] * len(more),
            out_specs=[o[0] for o in outs],
        ),
        out_shape=[o[1] for o in outs],
        compiler_params=pltpu.CompilerParams(vmem_limit_bytes=VMEM),
        cost_estimate=OTHER if got is None else OWN,
        name="head_grads_two",
    )(half, left, low, mod_grad, timed_grad, dealt, embed_grad, sinus, first_grad, *more)


def attend_kernel(QB, at_ref, bucket_ref, q_ref, k_ref, v_ref, o_ref, lse_ref):
    length=BUFFER + bucket_ref[at_ref[0]]
    low=lax.broadcasted_iota(jnp.int32,(1,128),1)<64
    bias=jnp.where(lax.broadcasted_iota(jnp.int32,(1,SEQ),1)<length,0.0,-1e30).astype(jnp.float32)
    k=k_ref[...]; v=v_ref[...]
    one=jnp.ones((),v.dtype); zero=jnp.zeros((),v.dtype)
    vs=(jnp.where(low,v,one),jnp.where(low,one,v))
    for b in range(SEQ//QB):
        rows=pl.ds(b*QB,QB)
        q=q_ref[rows,:]
        outs=[];lses=[]
        for h in range(2):
            qh=jnp.where(low,q,zero) if h==0 else jnp.where(low,zero,q)
            s=nt(qh,k)+bias
            top=jnp.max(s,axis=1,keepdims=True)
            p=jnp.exp(s-top).astype(jnp.bfloat16)
            o=nn(p,vs[h])
            total=pltpu.roll(o,64,1)
            outs.append(o/total)
            lses.append(top+jnp.log(total))
        o_ref[rows,:]=jnp.where(low,outs[0],outs[1]).astype(jnp.bfloat16)
        lse_ref[rows,:]=jnp.where(low,lses[0],lses[1])

def attend(at,bucket,joint,QB=272):
    spec=lambda off: pl.BlockSpec((SEQ,128),lambda i,off=off:(0,i+off))
    return pl.pallas_call(partial(attend_kernel,QB),
        grid=(PAIRS,),
        in_specs=[smem(),smem(),spec(0),spec(6),spec(12)],
        out_specs=[spec(0),spec(0)],
        out_shape=[jax.ShapeDtypeStruct((SEQ,D),jnp.bfloat16),jax.ShapeDtypeStruct((SEQ,D),jnp.float32)],
        compiler_params=pltpu.CompilerParams(vmem_limit_bytes=VMEM),
        cost_estimate=OTHER,
        name='attend')(at,bucket,joint,joint,joint)

def attend_back_kernel(KB, at_ref, bucket_ref,q_ref,k_ref,v_ref,do_ref,o_ref,lse_ref,grads_ref,ds_ref):
    length=BUFFER + bucket_ref[at_ref[0]]
    low=lax.broadcasted_iota(jnp.int32,(1,128),1)<64
    q=q_ref[...]; do=do_ref[...]
    zero=jnp.zeros((),q.dtype)
    prod=do.astype(jnp.float32)*o_ref[...].astype(jnp.float32)
    prodT=prod.T
    lseT=lse_ref[...].T
    deltas=(jnp.sum(prodT[:64],axis=0,keepdims=True),jnp.sum(prodT[64:],axis=0,keepdims=True))
    lses=(lseT[0:1],lseT[64:65])
    for b in range(SEQ//KB):
        rows=pl.ds(b*KB,KB)
        k=k_ref[rows,:]; v=v_ref[rows,:]
        bias=jnp.where(lax.broadcasted_iota(jnp.int32,(KB,1),0)+b*KB<length,0.0,-1e30).astype(jnp.float32)
        dks=[];dvs=[]
        for h in range(2):
            pick=(lambda a: jnp.where(low,a,zero)) if h==0 else (lambda a: jnp.where(low,zero,a))
            s=nt(pick(k),q)+bias
            p=jnp.exp(s-lses[h])
            dp=nt(pick(v),do)
            ds=(p*(dp-deltas[h])).astype(jnp.bfloat16)
            dvs.append(nn(p.astype(jnp.bfloat16),do))
            dks.append(nn(ds,q))
            ds_ref[h,rows,:]=ds
        grads_ref[1,rows,:]=jnp.where(low,dks[0],dks[1]).astype(jnp.bfloat16)
        grads_ref[2,rows,:]=jnp.where(low,dvs[0],dvs[1]).astype(jnp.bfloat16)
    kT=k_ref[...].astype(jnp.float32).T.astype(jnp.bfloat16)
    dqT=jnp.concatenate([nn(kT[64*h:64*h+64],ds_ref[h]) for h in range(2)],axis=0)
    grads_ref[0]=(dqT.T*0.125).astype(jnp.bfloat16)

def attend_back(first,count,at,bucket,joint,do,o,lse,KB=544):
    spec=lambda off: pl.BlockSpec((SEQ,128),lambda i,off=off:(0,i+off))
    return pl.pallas_call(partial(attend_back_kernel,KB),
        grid=(count,),
        in_specs=[smem(),smem(),spec(first),spec(6+first),spec(12+first),spec(first),spec(first),spec(first)],
        out_specs=pl.BlockSpec((3,SEQ,128),lambda i:(0,0,i)),
        out_shape=jax.ShapeDtypeStruct((3,SEQ,count*128),jnp.bfloat16),
        scratch_shapes=[pltpu.VMEM((2,SEQ,SEQ),jnp.bfloat16)],
        compiler_params=pltpu.CompilerParams(vmem_limit_bytes=VMEM),
        cost_estimate=OWN,
        name="attend_back")(at,bucket,joint,joint,joint,do,o,lse)


def line(ref):
    return ref[...].reshape(1, ref.shape[0])


def smem():
    return pl.BlockSpec(memory_space=pltpu.SMEM)


def place_kernel(wide, at_ref, bucket_ref, start_ref, chosen_ref, spot_ref, live_ref):
    image, place_wide, place_narrow, narrow = at_ref[0], at_ref[1], at_ref[2], at_ref[3]
    seq = chosen_ref.shape[1]
    slots = live_ref.shape[1]
    shift = wide.bit_length() - 1
    deep = slots // wide
    deep_shift = deep.bit_length() - 1
    row = lax.broadcasted_iota(jnp.int32, (seq, seq), 0)
    column = lax.broadcasted_iota(jnp.int32, (seq, seq), 1)
    lower = (column <= row).astype(jnp.float32).astype(jnp.bfloat16)
    chosen = jnp.broadcast_to(chosen_ref[...], (8, seq)).astype(jnp.float32).astype(jnp.bfloat16)
    counted = nt(lower, chosen)
    first_row = lax.broadcasted_iota(jnp.int32, counted.shape, 0) == 0
    before = jnp.where(first_row, 0.0, pltpu.roll(counted, 1, 0))
    is_chosen = (counted - before)[:, :1] > 0.5
    order = counted[:, :1].astype(jnp.int32) - 1
    target = ((start_ref[image] + order) & (wide - 1)) * deep + (order >> shift)
    target = jnp.where(is_chosen, target, -1)
    slot = lax.broadcasted_iota(jnp.int32, (seq, slots), 1)
    spot_ref[...] = (slot == target).astype(jnp.float32).astype(jnp.bfloat16)
    lane = lax.broadcasted_iota(jnp.int32, (1, slots), 1)
    live = jnp.zeros((1, slots), jnp.float32)
    for source in range(wide):
        other = source * narrow + place_narrow
        count = bucket_ref[other] * MASK_MAX // IMAGE_MAX
        rank = (place_wide - start_ref[other]) & (wide - 1)
        arrived = jnp.maximum((count - rank + wide - 1) >> shift, 0)
        inside = ((lane >> deep_shift) == source) & ((lane & (deep - 1)) < arrived)
        live = jnp.where(inside, 1.0, live)
    live_ref[...] = live


def places(at, bucket, deal_start, masked, wide):
    seq = masked.shape[1]
    return pl.pallas_call(
        partial(place_kernel, wide),
        in_specs=[smem(), smem(), smem(), whole_block((1, seq))],
        out_specs=[whole_block((seq, MASK_MAX)), whole_block((1, MASK_MAX))],
        grid=(1,),
        out_shape=[
            jax.ShapeDtypeStruct((seq, MASK_MAX), jnp.bfloat16),
            jax.ShapeDtypeStruct((1, MASK_MAX), jnp.float32),
        ],
        compiler_params=pltpu.CompilerParams(vmem_limit_bytes=VMEM),
        cost_estimate=OTHER,
        name="places",
    )(at, bucket, deal_start, masked)


def joint_kernel(tokens_ref, gain_ref, shift_ref, weight_ref, bias_ref, first_ref, joint_ref):
    normed, unused = normalize(tokens_ref[...].astype(jnp.float32))
    first = (normed * line(gain_ref) + line(shift_ref)).astype(jnp.bfloat16)
    first_ref[...] = first
    for part in range(3):
        cols = slice(part * D, (part + 1) * D)
        out = nn(first, weight_ref[:, cols])
        if part != 1:
            out = out + line(bias_ref)[:, part // 2 * D : part // 2 * D + D]
        out = out.astype(jnp.bfloat16)
        if part == 0:
            out = out * jnp.bfloat16(HEAD_DIM ** (-0.5))
        joint_ref[:, cols] = out


ROWS = 272


def by_block(columns):
    return pl.BlockSpec((ROWS, columns), lambda i: (i, 0))


def joint_pass(tokens, gain, shift, weight, bias):
    seq = tokens.shape[0]
    return pl.pallas_call(
        joint_kernel,
        grid=(seq // ROWS,),
        in_specs=[by_block(D)] + [whole_block(a.shape) for a in (gain, shift, weight, bias)],
        out_specs=[by_block(D), by_block(3 * D)],
        out_shape=[
            jax.ShapeDtypeStruct((seq, D), jnp.bfloat16),
            jax.ShapeDtypeStruct((seq, 3 * D), jnp.bfloat16),
        ],
        compiler_params=pltpu.CompilerParams(vmem_limit_bytes=VMEM),
        cost_estimate=OTHER,
        name="joint_pass",
    )(tokens, gain, shift, weight, bias)


def gelu_parts(value):
    size = jnp.abs(value)
    bell = jnp.exp(-0.5 * value * value)
    step = 1.0 / (1.0 + (0.3275911 * math.sqrt(0.5)) * size)
    tail = 0.5 * 1.061405429 * step - 0.5 * 1.453152027
    tail = tail * step + 0.5 * 1.421413741
    tail = tail * step - 0.5 * 0.284496736
    tail = tail * step + 0.5 * 0.254829592
    tail = tail * step * bell
    return jnp.where(value < 0.0, tail, 1.0 - tail), bell * (1.0 / math.sqrt(2.0 * math.pi))


def keep_column(at_ref, bucket_ref, rows):
    position = lax.broadcasted_iota(jnp.int32, (rows, 1), 0) + pl.program_id(0) * rows
    return (position < BUFFER + bucket_ref[at_ref[0]]).astype(jnp.float32)


def feed_kernel(
    at_ref,
    bucket_ref,
    mixed_ref,
    tokens_ref,
    latent_ref,
    spot_ref,
    out_w_ref,
    out_b_ref,
    gain_ref,
    shift_ref,
    expand_ref,
    expand_b_ref,
    reduce_ref,
    reduce_b_ref,
    output_ref,
    middle_ref,
    second_ref,
    active_ref,
    slope_ref,
    dealt_ref,
    spread_ref,
    dealt_scratch,
    spread_scratch,
):
    step = pl.program_id(0)

    @pl.when(step == 0)
    def _():
        dealt_scratch[...] = jnp.zeros_like(dealt_scratch)
        spread_scratch[...] = jnp.zeros_like(spread_scratch)

    keep = keep_column(at_ref, bucket_ref, mixed_ref.shape[0])
    branch = nn(mixed_ref[...], out_w_ref[...]) + line(out_b_ref)
    middle = tokens_ref[...].astype(jnp.float32) + branch
    middle_ref[...] = middle
    normed, unused = normalize(middle)
    second = (normed * line(gain_ref) + line(shift_ref)).astype(jnp.bfloat16)
    second_ref[...] = second
    hidden_width = expand_ref.shape[1]
    expand_b = line(expand_b_ref)
    feed = line(reduce_b_ref)
    for part in range(hidden_width // D):
        cols = slice(part * D, (part + 1) * D)
        hidden = nn(second, expand_ref[:, cols]) + expand_b[:, cols]
        phi, density = gelu_parts(hidden)
        active = (hidden * phi).astype(jnp.bfloat16)
        active_ref[:, cols] = active
        slope_ref[:, cols] = (phi + hidden * density).astype(jnp.bfloat16)
        feed = feed + nn(active, reduce_ref[cols, :])
    output = ((middle + feed) * keep).astype(jnp.bfloat16)
    output_ref[...] = output
    spread_scratch[0:1, :] += jnp.sum(keep * branch * branch, axis=0, keepdims=True)
    spread_scratch[1:2, :] += jnp.sum(keep * feed * feed, axis=0, keepdims=True)
    spot = spot_ref[...]
    dealt_scratch[:, :D] += tn(spot, output)
    dealt_scratch[:, D : D + TOKEN_DIM] += tn(spot, latent_ref[...])

    @pl.when(step == pl.num_programs(0) - 1)
    def _():
        dealt_ref[...] = dealt_scratch[...].astype(jnp.bfloat16)
        count = (BUFFER + bucket_ref[at_ref[0]]).astype(jnp.float32) * D
        total = jnp.sum(spread_scratch[...], axis=1, keepdims=True)
        spread_ref[...] = jnp.sqrt(jnp.broadcast_to(total, spread_ref.shape) / count)


def feed_pass(at, bucket, mixed, tokens, latents, spot, weights):
    seq = tokens.shape[0]
    slots = spot.shape[1]
    hidden = weights[4].shape[1]
    low = lambda *s: jax.ShapeDtypeStruct(s, jnp.bfloat16)
    full = lambda *s: jax.ShapeDtypeStruct(s, jnp.float32)
    return pl.pallas_call(
        feed_kernel,
        grid=(seq // ROWS,),
        in_specs=[smem(), smem(), by_block(D), by_block(D), by_block(TOKEN_DIM), by_block(slots)]
        + [whole_block(a.shape) for a in weights],
        out_specs=[
            by_block(D),
            by_block(D),
            by_block(D),
            by_block(hidden),
            by_block(hidden),
            whole_block((slots, D + 128)),
            whole_block((8, 128)),
        ],
        out_shape=[
            low(seq, D),
            full(seq, D),
            low(seq, D),
            low(seq, hidden),
            low(seq, hidden),
            low(slots, D + 128),
            full(8, 128),
        ],
        scratch_shapes=[pltpu.VMEM((slots, D + 128), jnp.float32), pltpu.VMEM((8, D), jnp.float32)],
        compiler_params=pltpu.CompilerParams(vmem_limit_bytes=VMEM),
        cost_estimate=OTHER,
        name="feed_pass",
    )(at, bucket, mixed, tokens, latents, spot, *weights)


def feed_back_kernel(
    at_ref,
    bucket_ref,
    cot_ref,
    spot_ref,
    middle_ref,
    slope_ref,
    returned_ref,
    out_w_ref,
    gain_ref,
    expand_ref,
    reduce_ref,
    feed_grad_ref,
    hidden_grad_ref,
    middle_grad_ref,
    branch_grad_ref,
    mixed_grad_ref,
    sums_ref,
    wide_sum_ref,
):
    @pl.when(pl.program_id(0) == 0)
    def _():
        sums_ref[...] = jnp.zeros_like(sums_ref)
        wide_sum_ref[...] = jnp.zeros_like(wide_sum_ref)

    def add_sum(row, value):
        sums_ref[row : row + 1, :] += jnp.sum(value, axis=0, keepdims=True)

    keep = keep_column(at_ref, bucket_ref, cot_ref.shape[0])
    grad = (cot_ref[...].astype(jnp.float32) + nn(spot_ref[...], returned_ref[...])) * keep
    feed_grad = grad.astype(jnp.bfloat16)
    feed_grad_ref[...] = feed_grad
    add_sum(0, feed_grad.astype(jnp.float32))
    second_grad = jnp.zeros(grad.shape, jnp.float32)
    for part in range(expand_ref.shape[1] // D):
        cols = slice(part * D, (part + 1) * D)
        active_grad = nt(feed_grad, reduce_ref[cols, :])
        hidden_grad = (active_grad * slope_ref[:, cols].astype(jnp.float32)).astype(jnp.bfloat16)
        hidden_grad_ref[:, cols] = hidden_grad
        wide_sum_ref[:, cols] += jnp.sum(hidden_grad.astype(jnp.float32), axis=0, keepdims=True)
        second_grad = second_grad + nt(hidden_grad, expand_ref[:, cols])
    normed, inverse = normalize(middle_ref[...])
    add_sum(1, second_grad * normed)
    add_sum(2, second_grad)
    middle_grad = grad + normalize_back(second_grad * line(gain_ref), normed, inverse)
    middle_grad_ref[...] = middle_grad
    branch_grad = middle_grad.astype(jnp.bfloat16)
    branch_grad_ref[...] = branch_grad
    add_sum(3, branch_grad.astype(jnp.float32))
    mixed_grad_ref[...] = nt(branch_grad, out_w_ref[...]).astype(jnp.bfloat16)


def feed_back(at, bucket, cotangent, spot, middle, slope, returned, weights):
    seq = cotangent.shape[0]
    slots = spot.shape[1]
    hidden = slope.shape[1]
    low = lambda *s: jax.ShapeDtypeStruct(s, jnp.bfloat16)
    full = lambda *s: jax.ShapeDtypeStruct(s, jnp.float32)
    return pl.pallas_call(
        feed_back_kernel,
        grid=(seq // ROWS,),
        in_specs=[smem(), smem(), by_block(D), by_block(slots), by_block(D), by_block(hidden)]
        + [whole_block(a.shape) for a in (returned,) + weights],
        out_specs=[
            by_block(D),
            by_block(hidden),
            by_block(D),
            by_block(D),
            by_block(D),
            whole_block((8, D)),
            whole_block((1, hidden)),
        ],
        out_shape=[
            low(seq, D),
            low(seq, hidden),
            full(seq, D),
            low(seq, D),
            low(seq, D),
            full(8, D),
            full(1, hidden),
        ],
        compiler_params=pltpu.CompilerParams(vmem_limit_bytes=VMEM),
        cost_estimate=OTHER,
        name="feed_back",
    )(at, bucket, cotangent, spot, middle, slope, returned, *weights)


def feed_grads_kernel(wide, half_ref, second_ref, hidden_ref, active_ref, grad_ref, *refs):
    step = pl.program_id(0)
    refs[-1][...] = jnp.zeros_like(refs[-1])

    @pl.when(step < 2)
    def _():
        grad = tn(second_ref[...], hidden_ref[...])
        if len(refs) == 3:
            refs[0][0] = grad.astype(jnp.bfloat16)
        else:
            grad = (grad + refs[0][0].astype(jnp.float32)).astype(jnp.bfloat16)

            @pl.when(step == 0)
            def _():
                refs[2][...] = grad[None]

            @pl.when(step == 1)
            def _():
                refs[3][...] = grad[None]

    @pl.when(step >= 2)
    def _():
        whole = tn(active_ref[...], grad_ref[...])
        pieces = 4
        rows = D // wide
        places = whole.shape[0] // (pieces * rows)
        whole = whole.reshape(places, pieces, rows, D // 2)
        for piece in range(pieces):
            at = (piece // 2, slice(None), slice(piece % 2 * (D // 2), (piece % 2 + 1) * (D // 2)))
            part = whole[:, piece].reshape(places * rows, D // 2)
            if len(refs) == 3:
                refs[1][at] = part.astype(jnp.bfloat16)
            else:
                part = part + refs[1][at].astype(jnp.float32)
                refs[4][at], refs[5][at] = split_rows(part, places, half_ref[2])


def feed_grads(half, second, hidden_grad, active, feed_grad, wide, got=None):
    seq, hidden = active.shape
    chunk = lambda i: jnp.maximum(i - 2, 0)
    turned = lambda i, half: jnp.minimum(i, 1) ^ (1 - half[1])
    low = lambda *s: jax.ShapeDtypeStruct(s, jnp.bfloat16)
    expand_tile = pl.BlockSpec((1, D, D), lambda i, half: (turned(i, half), 0, 0))
    rows_of = lambda rows: pl.BlockSpec((2, rows, D), lambda i, half: (0, chunk(i), 0))
    if got is None:
        more = ()
        outs = [(expand_tile, low(2, D, D)), (rows_of(D // 4), low(2, D, D))]
    else:
        more = tuple(got)
        outs = [(whole_block((1, D, D)), low(1, D, D))] * 2
        outs += [(rows_of(D // 8), low(2, D // 2, D))] * 2
    outs.append((whole_block((8, 128)), MARK))
    return pl.pallas_call(
        partial(feed_grads_kernel, wide),
        grid_spec=pltpu.PrefetchScalarGridSpec(
            num_scalar_prefetch=1,
            grid=(6,),
            in_specs=[
                whole_block((seq, D)),
                pl.BlockSpec((seq, D), lambda i, half: (0, half[0] * 2 + turned(i, half))),
                pl.BlockSpec((seq, D), lambda i, half: (0, chunk(i))),
                pl.BlockSpec((seq, D // 2), lambda i, half: (0, half[0])),
            ]
            + [expand_tile, rows_of(D // 4)][: len(more)],
            out_specs=[o[0] for o in outs],
        ),
        out_shape=[o[1] for o in outs],
        compiler_params=pltpu.CompilerParams(vmem_limit_bytes=VMEM),
        cost_estimate=OTHER if got is None else OWN,
        name="feed_grads",
    )(half, second, hidden_grad, active, feed_grad, *more)


def last_kind(turn, half):
    return (turn // 2 ^ (1 - half[0])) * 2 + turn % 2


def last_grads_kernel(
    half_ref, first_ref, mixed_ref, a_ref, b_ref, c_ref, branch_ref, sent_ref, kept_ref, mark_ref
):
    turn = pl.program_id(0)
    kind = last_kind(turn, half_ref)
    mark_ref[...] = jnp.zeros_like(mark_ref)

    def put(whole):
        whole = whole.astype(jnp.bfloat16)

        @pl.when(turn < 2)
        def _():
            for i in range(6):
                sent_ref[i] = whole[:, i * 128 : (i + 1) * 128]

        @pl.when(turn >= 2)
        def _():
            for i in range(6):
                kept_ref[i] = whole[:, i * 128 : (i + 1) * 128]

    @pl.when(kind < 3)
    def _():
        put(tn(first_ref[...], jnp.concatenate([a_ref[0], b_ref[0], c_ref[0]], axis=1)))

    @pl.when(kind == 3)
    def _():
        put(tn(mixed_ref[...], branch_ref[...]))


def last_grads(half, first_in, mixed, parts, branch_grad):
    seq = mixed.shape[0]
    part = lambda a: pl.BlockSpec(
        (1,) + a.shape[1:], lambda i, half: (jnp.minimum(last_kind(i, half), 2), 0, 0)
    )
    tiles = jax.ShapeDtypeStruct((12, D, 128), jnp.bfloat16)
    return pl.pallas_call(
        last_grads_kernel,
        grid_spec=pltpu.PrefetchScalarGridSpec(
            num_scalar_prefetch=1,
            grid=(4,),
            in_specs=[whole_block((seq, D)), whole_block((seq, D))]
            + [part(a) for a in parts]
            + [whole_block((seq, D))],
            out_specs=[
                pl.BlockSpec((6, D, 128), lambda i, half: (jnp.minimum(i, 1), 0, 0)),
                pl.BlockSpec((6, D, 128), lambda i, half: (jnp.maximum(i - 2, 0), 0, 0)),
                whole_block((8, 128)),
            ],
        ),
        out_shape=[tiles, tiles, MARK],
        compiler_params=pltpu.CompilerParams(vmem_limit_bytes=VMEM),
        cost_estimate=OTHER,
        name="last_grads",
    )(half, first_in, mixed, *parts, branch_grad)


def tokens_back_kernel(
    tokens_ref, a_ref, b_ref, c_ref, middle_ref, gain_ref, weight_ref, out_ref, packed_ref, sums_ref
):
    @pl.when(pl.program_id(0) == 0)
    def _():
        sums_ref[...] = jnp.zeros_like(sums_ref)

    def add_sum(row, value):
        sums_ref[row : row + 1, :] += jnp.sum(value, axis=0, keepdims=True)

    query, keys, value = [
        jnp.concatenate([a_ref[i], b_ref[i], c_ref[i]], axis=1) for i in range(3)
    ]
    grad = nt(query, weight_ref[:, :D])
    grad = grad + nt(keys, weight_ref[:, D : 2 * D])
    grad = grad + nt(value, weight_ref[:, 2 * D :])
    normed, inverse = normalize(tokens_ref[...].astype(jnp.float32))
    add_sum(0, grad * normed)
    add_sum(1, grad)
    add_sum(2, query.astype(jnp.float32))
    add_sum(3, value.astype(jnp.float32))
    out_ref[...] = middle_ref[...] + normalize_back(grad * line(gain_ref), normed, inverse)

    @pl.when(pl.program_id(0) == pl.num_programs(0) - 1)
    def _():
        wide = packed_ref.shape[0]
        part = D // wide
        for w in range(wide):
            packed_ref[w : w + 1, :part] = sums_ref[0:1, w * part : (w + 1) * part]
            packed_ref[w : w + 1, part : 2 * part] = sums_ref[1:2, w * part : (w + 1) * part]
            bias_row = 2 + w * 2 // wide
            at = w % (wide // 2) * 2 * part
            packed_ref[w : w + 1, 2 * part :] = sums_ref[bias_row : bias_row + 1, at : at + 2 * part]


def tokens_back(tokens, parts, middle_grad, gain, weight, wide):
    seq = tokens.shape[0]
    return pl.pallas_call(
        tokens_back_kernel,
        grid=(seq // ROWS,),
        in_specs=[by_block(D)]
        + [pl.BlockSpec((3, ROWS, a.shape[2]), lambda i: (0, i, 0)) for a in parts]
        + [by_block(D)] + [whole_block(gain.shape), whole_block(weight.shape)],
        out_specs=[by_block(D), whole_block((wide, 4 * D // wide))],
        out_shape=[
            jax.ShapeDtypeStruct((seq, D), jnp.float32),
            jax.ShapeDtypeStruct((wide, 4 * D // wide), jnp.float32),
        ],
        scratch_shapes=[pltpu.VMEM((8, D), jnp.float32)],
        compiler_params=pltpu.CompilerParams(vmem_limit_bytes=VMEM),
        cost_estimate=OTHER,
        name="tokens_back",
    )(tokens, *parts, middle_grad, gain, weight)


def pack_kernel(feed_ref, hidden_ref, input_ref, final_ref, token_ref, *refs):
    low_ref, out_ref = refs[-2:]
    out_ref[...] = jnp.zeros_like(out_ref)
    wide, rows, cols = out_ref.shape
    part = D // wide
    block = input_ref.shape[1] // wide
    for w in range(wide):
        out_ref[w, :TOKEN_DIM, :block] = input_ref[:, w * block : (w + 1) * block]
        out_ref[w, :TOKEN_DIM, block : 2 * block] = final_ref[:, w * block : (w + 1) * block]
        out_ref[w, TOKEN_DIM : TOKEN_DIM + 1, :] = hidden_ref[:, w * cols : (w + 1) * cols]
        out_ref[w, TOKEN_DIM + 2 : TOKEN_DIM + 3, :] = token_ref[w : w + 1, :]
        for i in range(4):
            out_ref[w, TOKEN_DIM + 1 : TOKEN_DIM + 2, i * part : (i + 1) * part] = feed_ref[
                i : i + 1, w * part : (w + 1) * part
            ]
    low_ref[...] = out_ref[...].astype(jnp.bfloat16)


def pack(feed_sums, hidden_sum, input_grad, final_grad, token_packed, marks):
    operands = (feed_sums, hidden_sum, input_grad, final_grad, token_packed)
    wide = token_packed.shape[0]
    shape = (wide, TOKEN_DIM + 16, hidden_sum.shape[1] // wide)
    return pl.pallas_call(
        pack_kernel,
        grid=(1,),
        in_specs=[whole_block(a.shape) for a in operands] + [pl.BlockSpec(memory_space=pl.ANY)] * len(marks),
        out_specs=whole_block(shape),
        out_shape=jax.ShapeDtypeStruct(shape, jnp.bfloat16),
        scratch_shapes=[pltpu.VMEM(shape, jnp.float32)],
        cost_estimate=OTHER,
        name="pack",
    )(*operands, *marks)


def add_up(terms):
    total = terms[0].astype(jnp.float32)
    for term in terms[1:]:
        total = total + term.astype(jnp.float32)
    return total


def swap(array, axis, mask):
    count = lax.axis_size(axis)
    return lax.ppermute(array, axis, [(i, i ^ mask) for i in range(count)])


def bit(axis, mask):
    return lax.axis_index(axis) // mask % 2


def pick(array, index, axis):
    return lax.dynamic_index_in_dim(array, index, axis, keepdims=False)


class Order:
    def __init__(self):
        self.mark = ()
        self.marks = ()

    def __call__(self, *values):
        out = lax.optimization_barrier(values + self.mark)[: len(values)]
        return out if len(values) > 1 else out[0]

    def at(self, *values):
        self.mark = values


def bits():
    return jnp.stack([bit("narrow", 1), bit("narrow", 2), bit("wide", 1)]).astype(jnp.int32)


class Flow:
    AXES = {"x": ("narrow", 2), "y": ("wide", 1)}

    def __init__(self, order, lanes, sends=None):
        self.order = order
        self.wide = lax.axis_size("wide").bit_length() - 1
        self.lanes = [[list(terms), tuple(left)] for terms, left in lanes]
        self.steps = self.run(sends)

    def step(self):
        next(self.steps)

    def take(self):
        got = self.order(*self.got)
        return got if isinstance(got, (tuple, list)) else (got,)

    def send(self, *sends):
        self.got = tuple(swap(*s) for s in sends)
        self.order.at(*[s[0] for s in sends])

    def shaped(self, array, left):
        dims = (2,) * (self.wide - ("y" not in left))
        if "x" in left:
            return array.reshape((2, array.shape[0] // 2) + dims + (-1, array.shape[2]))
        return array.reshape((array.shape[0],) + dims + (-1, array.shape[2]))

    def exchange(self, lane, goal):
        terms, left = lane
        dim = 0 if goal == "x" else self.wide + ("x" in left)
        mine = bit(*self.AXES[goal])
        sent = add_up([pick(t, 1 - mine, dim) for t in terms]).astype(jnp.bfloat16)
        lane[0] = [pick(t, mine, dim) for t in terms]
        lane[1] = tuple(n for n in left if n != goal)
        return (sent,) + self.AXES[goal]

    def run(self, sends):
        if sends is not None:
            shapes = [lane[0][0].shape for lane in self.lanes]
            self.send(*sends)
            yield
            got = self.take()
            for lane, g, shape in zip(self.lanes, got, shapes):
                lane[0].append(g.reshape(shape))
        while any(lane[1] for lane in self.lanes):
            self.send(*[self.exchange(lane, lane[1][0]) for lane in self.lanes])
            yield
            for lane, got in zip(self.lanes, self.take()):
                lane[0].append(got)
        parts = [lane[0] for lane in self.lanes]
        both = []
        for b in reversed(range(1, self.wide)):
            mask = 1 << b
            mine = bit("wide", mask)
            sent = [add_up([pick(t, 1 - mine, 1) for t in terms]) for terms in parts]
            sent = [jnp.concatenate(sent, axis=0)] + [pick(t, 1 - mine, 1) for t in both]
            parts = [[pick(t, mine, 1) for t in terms] for terms in parts]
            both = [pick(t, mine, 1) for t in both]
            self.send((add_up(sent).astype(jnp.bfloat16), "wide", mask))
            yield
            both.append(self.take()[0])
        own = jnp.concatenate([add_up(terms) for terms in parts], axis=0)
        share = add_up([own] + both).astype(jnp.bfloat16)
        self.send((share, "narrow", 2))
        yield
        (other,) = self.take()
        share = self.order(share)
        self.send((share, "narrow", 1), (other, "narrow", 1))
        yield
        self.result = (share, other) + tuple(self.take())
        yield

    def finish(self):
        for unused in self.steps:
            pass
        return self.result


class Halves:
    def __init__(self, order, sent):
        *sent, mark = sent
        self.order = order
        self.flight = tuple(swap(a, "narrow", 1) for a in sent)
        order.at(mark)
        order.marks += (mark,)

    def got(self):
        got = self.order(*self.flight)
        return tuple(got) if isinstance(got, (tuple, list)) else (got,)


def unpack_kernel(put, bits_ref, *refs):
    shares, outs = refs[:4], refs[4:]
    core, x = bits_ref[0], bits_ref[1]
    for c in range(2):
        for k in range(2):
            same_x, same_core = x == k, core == c
            for t in range(shares[0].shape[0]):
                one, two, three, four = [s[t].astype(jnp.float32) for s in shares]
                near = jnp.where(same_x, one, two)
                far = jnp.where(same_x, three, four)
                put(outs, c, k, t, jnp.where(same_core, near, far))


def unpack(put, shares, shapes):
    return pl.pallas_call(
        partial(unpack_kernel, put),
        grid=(1,),
        in_specs=[smem()] + [whole_block(a.shape) for a in shares],
        out_specs=[whole_block(s) for s in shapes],
        out_shape=[jax.ShapeDtypeStruct(s, jnp.float32) for s in shapes],
        compiler_params=pltpu.CompilerParams(vmem_limit_bytes=VMEM),
        cost_estimate=OTHER,
        name="unpack",
    )(bits(), *shares)


def put_columns(spans, tiles):
    def put(outs, c, x, t, value):
        column = (c * 2 + x) * tiles + t
        for out_ref, (first, stop) in zip(outs, spans):
            if first <= column < stop:
                at = (column - first) * value.shape[1]
                out_ref[:, at : at + value.shape[1]] = value

    return put


def small_steps(order, rows):
    def send(*sends):
        order.at(*[s[0] for s in sends])
        return [swap(*s) for s in sends]

    wide = lax.axis_size("wide")
    low = rows.astype(jnp.bfloat16)
    for mask in (1, 2):
        (got,) = send((low, "narrow", mask))
        yield
        low = add_up([low, order(got)]).astype(jnp.bfloat16)
    low = low.reshape((wide // 2, 2) + low.shape[1:])
    mine = bit("wide", 1)
    (got,) = send((pick(low, 1 - mine, 1), "wide", 1))
    yield
    low = add_up([pick(low, mine, 1), order(got)]).astype(jnp.bfloat16)
    place = lax.axis_index("wide") // 2
    got = send(*[(pick(low, place ^ (m // 2), 0), "wide", m) for m in range(2, wide, 2)])
    yield
    yield add_up([pick(low, place, 0)] + list(order(*got)))


def shards(
    tokens,
    cotangent,
    latents,
    added_noise,
    timesteps,
    bucket,
    masked,
    deal_start,
    first_gain,
    first_shift,
    joint_weight,
    query_value_bias,
    output_weight,
    output_bias,
    second_gain,
    second_shift,
    expand_weight,
    expand_bias,
    reduce_weight,
    reduce_bias,
    input_proj,
    cond_proj,
    time_first,
    time_second,
    block_mod,
    block_expand,
    block_reduce,
    final_mod,
    final_proj,
):
    wide = lax.axis_size("wide")
    narrow = lax.axis_size("narrow")
    place_wide = lax.axis_index("wide")
    place_narrow = lax.axis_index("narrow")
    mine = bits()
    other = mine.at[0].set(1 - mine[0])
    image_index = place_wide * narrow + place_narrow
    at = jnp.stack([image_index, place_wide, place_narrow, jnp.int32(narrow)]).astype(jnp.int32)

    spot, live = places(at, bucket, deal_start, masked, wide)
    slots = spot.shape[1]
    steps = timesteps.astype(jnp.float32)
    half = time_first.shape[0] // 2
    freqs = jnp.exp(-math.log(10000.0) * jnp.arange(half).astype(jnp.float32) / half)
    angles = steps.reshape(-1, 1) * freqs
    sinus = jnp.concatenate([jnp.cos(angles), jnp.sin(angles)], axis=-1).astype(jnp.bfloat16)
    offset = steps * STEP_ANGLE
    keep_sig = jnp.cos(offset + SHIFT_ANGLE) / math.cos(SHIFT_ANGLE)
    drop_sig = jnp.sqrt(jnp.sin(offset) * jnp.sin(offset + 2.0 * SHIFT_ANGLE)) / math.cos(SHIFT_ANGLE)
    input_turned = input_proj.T
    final_turned = final_proj.T

    first_in, joint = joint_pass(
        tokens, first_gain, first_shift, joint_weight, query_value_bias
    )
    mixed, logsum = attend(at, bucket, joint)
    block_output, middle, second_in, active, slope, dealt, spread = feed_pass(
        at,
        bucket,
        mixed,
        tokens,
        latents,
        spot,
        (
            output_weight,
            output_bias,
            second_gain,
            second_shift,
            expand_weight,
            expand_bias,
            reduce_weight,
            reduce_bias,
        ),
    )

    def deal(array):
        shape = array.shape
        return lax.all_to_all(
            array.reshape(wide, -1, shape[1]), "wide", split_axis=0, concat_axis=0, tiled=True
        ).reshape(shape)

    dealt = deal(dealt)
    low_turned, time_slope, timed = time_embedding(sinus, time_first, time_second)
    (
        guess,
        left,
        fin_grad,
        branch_grad,
        upper_grad,
        mod_grad,
        timed_grad,
        embed_grad,
        rows_grad,
        input_grad,
        final_grad,
    ) = head_pass(
        dealt,
        timed,
        keep_sig[:, None, :],
        drop_sig[:, None, :],
        added_noise,
        live,
        (input_turned, cond_proj, block_mod, block_expand, block_reduce, final_mod, final_turned),
    )
    order = Order()
    order.at(rows_grad)
    returned = deal(rows_grad)
    first_grad = time_back(order(timed_grad), time_second, time_slope)
    order.at(first_grad)
    one_args = (fin_grad, branch_grad, upper_grad)
    halves_one = Halves(order, head_grads_one(other, order(left), *one_args))
    two_args = (mod_grad, timed_grad, dealt, embed_grad, sinus, first_grad, wide)
    halves_two = Halves(order, head_grads_two(other, left, order(low_turned), *two_args))
    returned = order(returned)
    order.at(returned, *order.mark)

    def note(mark):
        order.marks += (mark,)
        order.at(mark)

    sent, kept, mark = head_grads_one(mine, order(left), *one_args, *halves_one.got())
    note(mark)
    shape = lambda a: a.reshape((a.shape[0],) + (2,) * (wide.bit_length() - 1) + (-1, a.shape[2]))
    half_shape = lambda a: a.reshape(
        (2, a.shape[0] // 2) + (2,) * (wide.bit_length() - 2) + (-1, a.shape[2])
    )
    one = Flow(order, [([shape(kept)], ("y",))], [(sent, "narrow", 2)])
    one.step()
    order.at(mark)
    sent_a, kept_a, sent_b, kept_b, mark = head_grads_two(
        mine, left, order(low_turned), *two_args, *halves_two.got()
    )
    note(mark)
    two = Flow(
        order,
        [([shape(kept_a)], ("y",)), ([half_shape(kept_b)], ("x",))],
        [(sent_a, "narrow", 2), (sent_b, "wide", 1)],
    )
    two.step()
    order.at(mark)
    feed_grad, hidden_grad, middle_grad, out_grad, mixed_grad, feed_sums, hidden_sum = feed_back(
        at,
        bucket,
        order(cotangent),
        spot,
        middle,
        slope,
        returned,
        (output_weight, second_gain, expand_weight, reduce_weight),
    )
    order.at(mixed_grad)
    feed_args = (hidden_grad, active, feed_grad, wide)
    halves_feed = Halves(order, feed_grads(other, order(second_in), *feed_args))
    one.step()
    parts = []

    def attend_back_part(i):
        grads = attend_back(2 * i, 2, at, bucket, joint, order(mixed_grad), mixed, logsum)
        order.at(grads)
        parts.append(grads)

    attend_back_part(0)
    two.step()
    sent_e, kept_e, sent_r, kept_r, mark = feed_grads(
        mine, order(second_in), *feed_args, halves_feed.got()
    )
    note(mark)
    feed = Flow(
        order,
        [([shape(kept_e)], ("y",)), ([half_shape(kept_r)], ("x",))],
        [(sent_e, "narrow", 2), (sent_r, "wide", 1)],
    )
    feed.step()
    order.at(mark)
    one.step()
    attend_back_part(1)
    two.step()
    one.step()
    feed.step()
    attend_back_part(2)
    feed.step()
    two.step()
    one.step()
    sent, own, mark = last_grads(mine, order(first_in), mixed, parts, out_grad)
    halves_last = Halves(order, (sent, mark))
    terms = [
        a.reshape((2, 6) + (2,) * (wide.bit_length() - 1) + (-1, 128)) for a in (own,) + halves_last.got()
    ]
    last = Flow(
        order, [([a[:, :3] for a in terms], ("x", "y")), ([a[:, 3:] for a in terms], ("y", "x"))]
    )
    last.step()
    tokens_gradient, token_packed = tokens_back(
        order(tokens), parts, middle_grad, first_gain, joint_weight, wide
    )
    order.at(token_packed)
    width = cond_proj.shape[1]
    rows = width // wide
    cut = cond_proj.shape[0] // wide

    def hold(outs):
        order.at(*outs)
        return outs

    last.step()
    two.step()
    feed.step()
    one.step()
    packed = pack(feed_sums, hidden_sum, input_grad, final_grad, order(token_packed), order.marks)
    order.at(packed)
    small = small_steps(order, packed)
    next(small)
    last.step()
    next(small)
    one = one.finish()
    final_mod_out, block_reduce_out, block_expand_out = hold(
        unpack(
            put_columns(((0, 4), (4, 6), (6, 8)), 2),
            (order(one[0]),) + one[1:],
            ((rows, 2 * width), (rows, width), (rows, width)),
        )
    )
    two.step()
    feed.step()
    two = two.finish()

    def put_two(outs, c, x, t, value):
        column = (c * 2 + x) * 5 + t
        if column < 16:
            put_columns(((0, 12), (12, 16)), 5)(outs, c, x, t, value)
        else:
            cols = slice((column - 16) * 256, (column - 15) * 256)
            outs[2][:, cols] = value[:cut]
            outs[3][:, cols] = value[cut:]

    block_mod_out, time_second_out, cond_out, time_first_out = hold(
        unpack(
            put_two,
            (order(two[0]),) + two[1:],
            ((rows, 3 * width), (rows, width), (cut, width), (rows - cut, width)),
        )
    )
    last.step()
    next(small)
    feed.step()
    feed = feed.finish()

    def put_feed(outs, c, x, t, value):
        if t == 0:
            at = (c * 2 + x) * D
            outs[0][:, at : at + D] = value
        else:
            for i in range(2):
                piece = x * 2 + i
                outs[1][piece * cut : (piece + 1) * cut, c * (D // 2) : (c + 1) * (D // 2)] = value[
                    :, i * (D // 2) : (i + 1) * (D // 2)
                ]

    last.step()
    next(small)
    expand_out, reduce_out = hold(
        unpack(put_feed, (order(feed[0]),) + feed[1:], ((cut, 4 * D), (4 * cut, D)))
    )
    last.step()
    small = next(small)
    last = last.finish()
    joint_out, output_out = unpack(
        put_columns(((0, 18), (18, 24)), 6), last, ((cut, 3 * D), (cut, D))
    )
    part = D // wide
    block = input_grad.shape[1] // wide
    vectors = [small[TOKEN_DIM + 1, i * part : (i + 1) * part] for i in range(4)]
    input_out = small[:TOKEN_DIM, :block].T
    final_out = small[:TOKEN_DIM, block : 2 * block].T
    late = small[TOKEN_DIM + 2]
    outs = [
        late[:part],
        late[part : 2 * part],
        late[2 * part :],
        vectors[3],
        vectors[1],
        vectors[2],
        small[TOKEN_DIM],
        vectors[0],
        input_out,
        final_out,
    ]
    return (
        block_output,
        guess,
        spread[:2, 0].reshape(1, 2),
        tokens_gradient,
        outs[0],
        outs[1],
        joint_out,
        outs[2],
        output_out,
        outs[3],
        outs[4],
        outs[5],
        expand_out,
        outs[6],
        reduce_out,
        outs[7],
        outs[8],
        cond_out,
        time_first_out,
        time_second_out,
        block_mod_out,
        block_expand_out,
        block_reduce_out,
        final_mod_out,
        outs[9],
    )


def solution(mesh):
    in_specs = (
        P(("wide", "narrow"), None),
        P(("wide", "narrow"), None),
        P(("wide", "narrow"), None),
        P(None, None, ("wide", "narrow")),
        P(None, ("wide", "narrow")),
        P(),
        P(("wide", "narrow"), None),
        P(),
        P(),
        P(),
        P(),
        P(),
        P(),
        P(),
        P(),
        P(),
        P(),
        P(),
        P(),
        P(),
        P(),
        P(),
        P(),
        P(),
        P(),
        P(),
        P(),
        P(),
        P(),
    )
    out_specs = (
        P(("wide", "narrow"), None),
        P(None, None, ("wide", "narrow")),
        P(("wide", "narrow"), None),
        P(("wide", "narrow"), None),
        P("wide"),
        P("wide"),
        P("wide", None),
        P("wide"),
        P("wide", None),
        P("wide"),
        P("wide"),
        P("wide"),
        P("wide", None),
        P("wide"),
        P("wide", None),
        P("wide"),
        P("wide", None),
        P("wide", None),
        P("wide", None),
        P("wide", None),
        P("wide", None),
        P("wide", None),
        P("wide", None),
        P("wide", None),
        P("wide", None),
    )
    return jax.shard_map(shards, mesh=mesh, in_specs=in_specs, out_specs=out_specs, check_vma=False)
```

```python
from functools import partial
import math

import jax
import jax.numpy as jnp
from jax import lax
from jax.experimental import pallas as pl
from jax.experimental.pallas import tpu as pltpu
from jax.sharding import PartitionSpec as P

D = 768
HEADS = 12
HEAD_DIM = 64
TOKEN_DIM = 16
BUFFER = 64
IMAGE_MAX = 1024
MASK_MAX = 256
REPEATS = 4
SEQ = 1088


SHIFT_ANGLE = 0.008 / 1.008 * math.pi / 2.0
STEP_ANGLE = math.pi / (2.0 * 1.008 * 1000.0)
PAIRS = 6
VMEM = 60 * 1024 * 1024

OWN = pl.CostEstimate(flops=1 << 40, bytes_accessed=1 << 20, transcendentals=0)
OTHER = pl.CostEstimate(flops=0, bytes_accessed=1 << 20, transcendentals=0)


def nt(a,b): return lax.dot_general(a,b,(((1,),(1,)),((),())),preferred_element_type=jnp.float32)
def nn(a,b): return jnp.dot(a,b,preferred_element_type=jnp.float32)
def tn(a,b): return lax.dot_general(a,b,(((0,),(0,)),((),())),preferred_element_type=jnp.float32)
def normalize(values):
    centre = values - jnp.mean(values, axis=-1, keepdims=True)
    inverse = lax.rsqrt(jnp.mean(centre * centre, axis=-1, keepdims=True) + 1e-06)
    return (centre * inverse, inverse)


def normalize_back(grad_normed, normed, inverse):
    return inverse * (
        grad_normed
        - jnp.mean(grad_normed, axis=-1, keepdims=True)
        - normed * jnp.mean(grad_normed * normed, axis=-1, keepdims=True)
    )


def sigmoid(value):
    return 0.5 * jnp.tanh(0.5 * value) + 0.5


def silu_slope(value, sigma):
    return sigma * (1.0 + value * (1.0 - sigma))


def whole_block(shape):
    zeros = (0,) * len(shape)
    return pl.BlockSpec(shape, lambda *unused: zeros, pipeline_mode=pl.Buffered(1))


def time_kernel(sinus_ref, first_ref, second_ref, low_ref, slope_ref, timed_ref):
    first = nn(sinus_ref[...], first_ref[...])
    sigma = sigmoid(first)
    low = (first * sigma).astype(jnp.bfloat16)
    slope_ref[...] = silu_slope(first, sigma).astype(jnp.bfloat16)
    low_ref[...] = low.T
    timed_ref[...] = nn(low, second_ref[...])


def time_embedding(sinus, time_first, time_second):
    count, freq = sinus.shape
    width = time_first.shape[1]
    rows = count // REPEATS
    by_rows = pl.BlockSpec((rows, width), lambda i: (i, 0))
    return pl.pallas_call(
        time_kernel,
        grid=(REPEATS,),
        in_specs=[
            pl.BlockSpec((rows, freq), lambda i: (i, 0)),
            whole_block(time_first.shape),
            whole_block(time_second.shape),
        ],
        out_specs=[pl.BlockSpec((width, rows), lambda i: (0, i)), by_rows, by_rows],
        out_shape=[
            jax.ShapeDtypeStruct((width, count), jnp.bfloat16),
            jax.ShapeDtypeStruct((count, width), jnp.bfloat16),
            jax.ShapeDtypeStruct((count, width), jnp.float32),
        ],
        compiler_params=pltpu.CompilerParams(vmem_limit_bytes=VMEM),
        cost_estimate=OTHER,
        name="time_embedding",
    )(sinus, time_first, time_second)


def head_kernel(
    dealt_ref,
    timed_ref,
    keep_ref,
    drop_ref,
    noise_ref,
    live_ref,
    input_ref,
    cond_ref,
    mod_ref,
    expand_ref,
    reduce_ref,
    fin_ref,
    final_ref,
    guess_ref,
    left_ref,
    fin_grad_ref,
    branch_grad_ref,
    upper_grad_ref,
    mod_grad_ref,
    timed_grad_ref,
    embed_grad_ref,
    rows_grad_ref,
    input_grad_ref,
    final_grad_ref,
    embed_scratch,
    total_scratch,
):
    turn = pl.program_id(0)
    width = timed_ref.shape[1]

    @pl.when(turn == 0)
    def _():
        embed_scratch[...] = nn(dealt_ref[:, :D], cond_ref[...])
        total_scratch[...] = jnp.zeros_like(total_scratch)
        input_grad_ref[...] = jnp.zeros_like(input_grad_ref)
        final_grad_ref[...] = jnp.zeros_like(final_grad_ref)

    cond = embed_scratch[...] + timed_ref[...]
    acted = (cond * sigmoid(cond)).astype(jnp.bfloat16)
    left_ref[0] = acted.T
    start = dealt_ref[:, D:].astype(jnp.float32).T[:TOKEN_DIM]
    noise = noise_ref[0]
    noisy = (keep_ref[0] * start + drop_ref[0] * noise).astype(jnp.bfloat16)
    entry = tn(noisy, input_ref[...])
    inner_normed, inner_inverse = normalize(entry)
    shift_a = nn(acted, mod_ref[:, :width])
    scale_a = nn(acted, mod_ref[:, width : 2 * width])
    gate_a = nn(acted, mod_ref[:, 2 * width :])
    inner = (inner_normed * (1.0 + scale_a) + shift_a).astype(jnp.bfloat16)
    left_ref[2] = inner.T
    upper = nn(inner, expand_ref[...])
    upper_sigma = sigmoid(upper)
    lifted = (upper * upper_sigma).astype(jnp.bfloat16)
    left_ref[1] = lifted.T
    branch = nn(lifted, reduce_ref[...])
    shift_b = nn(acted, fin_ref[:, :width])
    scale_b = nn(acted, fin_ref[:, width:])
    last_normed, last_inverse = normalize(entry + gate_a * branch)
    last = (last_normed * (1.0 + scale_b) + shift_b).astype(jnp.bfloat16)
    live = live_ref[...]
    guess = nt(final_ref[...], last) * live
    guess_ref[0] = guess
    guess_grad = (2.0 / REPEATS * (guess - noise * live) * live).astype(jnp.bfloat16)
    final_grad_ref[...] += nn(guess_grad, last)
    last_grad = tn(guess_grad, final_ref[...])
    fin_grad = jnp.concatenate([last_grad, last_grad * last_normed], axis=1).astype(jnp.bfloat16)
    fin_grad_ref[...] = fin_grad
    after_grad = normalize_back(last_grad * (1.0 + scale_b), last_normed, last_inverse)
    branch_grad = (after_grad * gate_a).astype(jnp.bfloat16)
    branch_grad_ref[...] = branch_grad
    lifted_grad = nt(branch_grad, reduce_ref[...])
    upper_grad = (lifted_grad * silu_slope(upper, upper_sigma)).astype(jnp.bfloat16)
    upper_grad_ref[...] = upper_grad
    inner_grad = nt(upper_grad, expand_ref[...])
    entry_grad = (
        after_grad + normalize_back(inner_grad * (1.0 + scale_a), inner_normed, inner_inverse)
    ).astype(jnp.bfloat16)
    input_grad_ref[...] += nn(noisy, entry_grad)
    mod_grad = jnp.concatenate(
        [inner_grad, inner_grad * inner_normed, after_grad * branch], axis=1
    ).astype(jnp.bfloat16)
    mod_grad_ref[...] = mod_grad
    acted_grad = nt(mod_grad, mod_ref[...]) + nt(fin_grad, fin_ref[...])
    cond = embed_scratch[...] + timed_ref[...]
    cond_grad = acted_grad * silu_slope(cond, sigmoid(cond))
    timed_grad_ref[...] = cond_grad.astype(jnp.bfloat16)
    total_scratch[...] += cond_grad

    @pl.when(turn == REPEATS - 1)
    def _():
        embed_grad = total_scratch[...].astype(jnp.bfloat16)
        embed_grad_ref[...] = embed_grad
        rows_grad_ref[...] = nt(embed_grad, cond_ref[...]).astype(jnp.bfloat16)


def head_pass(dealt, timed, keep_sig, drop_sig, noise, live, weights):
    input_proj, cond_proj, block_mod, block_expand, block_reduce, final_mod, final_proj = weights
    slots = dealt.shape[0]
    width = cond_proj.shape[1]
    count = REPEATS * slots
    by_rows = lambda n: pl.BlockSpec((slots, n), lambda i: (i, 0))
    by_turn = lambda a: pl.BlockSpec((1,) + a, lambda i: (i, 0, 0))
    low = lambda *s: jax.ShapeDtypeStruct(s, jnp.bfloat16)
    full = lambda *s: jax.ShapeDtypeStruct(s, jnp.float32)
    operands = (
        dealt,
        timed,
        keep_sig,
        drop_sig,
        noise,
        live,
        input_proj,
        cond_proj,
        block_mod,
        block_expand,
        block_reduce,
        final_mod,
        final_proj,
    )
    return pl.pallas_call(
        head_kernel,
        grid=(REPEATS,),
        in_specs=[
            whole_block(dealt.shape),
            by_rows(width),
            by_turn((1, slots)),
            by_turn((1, slots)),
            by_turn((TOKEN_DIM, slots)),
        ]
        + [whole_block(a.shape) for a in operands[5:]],
        out_specs=[
            by_turn((TOKEN_DIM, slots)),
            pl.BlockSpec((3, width, slots), lambda i: (0, 0, i)),
            by_rows(2 * width),
            by_rows(width),
            by_rows(width),
            by_rows(3 * width),
            by_rows(width),
            whole_block((slots, width)),
            whole_block((slots, D)),
            whole_block((TOKEN_DIM, width)),
            whole_block((TOKEN_DIM, width)),
        ],
        out_shape=[
            full(REPEATS, TOKEN_DIM, slots),
            low(3, width, count),
            low(count, 2 * width),
            low(count, width),
            low(count, width),
            low(count, 3 * width),
            low(count, width),
            low(slots, width),
            low(slots, D),
            full(TOKEN_DIM, width),
            full(TOKEN_DIM, width),
        ],
        scratch_shapes=[pltpu.VMEM((slots, width), jnp.float32)] * 2,
        compiler_params=pltpu.CompilerParams(vmem_limit_bytes=VMEM),
        cost_estimate=OTHER,
        name="head_pass",
    )(*operands)


MARK = jax.ShapeDtypeStruct((8, 128), jnp.float32)


def head_grads_one_kernel(half_ref, left_ref, fin_ref, branch_ref, upper_ref, *refs):
    turn = pl.program_id(0)
    tile = head_one_tile(turn, half_ref)

    def put(grad):
        if len(refs) == 2:
            out_ref, mark_ref = refs
            out_ref[0] = grad.astype(jnp.bfloat16)
        else:
            got_ref, sent_ref, kept_ref, mark_ref = refs
            grad = (grad + got_ref[0].astype(jnp.float32)).astype(jnp.bfloat16)

            @pl.when(turn < 2)
            def _():
                sent_ref[0] = grad

            @pl.when(turn >= 2)
            def _():
                kept_ref[0] = grad

        mark_ref[...] = jnp.zeros_like(mark_ref)

    @pl.when(tile < 4)
    def _():
        put(nn(left_ref[0], fin_ref[...]))

    @pl.when((tile >= 4) & (tile < 6))
    def _():
        put(nn(left_ref[0], branch_ref[...]))

    @pl.when(tile >= 6)
    def _():
        put(nn(left_ref[0], upper_ref[...]))


def head_one_tile(turn, half):
    return half[0] * 4 + (turn ^ (2 - 2 * half[1]))


def head_grads_one(half, left, fin_grad, branch_grad, upper_grad, got=None):
    width, count = left.shape[1:]
    cols = width // 2

    def at(first, tiles):
        return lambda i, half: (0, jnp.clip(head_one_tile(i, half) - first, 0, tiles - 1))

    def which(i, half):
        tile = head_one_tile(i, half)
        return (jnp.where(tile < 4, 0, jnp.where(tile < 6, 1, 2)), 0, 0)

    tiles = lambda n: jax.ShapeDtypeStruct((n, width, cols), jnp.bfloat16)
    block = lambda where: pl.BlockSpec((1, width, cols), where)
    if got is None:
        more = ()
        outs = [(block(lambda i, half: (i ^ (2 - 2 * half[1]), 0, 0)), tiles(4))]
    else:
        more = (got,)
        outs = [
            (block(lambda i, half: (jnp.minimum(i, 1), 0, 0)), tiles(2)),
            (block(lambda i, half: (jnp.maximum(i - 2, 0), 0, 0)), tiles(2)),
        ]
    outs.append((whole_block((8, 128)), MARK))
    return pl.pallas_call(
        head_grads_one_kernel,
        grid_spec=pltpu.PrefetchScalarGridSpec(
            num_scalar_prefetch=1,
            grid=(4,),
            in_specs=[
                pl.BlockSpec((1, width, count), which),
                pl.BlockSpec((count, cols), at(0, 4)),
                pl.BlockSpec((count, cols), at(4, 2)),
                pl.BlockSpec((count, cols), at(6, 2)),
            ]
            + [block(lambda i, half: (i ^ (2 - 2 * half[1]), 0, 0))] * len(more),
            out_specs=[o[0] for o in outs],
        ),
        out_shape=[o[1] for o in outs],
        compiler_params=pltpu.CompilerParams(vmem_limit_bytes=VMEM),
        cost_estimate=OTHER if got is None else OWN,
        name="head_grads_one",
    )(half, left, fin_grad, branch_grad, upper_grad, *more)


def time_back_kernel(grad_ref, weight_ref, slope_ref, out_ref):
    grad = nt(grad_ref[...], weight_ref[...])
    out_ref[...] = (grad * slope_ref[...].astype(jnp.float32)).astype(jnp.bfloat16)


def time_back(timed_grad, weight, slope):
    count, width = timed_grad.shape
    by_rows = pl.BlockSpec((count // 4, width), lambda i: (i, 0))
    return pl.pallas_call(
        time_back_kernel,
        grid=(4,),
        in_specs=[by_rows, whole_block(weight.shape), by_rows],
        out_specs=by_rows,
        out_shape=jax.ShapeDtypeStruct((count, width), jnp.bfloat16),
        compiler_params=pltpu.CompilerParams(vmem_limit_bytes=VMEM),
        cost_estimate=OTHER,
        name="time_back",
    )(timed_grad, weight, slope)


def split_rows(grad, wide, y):
    grad = grad.reshape((wide // 2, 2, -1) + grad.shape[1:])
    own, other = jnp.where(y == 0, grad[:, 0], grad[:, 1]), jnp.where(y == 0, grad[:, 1], grad[:, 0])
    flat = lambda a: a.reshape((-1,) + a.shape[2:]).astype(jnp.bfloat16)
    return flat(other), flat(own)


def head_grads_two_kernel(
    wide, half_ref, acted_ref, low_ref, mod_ref, timed_ref, rows_ref, embed_ref, sinus_ref, first_ref, *refs
):
    turn = pl.program_id(0)
    tile = half_ref[0] * 10 + head_two_tile(turn, half_ref)

    def put(grad):
        refs[-1][...] = jnp.zeros_like(refs[-1])
        if len(refs) == 2:
            refs[0][0] = grad.astype(jnp.bfloat16)
            return
        got_ref, sent_one, kept_one, sent_two, kept_two, unused = refs
        grad = grad + got_ref[0].astype(jnp.float32)

        @pl.when(turn < 2)
        def _():
            sent_one[0] = grad.astype(jnp.bfloat16)

        @pl.when((turn >= 5) & (turn < 7))
        def _():
            kept_one[0] = grad.astype(jnp.bfloat16)

        @pl.when(turn % 5 >= 2)
        def _():
            sent_two[0], kept_two[0] = split_rows(grad, wide, half_ref[2])

    @pl.when(tile < 12)
    def _():
        put(nn(acted_ref[0], mod_ref[...]))

    @pl.when((tile >= 12) & (tile < 16))
    def _():
        put(nn(low_ref[...], timed_ref[...]))

    @pl.when(tile >= 16)
    def _():
        cond = tn(rows_ref[:, :D], embed_ref[...])
        time = tn(sinus_ref[...], first_ref[...])
        cols = cond.shape[1]
        both = jnp.concatenate(
            [cond.reshape(wide, -1, cols), time.reshape(wide, -1, cols)], axis=1
        )
        put(both.reshape(-1, cols))


def head_two_tile(turn, half):
    return (turn // 5 ^ (1 - half[1])) * 5 + turn % 5


def head_grads_two(half, left, low, mod_grad, timed_grad, dealt, embed_grad, sinus, first_grad, wide, got=None):
    width, count = left.shape[1:]
    slots = dealt.shape[0]
    cols = width // 4

    def at(first, tiles):
        return lambda i, half: (0, jnp.clip(half[0] * 10 + head_two_tile(i, half) - first, 0, tiles - 1))

    whole = pl.BlockSpec((1, width, cols), lambda i, half: (head_two_tile(i, half), 0, 0))
    like = lambda n, rows: jax.ShapeDtypeStruct((n, rows, cols), jnp.bfloat16)
    if got is None:
        more = ()
        outs = [(whole, like(10, width))]
    else:
        more = (got,)
        block = lambda rows, where: pl.BlockSpec((1, rows, cols), where)

        def second(i, half):
            return ((i // 5 ^ (1 - half[1])) * 3 + jnp.maximum(i % 5 - 2, 0), 0, 0)

        outs = [
            (block(width, lambda i, half: (jnp.minimum(i, 1), 0, 0)), like(2, width)),
            (block(width, lambda i, half: (jnp.clip(i - 5, 0, 1), 0, 0)), like(2, width)),
            (block(width // 2, second), like(6, width // 2)),
            (block(width // 2, second), like(6, width // 2)),
        ]
    outs.append((whole_block((8, 128)), MARK))
    return pl.pallas_call(
        partial(head_grads_two_kernel, wide),
        grid_spec=pltpu.PrefetchScalarGridSpec(
            num_scalar_prefetch=1,
            grid=(10,),
            in_specs=[
                whole_block((1, width, count)),
                whole_block((width, count)),
                pl.BlockSpec((count, cols), at(0, 12)),
                pl.BlockSpec((count, cols), at(12, 4)),
                whole_block(dealt.shape),
                pl.BlockSpec((slots, cols), at(16, 4)),
                whole_block(sinus.shape),
                pl.BlockSpec((count, cols), at(16, 4)),
            ]
            + [whole] * len(more),
            out_specs=[o[0] for o in outs],
        ),
        out_shape=[o[1] for o in outs],
        compiler_params=pltpu.CompilerParams(vmem_limit_bytes=VMEM),
        cost_estimate=OTHER if got is None else OWN,
        name="head_grads_two",
    )(half, left, low, mod_grad, timed_grad, dealt, embed_grad, sinus, first_grad, *more)


def attend_kernel(QB, at_ref, bucket_ref, q_ref, k_ref, v_ref, o_ref, lse_ref):
    length=BUFFER + bucket_ref[at_ref[0]]
    low=lax.broadcasted_iota(jnp.int32,(1,128),1)<64
    bias=jnp.where(lax.broadcasted_iota(jnp.int32,(1,SEQ),1)<length,0.0,-1e30).astype(jnp.float32)
    k=k_ref[...]; v=v_ref[...]
    one=jnp.ones((),v.dtype); zero=jnp.zeros((),v.dtype)
    vs=(jnp.where(low,v,one),jnp.where(low,one,v))
    for b in range(SEQ//QB):
        rows=pl.ds(b*QB,QB)
        q=q_ref[rows,:]
        outs=[];lses=[]
        for h in range(2):
            qh=jnp.where(low,q,zero) if h==0 else jnp.where(low,zero,q)
            s=nt(qh,k)+bias
            top=jnp.max(s,axis=1,keepdims=True)
            p=jnp.exp(s-top).astype(jnp.bfloat16)
            o=nn(p,vs[h])
            total=pltpu.roll(o,64,1)
            outs.append(o/total)
            lses.append(top+jnp.log(total))
        o_ref[rows,:]=jnp.where(low,outs[0],outs[1]).astype(jnp.bfloat16)
        lse_ref[rows,:]=jnp.where(low,lses[0],lses[1])

def attend(at,bucket,joint,QB=272):
    spec=lambda off: pl.BlockSpec((SEQ,128),lambda i,off=off:(0,i+off))
    return pl.pallas_call(partial(attend_kernel,QB),
        grid=(PAIRS,),
        in_specs=[smem(),smem(),spec(0),spec(6),spec(12)],
        out_specs=[spec(0),spec(0)],
        out_shape=[jax.ShapeDtypeStruct((SEQ,D),jnp.bfloat16),jax.ShapeDtypeStruct((SEQ,D),jnp.float32)],
        compiler_params=pltpu.CompilerParams(vmem_limit_bytes=VMEM),
        cost_estimate=OTHER,
        name='attend')(at,bucket,joint,joint,joint)

def attend_back_kernel(KB, at_ref, bucket_ref,q_ref,k_ref,v_ref,do_ref,o_ref,lse_ref,grads_ref,ds_ref):
    length=BUFFER + bucket_ref[at_ref[0]]
    low=lax.broadcasted_iota(jnp.int32,(1,128),1)<64
    q=q_ref[...]; do=do_ref[...]
    zero=jnp.zeros((),q.dtype)
    prod=do.astype(jnp.float32)*o_ref[...].astype(jnp.float32)
    prodT=prod.T
    lseT=lse_ref[...].T
    deltas=(jnp.sum(prodT[:64],axis=0,keepdims=True),jnp.sum(prodT[64:],axis=0,keepdims=True))
    lses=(lseT[0:1],lseT[64:65])
    for b in range(SEQ//KB):
        rows=pl.ds(b*KB,KB)
        k=k_ref[rows,:]; v=v_ref[rows,:]
        bias=jnp.where(lax.broadcasted_iota(jnp.int32,(KB,1),0)+b*KB<length,0.0,-1e30).astype(jnp.float32)
        dks=[];dvs=[]
        for h in range(2):
            pick=(lambda a: jnp.where(low,a,zero)) if h==0 else (lambda a: jnp.where(low,zero,a))
            s=nt(pick(k),q)+bias
            p=jnp.exp(s-lses[h])
            dp=nt(pick(v),do)
            ds=(p*(dp-deltas[h])).astype(jnp.bfloat16)
            dvs.append(nn(p.astype(jnp.bfloat16),do))
            dks.append(nn(ds,q))
            ds_ref[h,rows,:]=ds
        grads_ref[1,rows,:]=jnp.where(low,dks[0],dks[1]).astype(jnp.bfloat16)
        grads_ref[2,rows,:]=jnp.where(low,dvs[0],dvs[1]).astype(jnp.bfloat16)
    kT=k_ref[...].astype(jnp.float32).T.astype(jnp.bfloat16)
    dqT=jnp.concatenate([nn(kT[64*h:64*h+64],ds_ref[h]) for h in range(2)],axis=0)
    grads_ref[0]=(dqT.T*0.125).astype(jnp.bfloat16)

def attend_back(first,count,at,bucket,joint,do,o,lse,KB=544):
    spec=lambda off: pl.BlockSpec((SEQ,128),lambda i,off=off:(0,i+off))
    return pl.pallas_call(partial(attend_back_kernel,KB),
        grid=(count,),
        in_specs=[smem(),smem(),spec(first),spec(6+first),spec(12+first),spec(first),spec(first),spec(first)],
        out_specs=pl.BlockSpec((3,SEQ,128),lambda i:(0,0,i)),
        out_shape=jax.ShapeDtypeStruct((3,SEQ,count*128),jnp.bfloat16),
        scratch_shapes=[pltpu.VMEM((2,SEQ,SEQ),jnp.bfloat16)],
        compiler_params=pltpu.CompilerParams(vmem_limit_bytes=VMEM),
        cost_estimate=OWN,
        name="attend_back")(at,bucket,joint,joint,joint,do,o,lse)


def line(ref):
    return ref[...].reshape(1, ref.shape[0])


def smem():
    return pl.BlockSpec(memory_space=pltpu.SMEM)


def place_kernel(wide, at_ref, bucket_ref, start_ref, chosen_ref, latent_ref, spot_ref, live_ref, dealt_ref):
    image, place_wide, place_narrow, narrow = at_ref[0], at_ref[1], at_ref[2], at_ref[3]
    seq = chosen_ref.shape[1]
    slots = live_ref.shape[1]
    shift = wide.bit_length() - 1
    deep = slots // wide
    deep_shift = deep.bit_length() - 1
    row = lax.broadcasted_iota(jnp.int32, (seq, seq), 0)
    column = lax.broadcasted_iota(jnp.int32, (seq, seq), 1)
    lower = (column <= row).astype(jnp.float32).astype(jnp.bfloat16)
    chosen = jnp.broadcast_to(chosen_ref[...], (8, seq)).astype(jnp.float32).astype(jnp.bfloat16)
    counted = nt(lower, chosen)
    first_row = lax.broadcasted_iota(jnp.int32, counted.shape, 0) == 0
    before = jnp.where(first_row, 0.0, pltpu.roll(counted, 1, 0))
    is_chosen = (counted - before)[:, :1] > 0.5
    order = counted[:, :1].astype(jnp.int32) - 1
    target = ((start_ref[image] + order) & (wide - 1)) * deep + (order >> shift)
    target = jnp.where(is_chosen, target, -1)
    slot = lax.broadcasted_iota(jnp.int32, (seq, slots), 1)
    spot = (slot == target).astype(jnp.float32).astype(jnp.bfloat16)
    spot_ref[...] = spot
    dealt_ref[...] = nn(latent_ref[...], spot).T.astype(jnp.bfloat16)
    lane = lax.broadcasted_iota(jnp.int32, (1, slots), 1)
    live = jnp.zeros((1, slots), jnp.float32)
    for source in range(wide):
        other = source * narrow + place_narrow
        count = bucket_ref[other] * MASK_MAX // IMAGE_MAX
        rank = (place_wide - start_ref[other]) & (wide - 1)
        arrived = jnp.maximum((count - rank + wide - 1) >> shift, 0)
        inside = ((lane >> deep_shift) == source) & ((lane & (deep - 1)) < arrived)
        live = jnp.where(inside, 1.0, live)
    live_ref[...] = live


def places(at, bucket, deal_start, masked, latents, wide):
    seq = masked.shape[1]
    return pl.pallas_call(
        partial(place_kernel, wide),
        in_specs=[smem(), smem(), smem(), whole_block((1, seq)), whole_block((TOKEN_DIM, seq))],
        out_specs=[
            whole_block((seq, MASK_MAX)),
            whole_block((1, MASK_MAX)),
            whole_block((MASK_MAX, TOKEN_DIM)),
        ],
        grid=(1,),
        out_shape=[
            jax.ShapeDtypeStruct((seq, MASK_MAX), jnp.bfloat16),
            jax.ShapeDtypeStruct((1, MASK_MAX), jnp.float32),
            jax.ShapeDtypeStruct((MASK_MAX, TOKEN_DIM), jnp.bfloat16),
        ],
        compiler_params=pltpu.CompilerParams(vmem_limit_bytes=VMEM),
        cost_estimate=OTHER,
        name="places",
    )(at, bucket, deal_start, masked, latents)


def joint_kernel(tokens_ref, gain_ref, shift_ref, weight_ref, bias_ref, first_ref, joint_ref):
    normed, unused = normalize(tokens_ref[...].astype(jnp.float32))
    first = (normed * line(gain_ref) + line(shift_ref)).astype(jnp.bfloat16)
    first_ref[...] = first
    for part in range(3):
        cols = slice(part * D, (part + 1) * D)
        out = nn(first, weight_ref[:, cols])
        if part != 1:
            out = out + line(bias_ref)[:, part // 2 * D : part // 2 * D + D]
        out = out.astype(jnp.bfloat16)
        if part == 0:
            out = out * jnp.bfloat16(HEAD_DIM ** (-0.5))
        joint_ref[:, cols] = out


ROWS = 272


def by_block(columns):
    return pl.BlockSpec((ROWS, columns), lambda i: (i, 0))


def joint_pass(tokens, gain, shift, weight, bias):
    seq = tokens.shape[0]
    return pl.pallas_call(
        joint_kernel,
        grid=(seq // ROWS,),
        in_specs=[by_block(D)] + [whole_block(a.shape) for a in (gain, shift, weight, bias)],
        out_specs=[by_block(D), by_block(3 * D)],
        out_shape=[
            jax.ShapeDtypeStruct((seq, D), jnp.bfloat16),
            jax.ShapeDtypeStruct((seq, 3 * D), jnp.bfloat16),
        ],
        compiler_params=pltpu.CompilerParams(vmem_limit_bytes=VMEM),
        cost_estimate=OTHER,
        name="joint_pass",
    )(tokens, gain, shift, weight, bias)


def gelu_parts(value):
    size = jnp.abs(value)
    bell = jnp.exp(-0.5 * value * value)
    step = 1.0 / (1.0 + (0.3275911 * math.sqrt(0.5)) * size)
    tail = 0.5 * 1.061405429 * step - 0.5 * 1.453152027
    tail = tail * step + 0.5 * 1.421413741
    tail = tail * step - 0.5 * 0.284496736
    tail = tail * step + 0.5 * 0.254829592
    tail = tail * step * bell
    return jnp.where(value < 0.0, tail, 1.0 - tail), bell * (1.0 / math.sqrt(2.0 * math.pi))


def keep_column(at_ref, bucket_ref, rows):
    position = lax.broadcasted_iota(jnp.int32, (rows, 1), 0) + pl.program_id(0) * rows
    return (position < BUFFER + bucket_ref[at_ref[0]]).astype(jnp.float32)


def feed_kernel(
    at_ref,
    bucket_ref,
    mixed_ref,
    tokens_ref,
    latent_ref,
    spot_ref,
    out_w_ref,
    out_b_ref,
    gain_ref,
    shift_ref,
    expand_ref,
    expand_b_ref,
    reduce_ref,
    reduce_b_ref,
    output_ref,
    middle_ref,
    second_ref,
    active_ref,
    slope_ref,
    dealt_ref,
    spread_ref,
    dealt_scratch,
    spread_scratch,
):
    step = pl.program_id(0)

    @pl.when(step == 0)
    def _():
        dealt_scratch[...] = jnp.zeros_like(dealt_scratch)
        spread_scratch[...] = jnp.zeros_like(spread_scratch)

    keep = keep_column(at_ref, bucket_ref, mixed_ref.shape[0])
    branch = nn(mixed_ref[...], out_w_ref[...]) + line(out_b_ref)
    middle = tokens_ref[...].astype(jnp.float32) + branch
    middle_ref[...] = middle
    normed, unused = normalize(middle)
    second = (normed * line(gain_ref) + line(shift_ref)).astype(jnp.bfloat16)
    second_ref[...] = second
    hidden_width = expand_ref.shape[1]
    expand_b = line(expand_b_ref)
    feed = line(reduce_b_ref)
    for part in range(hidden_width // D):
        cols = slice(part * D, (part + 1) * D)
        hidden = nn(second, expand_ref[:, cols]) + expand_b[:, cols]
        phi, density = gelu_parts(hidden)
        active = (hidden * phi).astype(jnp.bfloat16)
        active_ref[:, cols] = active
        slope_ref[:, cols] = (phi + hidden * density).astype(jnp.bfloat16)
        feed = feed + nn(active, reduce_ref[cols, :])
    output = ((middle + feed) * keep).astype(jnp.bfloat16)
    output_ref[...] = output
    spread_scratch[0:1, :] += jnp.sum(keep * branch * branch, axis=0, keepdims=True)
    spread_scratch[1:2, :] += jnp.sum(keep * feed * feed, axis=0, keepdims=True)
    spot = spot_ref[...]
    dealt_scratch[:, :D] += tn(spot, output)

    @pl.when(step == pl.num_programs(0) - 1)
    def _():
        dealt_scratch[:, D : D + TOKEN_DIM] = latent_ref[...].astype(jnp.float32)
        dealt_ref[...] = dealt_scratch[...].astype(jnp.bfloat16)
        count = (BUFFER + bucket_ref[at_ref[0]]).astype(jnp.float32) * D
        total = jnp.sum(spread_scratch[...], axis=1, keepdims=True)
        spread_ref[...] = jnp.sqrt(jnp.broadcast_to(total, spread_ref.shape) / count)


def feed_pass(at, bucket, mixed, tokens, latents, spot, weights):
    seq = tokens.shape[0]
    slots = spot.shape[1]
    hidden = weights[4].shape[1]
    low = lambda *s: jax.ShapeDtypeStruct(s, jnp.bfloat16)
    full = lambda *s: jax.ShapeDtypeStruct(s, jnp.float32)
    return pl.pallas_call(
        feed_kernel,
        grid=(seq // ROWS,),
        in_specs=[smem(), smem(), by_block(D), by_block(D), whole_block((slots, TOKEN_DIM)), by_block(slots)]
        + [whole_block(a.shape) for a in weights],
        out_specs=[
            by_block(D),
            by_block(D),
            by_block(D),
            by_block(hidden),
            by_block(hidden),
            whole_block((slots, D + 128)),
            whole_block((8, 128)),
        ],
        out_shape=[
            low(seq, D),
            full(seq, D),
            low(seq, D),
            low(seq, hidden),
            low(seq, hidden),
            low(slots, D + 128),
            full(8, 128),
        ],
        scratch_shapes=[pltpu.VMEM((slots, D + 128), jnp.float32), pltpu.VMEM((8, D), jnp.float32)],
        compiler_params=pltpu.CompilerParams(vmem_limit_bytes=VMEM),
        cost_estimate=OTHER,
        name="feed_pass",
    )(at, bucket, mixed, tokens, latents, spot, *weights)


def feed_back_kernel(
    at_ref,
    bucket_ref,
    cot_ref,
    spot_ref,
    middle_ref,
    slope_ref,
    returned_ref,
    out_w_ref,
    gain_ref,
    expand_ref,
    reduce_ref,
    feed_grad_ref,
    hidden_grad_ref,
    middle_grad_ref,
    branch_grad_ref,
    mixed_grad_ref,
    sums_ref,
    wide_sum_ref,
):
    @pl.when(pl.program_id(0) == 0)
    def _():
        sums_ref[...] = jnp.zeros_like(sums_ref)
        wide_sum_ref[...] = jnp.zeros_like(wide_sum_ref)

    def add_sum(row, value):
        sums_ref[row : row + 1, :] += jnp.sum(value, axis=0, keepdims=True)

    keep = keep_column(at_ref, bucket_ref, cot_ref.shape[0])
    grad = (cot_ref[...].astype(jnp.float32) + nn(spot_ref[...], returned_ref[...])) * keep
    feed_grad = grad.astype(jnp.bfloat16)
    feed_grad_ref[...] = feed_grad
    add_sum(0, feed_grad.astype(jnp.float32))
    second_grad = jnp.zeros(grad.shape, jnp.float32)
    for part in range(expand_ref.shape[1] // D):
        cols = slice(part * D, (part + 1) * D)
        active_grad = nt(feed_grad, reduce_ref[cols, :])
        hidden_grad = (active_grad * slope_ref[:, cols].astype(jnp.float32)).astype(jnp.bfloat16)
        hidden_grad_ref[:, cols] = hidden_grad
        wide_sum_ref[:, cols] += jnp.sum(hidden_grad.astype(jnp.float32), axis=0, keepdims=True)
        second_grad = second_grad + nt(hidden_grad, expand_ref[:, cols])
    normed, inverse = normalize(middle_ref[...])
    add_sum(1, second_grad * normed)
    add_sum(2, second_grad)
    middle_grad = grad + normalize_back(second_grad * line(gain_ref), normed, inverse)
    middle_grad_ref[...] = middle_grad
    branch_grad = middle_grad.astype(jnp.bfloat16)
    branch_grad_ref[...] = branch_grad
    add_sum(3, branch_grad.astype(jnp.float32))
    mixed_grad_ref[...] = nt(branch_grad, out_w_ref[...]).astype(jnp.bfloat16)


def feed_back(at, bucket, cotangent, spot, middle, slope, returned, weights):
    seq = cotangent.shape[0]
    slots = spot.shape[1]
    hidden = slope.shape[1]
    low = lambda *s: jax.ShapeDtypeStruct(s, jnp.bfloat16)
    full = lambda *s: jax.ShapeDtypeStruct(s, jnp.float32)
    return pl.pallas_call(
        feed_back_kernel,
        grid=(seq // ROWS,),
        in_specs=[smem(), smem(), by_block(D), by_block(slots), by_block(D), by_block(hidden)]
        + [whole_block(a.shape) for a in (returned,) + weights],
        out_specs=[
            by_block(D),
            by_block(hidden),
            by_block(D),
            by_block(D),
            by_block(D),
            whole_block((8, D)),
            whole_block((1, hidden)),
        ],
        out_shape=[
            low(seq, D),
            low(seq, hidden),
            full(seq, D),
            low(seq, D),
            low(seq, D),
            full(8, D),
            full(1, hidden),
        ],
        compiler_params=pltpu.CompilerParams(vmem_limit_bytes=VMEM),
        cost_estimate=OTHER,
        name="feed_back",
    )(at, bucket, cotangent, spot, middle, slope, returned, *weights)


def feed_grads_kernel(wide, half_ref, second_ref, hidden_ref, active_ref, grad_ref, *refs):
    step = pl.program_id(0)
    refs[-1][...] = jnp.zeros_like(refs[-1])

    @pl.when(step < 2)
    def _():
        grad = tn(second_ref[...], hidden_ref[...])
        if len(refs) == 3:
            refs[0][0] = grad.astype(jnp.bfloat16)
        else:
            grad = (grad + refs[0][0].astype(jnp.float32)).astype(jnp.bfloat16)

            @pl.when(step == 0)
            def _():
                refs[2][...] = grad[None]

            @pl.when(step == 1)
            def _():
                refs[3][...] = grad[None]

    @pl.when(step >= 2)
    def _():
        whole = tn(active_ref[...], grad_ref[...])
        pieces = 4
        rows = D // wide
        places = whole.shape[0] // (pieces * rows)
        whole = whole.reshape(places, pieces, rows, D // 2)
        for piece in range(pieces):
            at = (piece // 2, slice(None), slice(piece % 2 * (D // 2), (piece % 2 + 1) * (D // 2)))
            part = whole[:, piece].reshape(places * rows, D // 2)
            if len(refs) == 3:
                refs[1][at] = part.astype(jnp.bfloat16)
            else:
                part = part + refs[1][at].astype(jnp.float32)
                refs[4][at], refs[5][at] = split_rows(part, places, half_ref[2])


def feed_grads(half, second, hidden_grad, active, feed_grad, wide, got=None):
    seq, hidden = active.shape
    chunk = lambda i: jnp.maximum(i - 2, 0)
    turned = lambda i, half: jnp.minimum(i, 1) ^ (1 - half[1])
    low = lambda *s: jax.ShapeDtypeStruct(s, jnp.bfloat16)
    expand_tile = pl.BlockSpec((1, D, D), lambda i, half: (turned(i, half), 0, 0))
    rows_of = lambda rows: pl.BlockSpec((2, rows, D), lambda i, half: (0, chunk(i), 0))
    if got is None:
        more = ()
        outs = [(expand_tile, low(2, D, D)), (rows_of(D // 4), low(2, D, D))]
    else:
        more = tuple(got)
        outs = [(whole_block((1, D, D)), low(1, D, D))] * 2
        outs += [(rows_of(D // 8), low(2, D // 2, D))] * 2
    outs.append((whole_block((8, 128)), MARK))
    return pl.pallas_call(
        partial(feed_grads_kernel, wide),
        grid_spec=pltpu.PrefetchScalarGridSpec(
            num_scalar_prefetch=1,
            grid=(6,),
            in_specs=[
                whole_block((seq, D)),
                pl.BlockSpec((seq, D), lambda i, half: (0, half[0] * 2 + turned(i, half))),
                pl.BlockSpec((seq, D), lambda i, half: (0, chunk(i))),
                pl.BlockSpec((seq, D // 2), lambda i, half: (0, half[0])),
            ]
            + [expand_tile, rows_of(D // 4)][: len(more)],
            out_specs=[o[0] for o in outs],
        ),
        out_shape=[o[1] for o in outs],
        compiler_params=pltpu.CompilerParams(vmem_limit_bytes=VMEM),
        cost_estimate=OTHER if got is None else OWN,
        name="feed_grads",
    )(half, second, hidden_grad, active, feed_grad, *more)


def last_kind(turn, half):
    return (turn // 2 ^ (1 - half[0])) * 2 + turn % 2


def last_grads_kernel(
    half_ref, first_ref, mixed_ref, a_ref, b_ref, c_ref, branch_ref, sent_ref, kept_ref, mark_ref
):
    turn = pl.program_id(0)
    kind = last_kind(turn, half_ref)
    mark_ref[...] = jnp.zeros_like(mark_ref)

    def put(whole):
        whole = whole.astype(jnp.bfloat16)

        @pl.when(turn < 2)
        def _():
            for i in range(6):
                sent_ref[i] = whole[:, i * 128 : (i + 1) * 128]

        @pl.when(turn >= 2)
        def _():
            for i in range(6):
                kept_ref[i] = whole[:, i * 128 : (i + 1) * 128]

    @pl.when(kind < 3)
    def _():
        put(tn(first_ref[...], jnp.concatenate([a_ref[0], b_ref[0], c_ref[0]], axis=1)))

    @pl.when(kind == 3)
    def _():
        put(tn(mixed_ref[...], branch_ref[...]))


def last_grads(half, first_in, mixed, parts, branch_grad):
    seq = mixed.shape[0]
    part = lambda a: pl.BlockSpec(
        (1,) + a.shape[1:], lambda i, half: (jnp.minimum(last_kind(i, half), 2), 0, 0)
    )
    tiles = jax.ShapeDtypeStruct((12, D, 128), jnp.bfloat16)
    return pl.pallas_call(
        last_grads_kernel,
        grid_spec=pltpu.PrefetchScalarGridSpec(
            num_scalar_prefetch=1,
            grid=(4,),
            in_specs=[whole_block((seq, D)), whole_block((seq, D))]
            + [part(a) for a in parts]
            + [whole_block((seq, D))],
            out_specs=[
                pl.BlockSpec((6, D, 128), lambda i, half: (jnp.minimum(i, 1), 0, 0)),
                pl.BlockSpec((6, D, 128), lambda i, half: (jnp.maximum(i - 2, 0), 0, 0)),
                whole_block((8, 128)),
            ],
        ),
        out_shape=[tiles, tiles, MARK],
        compiler_params=pltpu.CompilerParams(vmem_limit_bytes=VMEM),
        cost_estimate=OTHER,
        name="last_grads",
    )(half, first_in, mixed, *parts, branch_grad)


def tokens_back_kernel(
    tokens_ref, a_ref, b_ref, c_ref, middle_ref, gain_ref, weight_ref, out_ref, packed_ref, sums_ref
):
    @pl.when(pl.program_id(0) == 0)
    def _():
        sums_ref[...] = jnp.zeros_like(sums_ref)

    def add_sum(row, value):
        sums_ref[row : row + 1, :] += jnp.sum(value, axis=0, keepdims=True)

    query, keys, value = [
        jnp.concatenate([a_ref[i], b_ref[i], c_ref[i]], axis=1) for i in range(3)
    ]
    grad = nt(query, weight_ref[:, :D])
    grad = grad + nt(keys, weight_ref[:, D : 2 * D])
    grad = grad + nt(value, weight_ref[:, 2 * D :])
    normed, inverse = normalize(tokens_ref[...].astype(jnp.float32))
    add_sum(0, grad * normed)
    add_sum(1, grad)
    add_sum(2, query.astype(jnp.float32))
    add_sum(3, value.astype(jnp.float32))
    out_ref[...] = middle_ref[...] + normalize_back(grad * line(gain_ref), normed, inverse)

    @pl.when(pl.program_id(0) == pl.num_programs(0) - 1)
    def _():
        wide = packed_ref.shape[0]
        part = D // wide
        for w in range(wide):
            packed_ref[w : w + 1, :part] = sums_ref[0:1, w * part : (w + 1) * part]
            packed_ref[w : w + 1, part : 2 * part] = sums_ref[1:2, w * part : (w + 1) * part]
            bias_row = 2 + w * 2 // wide
            at = w % (wide // 2) * 2 * part
            packed_ref[w : w + 1, 2 * part :] = sums_ref[bias_row : bias_row + 1, at : at + 2 * part]


def tokens_back(tokens, parts, middle_grad, gain, weight, wide):
    seq = tokens.shape[0]
    return pl.pallas_call(
        tokens_back_kernel,
        grid=(seq // ROWS,),
        in_specs=[by_block(D)]
        + [pl.BlockSpec((3, ROWS, a.shape[2]), lambda i: (0, i, 0)) for a in parts]
        + [by_block(D)] + [whole_block(gain.shape), whole_block(weight.shape)],
        out_specs=[by_block(D), whole_block((wide, 4 * D // wide))],
        out_shape=[
            jax.ShapeDtypeStruct((seq, D), jnp.float32),
            jax.ShapeDtypeStruct((wide, 4 * D // wide), jnp.float32),
        ],
        scratch_shapes=[pltpu.VMEM((8, D), jnp.float32)],
        compiler_params=pltpu.CompilerParams(vmem_limit_bytes=VMEM),
        cost_estimate=OTHER,
        name="tokens_back",
    )(tokens, *parts, middle_grad, gain, weight)


def pack_kernel(feed_ref, hidden_ref, input_ref, final_ref, token_ref, *refs):
    low_ref, out_ref = refs[-2:]
    out_ref[...] = jnp.zeros_like(out_ref)
    wide, rows, cols = out_ref.shape
    part = D // wide
    block = input_ref.shape[1] // wide
    for w in range(wide):
        out_ref[w, :TOKEN_DIM, :block] = input_ref[:, w * block : (w + 1) * block]
        out_ref[w, :TOKEN_DIM, block : 2 * block] = final_ref[:, w * block : (w + 1) * block]
        out_ref[w, TOKEN_DIM : TOKEN_DIM + 1, :] = hidden_ref[:, w * cols : (w + 1) * cols]
        out_ref[w, TOKEN_DIM + 2 : TOKEN_DIM + 3, :] = token_ref[w : w + 1, :]
        for i in range(4):
            out_ref[w, TOKEN_DIM + 1 : TOKEN_DIM + 2, i * part : (i + 1) * part] = feed_ref[
                i : i + 1, w * part : (w + 1) * part
            ]
    low_ref[...] = out_ref[...].astype(jnp.bfloat16)


def pack(feed_sums, hidden_sum, input_grad, final_grad, token_packed, marks):
    operands = (feed_sums, hidden_sum, input_grad, final_grad, token_packed)
    wide = token_packed.shape[0]
    shape = (wide, TOKEN_DIM + 16, hidden_sum.shape[1] // wide)
    return pl.pallas_call(
        pack_kernel,
        grid=(1,),
        in_specs=[whole_block(a.shape) for a in operands] + [pl.BlockSpec(memory_space=pl.ANY)] * len(marks),
        out_specs=whole_block(shape),
        out_shape=jax.ShapeDtypeStruct(shape, jnp.bfloat16),
        scratch_shapes=[pltpu.VMEM(shape, jnp.float32)],
        cost_estimate=OTHER,
        name="pack",
    )(*operands, *marks)


def add_up(terms):
    total = terms[0].astype(jnp.float32)
    for term in terms[1:]:
        total = total + term.astype(jnp.float32)
    return total


def swap(array, axis, mask):
    count = lax.axis_size(axis)
    return lax.ppermute(array, axis, [(i, i ^ mask) for i in range(count)])


def bit(axis, mask):
    return lax.axis_index(axis) // mask % 2


def pick(array, index, axis):
    return lax.dynamic_index_in_dim(array, index, axis, keepdims=False)


class Order:
    def __init__(self):
        self.mark = ()
        self.marks = ()

    def __call__(self, *values):
        out = lax.optimization_barrier(values + self.mark)[: len(values)]
        return out if len(values) > 1 else out[0]

    def at(self, *values):
        self.mark = values


def bits():
    return jnp.stack([bit("narrow", 1), bit("narrow", 2), bit("wide", 1)]).astype(jnp.int32)


class Flow:
    AXES = {"x": ("narrow", 2), "y": ("wide", 1)}

    def __init__(self, order, lanes, sends=None):
        self.order = order
        self.wide = lax.axis_size("wide").bit_length() - 1
        self.lanes = [[list(terms), tuple(left)] for terms, left in lanes]
        self.steps = self.run(sends)

    def step(self):
        next(self.steps)

    def take(self):
        got = self.order(*self.got)
        return got if isinstance(got, (tuple, list)) else (got,)

    def send(self, *sends):
        self.got = tuple(swap(*s) for s in sends)
        self.order.at(*[s[0] for s in sends])

    def shaped(self, array, left):
        dims = (2,) * (self.wide - ("y" not in left))
        if "x" in left:
            return array.reshape((2, array.shape[0] // 2) + dims + (-1, array.shape[2]))
        return array.reshape((array.shape[0],) + dims + (-1, array.shape[2]))

    def exchange(self, lane, goal):
        terms, left = lane
        dim = 0 if goal == "x" else self.wide + ("x" in left)
        mine = bit(*self.AXES[goal])
        sent = add_up([pick(t, 1 - mine, dim) for t in terms]).astype(jnp.bfloat16)
        lane[0] = [pick(t, mine, dim) for t in terms]
        lane[1] = tuple(n for n in left if n != goal)
        return (sent,) + self.AXES[goal]

    def run(self, sends):
        if sends is not None:
            shapes = [lane[0][0].shape for lane in self.lanes]
            self.send(*sends)
            yield
            got = self.take()
            for lane, g, shape in zip(self.lanes, got, shapes):
                lane[0].append(g.reshape(shape))
        while any(lane[1] for lane in self.lanes):
            self.send(*[self.exchange(lane, lane[1][0]) for lane in self.lanes])
            yield
            for lane, got in zip(self.lanes, self.take()):
                lane[0].append(got)
        parts = [lane[0] for lane in self.lanes]
        both = []
        for b in reversed(range(1, self.wide)):
            mask = 1 << b
            mine = bit("wide", mask)
            sent = [add_up([pick(t, 1 - mine, 1) for t in terms]) for terms in parts]
            sent = [jnp.concatenate(sent, axis=0)] + [pick(t, 1 - mine, 1) for t in both]
            parts = [[pick(t, mine, 1) for t in terms] for terms in parts]
            both = [pick(t, mine, 1) for t in both]
            self.send((add_up(sent).astype(jnp.bfloat16), "wide", mask))
            yield
            both.append(self.take()[0])
        own = jnp.concatenate([add_up(terms) for terms in parts], axis=0)
        share = add_up([own] + both).astype(jnp.bfloat16)
        self.send((share, "narrow", 2))
        yield
        (other,) = self.take()
        share = self.order(share)
        self.send((share, "narrow", 1), (other, "narrow", 1))
        yield
        self.result = (share, other) + tuple(self.take())
        yield

    def finish(self):
        for unused in self.steps:
            pass
        return self.result


class Halves:
    def __init__(self, order, sent):
        *sent, mark = sent
        self.order = order
        self.flight = tuple(swap(a, "narrow", 1) for a in sent)
        order.at(mark)
        order.marks += (mark,)

    def got(self):
        got = self.order(*self.flight)
        return tuple(got) if isinstance(got, (tuple, list)) else (got,)


def unpack_kernel(put, bits_ref, *refs):
    shares, outs = refs[:4], refs[4:]
    core, x = bits_ref[0], bits_ref[1]
    for c in range(2):
        for k in range(2):
            same_x, same_core = x == k, core == c
            for t in range(shares[0].shape[0]):
                one, two, three, four = [s[t].astype(jnp.float32) for s in shares]
                near = jnp.where(same_x, one, two)
                far = jnp.where(same_x, three, four)
                put(outs, c, k, t, jnp.where(same_core, near, far))


def unpack(put, shares, shapes):
    return pl.pallas_call(
        partial(unpack_kernel, put),
        grid=(1,),
        in_specs=[smem()] + [whole_block(a.shape) for a in shares],
        out_specs=[whole_block(s) for s in shapes],
        out_shape=[jax.ShapeDtypeStruct(s, jnp.float32) for s in shapes],
        compiler_params=pltpu.CompilerParams(vmem_limit_bytes=VMEM),
        cost_estimate=OTHER,
        name="unpack",
    )(bits(), *shares)


def put_columns(spans, tiles):
    def put(outs, c, x, t, value):
        column = (c * 2 + x) * tiles + t
        for out_ref, (first, stop) in zip(outs, spans):
            if first <= column < stop:
                at = (column - first) * value.shape[1]
                out_ref[:, at : at + value.shape[1]] = value

    return put


def small_steps(order, rows):
    def send(*sends):
        order.at(*[s[0] for s in sends])
        return [swap(*s) for s in sends]

    wide = lax.axis_size("wide")
    low = rows.astype(jnp.bfloat16)
    for mask in (1, 2):
        (got,) = send((low, "narrow", mask))
        yield
        low = add_up([low, order(got)]).astype(jnp.bfloat16)
    low = low.reshape((wide // 2, 2) + low.shape[1:])
    mine = bit("wide", 1)
    (got,) = send((pick(low, 1 - mine, 1), "wide", 1))
    yield
    low = add_up([pick(low, mine, 1), order(got)]).astype(jnp.bfloat16)
    place = lax.axis_index("wide") // 2
    got = send(*[(pick(low, place ^ (m // 2), 0), "wide", m) for m in range(2, wide, 2)])
    yield
    yield add_up([pick(low, place, 0)] + list(order(*got)))


def shards(
    tokens,
    cotangent,
    latents,
    added_noise,
    timesteps,
    bucket,
    masked,
    deal_start,
    first_gain,
    first_shift,
    joint_weight,
    query_value_bias,
    output_weight,
    output_bias,
    second_gain,
    second_shift,
    expand_weight,
    expand_bias,
    reduce_weight,
    reduce_bias,
    input_proj,
    cond_proj,
    time_first,
    time_second,
    block_mod,
    block_expand,
    block_reduce,
    final_mod,
    final_proj,
):
    wide = lax.axis_size("wide")
    narrow = lax.axis_size("narrow")
    place_wide = lax.axis_index("wide")
    place_narrow = lax.axis_index("narrow")
    mine = bits()
    other = mine.at[0].set(1 - mine[0])
    image_index = place_wide * narrow + place_narrow
    at = jnp.stack([image_index, place_wide, place_narrow, jnp.int32(narrow)]).astype(jnp.int32)

    spot, live, dealt_latents = places(at, bucket, deal_start, masked, latents.T, wide)
    slots = spot.shape[1]
    steps = timesteps.astype(jnp.float32)
    half = time_first.shape[0] // 2
    freqs = jnp.exp(-math.log(10000.0) * jnp.arange(half).astype(jnp.float32) / half)
    angles = steps.reshape(-1, 1) * freqs
    sinus = jnp.concatenate([jnp.cos(angles), jnp.sin(angles)], axis=-1).astype(jnp.bfloat16)
    offset = steps * STEP_ANGLE
    keep_sig = jnp.cos(offset + SHIFT_ANGLE) / math.cos(SHIFT_ANGLE)
    drop_sig = jnp.sqrt(jnp.sin(offset) * jnp.sin(offset + 2.0 * SHIFT_ANGLE)) / math.cos(SHIFT_ANGLE)
    input_turned = input_proj.T
    final_turned = final_proj.T

    first_in, joint = joint_pass(
        tokens, first_gain, first_shift, joint_weight, query_value_bias
    )
    mixed, logsum = attend(at, bucket, joint)
    block_output, middle, second_in, active, slope, dealt, spread = feed_pass(
        at,
        bucket,
        mixed,
        tokens,
        dealt_latents,
        spot,
        (
            output_weight,
            output_bias,
            second_gain,
            second_shift,
            expand_weight,
            expand_bias,
            reduce_weight,
            reduce_bias,
        ),
    )

    def deal(array):
        shape = array.shape
        return lax.all_to_all(
            array.reshape(wide, -1, shape[1]), "wide", split_axis=0, concat_axis=0, tiled=True
        ).reshape(shape)

    dealt = deal(dealt)
    low_turned, time_slope, timed = time_embedding(sinus, time_first, time_second)
    (
        guess,
        left,
        fin_grad,
        branch_grad,
        upper_grad,
        mod_grad,
        timed_grad,
        embed_grad,
        rows_grad,
        input_grad,
        final_grad,
    ) = head_pass(
        dealt,
        timed,
        keep_sig[:, None, :],
        drop_sig[:, None, :],
        added_noise,
        live,
        (input_turned, cond_proj, block_mod, block_expand, block_reduce, final_mod, final_turned),
    )
    order = Order()
    order.at(rows_grad)
    returned = deal(rows_grad)
    first_grad = time_back(order(timed_grad), time_second, time_slope)
    order.at(first_grad)
    one_args = (fin_grad, branch_grad, upper_grad)
    halves_one = Halves(order, head_grads_one(other, order(left), *one_args))
    two_args = (mod_grad, timed_grad, dealt, embed_grad, sinus, first_grad, wide)
    halves_two = Halves(order, head_grads_two(other, left, order(low_turned), *two_args))
    returned = order(returned)
    order.at(returned, *order.mark)

    def note(mark):
        order.marks += (mark,)
        order.at(mark)

    sent, kept, mark = head_grads_one(mine, order(left), *one_args, *halves_one.got())
    note(mark)
    shape = lambda a: a.reshape((a.shape[0],) + (2,) * (wide.bit_length() - 1) + (-1, a.shape[2]))
    half_shape = lambda a: a.reshape(
        (2, a.shape[0] // 2) + (2,) * (wide.bit_length() - 2) + (-1, a.shape[2])
    )
    one = Flow(order, [([shape(kept)], ("y",))], [(sent, "narrow", 2)])
    one.step()
    order.at(mark)
    sent_a, kept_a, sent_b, kept_b, mark = head_grads_two(
        mine, left, order(low_turned), *two_args, *halves_two.got()
    )
    note(mark)
    two = Flow(
        order,
        [([shape(kept_a)], ("y",)), ([half_shape(kept_b)], ("x",))],
        [(sent_a, "narrow", 2), (sent_b, "wide", 1)],
    )
    two.step()
    order.at(mark)
    feed_grad, hidden_grad, middle_grad, out_grad, mixed_grad, feed_sums, hidden_sum = feed_back(
        at,
        bucket,
        order(cotangent),
        spot,
        middle,
        slope,
        returned,
        (output_weight, second_gain, expand_weight, reduce_weight),
    )
    order.at(mixed_grad)
    feed_args = (hidden_grad, active, feed_grad, wide)
    halves_feed = Halves(order, feed_grads(other, order(second_in), *feed_args))
    one.step()
    parts = []

    def attend_back_part(i):
        grads = attend_back(2 * i, 2, at, bucket, joint, order(mixed_grad), mixed, logsum)
        order.at(grads)
        parts.append(grads)

    attend_back_part(0)
    two.step()
    sent_e, kept_e, sent_r, kept_r, mark = feed_grads(
        mine, order(second_in), *feed_args, halves_feed.got()
    )
    note(mark)
    feed = Flow(
        order,
        [([shape(kept_e)], ("y",)), ([half_shape(kept_r)], ("x",))],
        [(sent_e, "narrow", 2), (sent_r, "wide", 1)],
    )
    feed.step()
    order.at(mark)
    one.step()
    attend_back_part(1)
    two.step()
    one.step()
    feed.step()
    attend_back_part(2)
    feed.step()
    two.step()
    one.step()
    sent, own, mark = last_grads(mine, order(first_in), mixed, parts, out_grad)
    halves_last = Halves(order, (sent, mark))
    terms = [
        a.reshape((2, 6) + (2,) * (wide.bit_length() - 1) + (-1, 128)) for a in (own,) + halves_last.got()
    ]
    last = Flow(
        order, [([a[:, :3] for a in terms], ("x", "y")), ([a[:, 3:] for a in terms], ("y", "x"))]
    )
    last.step()
    tokens_gradient, token_packed = tokens_back(
        order(tokens), parts, middle_grad, first_gain, joint_weight, wide
    )
    order.at(token_packed)
    width = cond_proj.shape[1]
    rows = width // wide
    cut = cond_proj.shape[0] // wide

    def hold(outs):
        order.at(*outs)
        return outs

    last.step()
    two.step()
    feed.step()
    one.step()
    packed = pack(feed_sums, hidden_sum, input_grad, final_grad, order(token_packed), order.marks)
    order.at(packed)
    small = small_steps(order, packed)
    next(small)
    last.step()
    next(small)
    one = one.finish()
    final_mod_out, block_reduce_out, block_expand_out = hold(
        unpack(
            put_columns(((0, 4), (4, 6), (6, 8)), 2),
            (order(one[0]),) + one[1:],
            ((rows, 2 * width), (rows, width), (rows, width)),
        )
    )
    two.step()
    feed.step()
    two = two.finish()

    def put_two(outs, c, x, t, value):
        column = (c * 2 + x) * 5 + t
        if column < 16:
            put_columns(((0, 12), (12, 16)), 5)(outs, c, x, t, value)
        else:
            cols = slice((column - 16) * 256, (column - 15) * 256)
            outs[2][:, cols] = value[:cut]
            outs[3][:, cols] = value[cut:]

    block_mod_out, time_second_out, cond_out, time_first_out = hold(
        unpack(
            put_two,
            (order(two[0]),) + two[1:],
            ((rows, 3 * width), (rows, width), (cut, width), (rows - cut, width)),
        )
    )
    last.step()
    next(small)
    feed.step()
    feed = feed.finish()

    def put_feed(outs, c, x, t, value):
        if t == 0:
            at = (c * 2 + x) * D
            outs[0][:, at : at + D] = value
        else:
            for i in range(2):
                piece = x * 2 + i
                outs[1][piece * cut : (piece + 1) * cut, c * (D // 2) : (c + 1) * (D // 2)] = value[
                    :, i * (D // 2) : (i + 1) * (D // 2)
                ]

    last.step()
    next(small)
    expand_out, reduce_out = hold(
        unpack(put_feed, (order(feed[0]),) + feed[1:], ((cut, 4 * D), (4 * cut, D)))
    )
    last.step()
    small = next(small)
    last = last.finish()
    joint_out, output_out = unpack(
        put_columns(((0, 18), (18, 24)), 6), last, ((cut, 3 * D), (cut, D))
    )
    part = D // wide
    block = input_grad.shape[1] // wide
    vectors = [small[TOKEN_DIM + 1, i * part : (i + 1) * part] for i in range(4)]
    input_out = small[:TOKEN_DIM, :block].T
    final_out = small[:TOKEN_DIM, block : 2 * block].T
    late = small[TOKEN_DIM + 2]
    outs = [
        late[:part],
        late[part : 2 * part],
        late[2 * part :],
        vectors[3],
        vectors[1],
        vectors[2],
        small[TOKEN_DIM],
        vectors[0],
        input_out,
        final_out,
    ]
    return (
        block_output,
        guess,
        spread[:2, 0].reshape(1, 2),
        tokens_gradient,
        outs[0],
        outs[1],
        joint_out,
        outs[2],
        output_out,
        outs[3],
        outs[4],
        outs[5],
        expand_out,
        outs[6],
        reduce_out,
        outs[7],
        outs[8],
        cond_out,
        time_first_out,
        time_second_out,
        block_mod_out,
        block_expand_out,
        block_reduce_out,
        final_mod_out,
        outs[9],
    )


def solution(mesh):
    in_specs = (
        P(("wide", "narrow"), None),
        P(("wide", "narrow"), None),
        P(("wide", "narrow"), None),
        P(None, None, ("wide", "narrow")),
        P(None, ("wide", "narrow")),
        P(),
        P(("wide", "narrow"), None),
        P(),
        P(),
        P(),
        P(),
        P(),
        P(),
        P(),
        P(),
        P(),
        P(),
        P(),
        P(),
        P(),
        P(),
        P(),
        P(),
        P(),
        P(),
        P(),
        P(),
        P(),
        P(),
    )
    out_specs = (
        P(("wide", "narrow"), None),
        P(None, None, ("wide", "narrow")),
        P(("wide", "narrow"), None),
        P(("wide", "narrow"), None),
        P("wide"),
        P("wide"),
        P("wide", None),
        P("wide"),
        P("wide", None),
        P("wide"),
        P("wide"),
        P("wide"),
        P("wide", None),
        P("wide"),
        P("wide", None),
        P("wide"),
        P("wide", None),
        P("wide", None),
        P("wide", None),
        P("wide", None),
        P("wide", None),
        P("wide", None),
        P("wide", None),
        P("wide", None),
        P("wide", None),
    )
    return jax.shard_map(shards, mesh=mesh, in_specs=in_specs, out_specs=out_specs, check_vma=False)
```

```python
from functools import partial
import math

import jax
import jax.numpy as jnp
from jax import lax
from jax.experimental import pallas as pl
from jax.experimental.pallas import tpu as pltpu
from jax.sharding import PartitionSpec as P

D = 768
HEADS = 12
HEAD_DIM = 64
TOKEN_DIM = 16
BUFFER = 64
IMAGE_MAX = 1024
MASK_MAX = 256
REPEATS = 4
SEQ = 1088


SHIFT_ANGLE = 0.008 / 1.008 * math.pi / 2.0
STEP_ANGLE = math.pi / (2.0 * 1.008 * 1000.0)
PAIRS = 6
VMEM = 60 * 1024 * 1024

OWN = pl.CostEstimate(flops=1 << 40, bytes_accessed=1 << 20, transcendentals=0)
OTHER = pl.CostEstimate(flops=0, bytes_accessed=1 << 20, transcendentals=0)


def nt(a,b): return lax.dot_general(a,b,(((1,),(1,)),((),())),preferred_element_type=jnp.float32)
def nn(a,b): return jnp.dot(a,b,preferred_element_type=jnp.float32)
def tn(a,b): return lax.dot_general(a,b,(((0,),(0,)),((),())),preferred_element_type=jnp.float32)
def normalize(values):
    centre = values - jnp.mean(values, axis=-1, keepdims=True)
    inverse = lax.rsqrt(jnp.mean(centre * centre, axis=-1, keepdims=True) + 1e-06)
    return (centre * inverse, inverse)


def normalize_back(grad_normed, normed, inverse):
    return inverse * (
        grad_normed
        - jnp.mean(grad_normed, axis=-1, keepdims=True)
        - normed * jnp.mean(grad_normed * normed, axis=-1, keepdims=True)
    )


def sigmoid(value):
    return 0.5 * jnp.tanh(0.5 * value) + 0.5


def silu_slope(value, sigma):
    return sigma * (1.0 + value * (1.0 - sigma))


def whole_block(shape):
    zeros = (0,) * len(shape)
    return pl.BlockSpec(shape, lambda *unused: zeros, pipeline_mode=pl.Buffered(1))


def time_kernel(sinus_ref, first_ref, second_ref, low_ref, slope_ref, timed_ref):
    first = nn(sinus_ref[...], first_ref[...])
    sigma = sigmoid(first)
    low = (first * sigma).astype(jnp.bfloat16)
    slope_ref[...] = silu_slope(first, sigma).astype(jnp.bfloat16)
    low_ref[...] = low.T
    timed_ref[...] = nn(low, second_ref[...])


def time_embedding(sinus, time_first, time_second):
    count, freq = sinus.shape
    width = time_first.shape[1]
    rows = count // REPEATS
    by_rows = pl.BlockSpec((rows, width), lambda i: (i, 0))
    return pl.pallas_call(
        time_kernel,
        grid=(REPEATS,),
        in_specs=[
            pl.BlockSpec((rows, freq), lambda i: (i, 0)),
            whole_block(time_first.shape),
            whole_block(time_second.shape),
        ],
        out_specs=[pl.BlockSpec((width, rows), lambda i: (0, i)), by_rows, by_rows],
        out_shape=[
            jax.ShapeDtypeStruct((width, count), jnp.bfloat16),
            jax.ShapeDtypeStruct((count, width), jnp.bfloat16),
            jax.ShapeDtypeStruct((count, width), jnp.float32),
        ],
        compiler_params=pltpu.CompilerParams(vmem_limit_bytes=VMEM),
        cost_estimate=OTHER,
        name="time_embedding",
    )(sinus, time_first, time_second)


def head_kernel(
    dealt_ref,
    timed_ref,
    keep_ref,
    drop_ref,
    noise_ref,
    live_ref,
    input_ref,
    cond_ref,
    mod_ref,
    expand_ref,
    reduce_ref,
    fin_ref,
    final_ref,
    guess_ref,
    left_ref,
    fin_grad_ref,
    branch_grad_ref,
    upper_grad_ref,
    mod_grad_ref,
    timed_grad_ref,
    embed_grad_ref,
    rows_grad_ref,
    input_grad_ref,
    final_grad_ref,
    embed_scratch,
    total_scratch,
):
    turn = pl.program_id(0)
    width = timed_ref.shape[1]

    @pl.when(turn == 0)
    def _():
        embed_scratch[...] = nn(dealt_ref[:, :D], cond_ref[...])
        total_scratch[...] = jnp.zeros_like(total_scratch)
        input_grad_ref[...] = jnp.zeros_like(input_grad_ref)
        final_grad_ref[...] = jnp.zeros_like(final_grad_ref)

    cond = embed_scratch[...] + timed_ref[...]
    acted = (cond * sigmoid(cond)).astype(jnp.bfloat16)
    left_ref[0] = acted.T
    start = dealt_ref[:, D:].astype(jnp.float32).T[:TOKEN_DIM]
    noise = noise_ref[0]
    noisy = (keep_ref[pl.ds(turn, 1), :] * start + drop_ref[pl.ds(turn, 1), :] * noise).astype(jnp.bfloat16)
    entry = tn(noisy, input_ref[...])
    inner_normed, inner_inverse = normalize(entry)
    shift_a = nn(acted, mod_ref[:, :width])
    scale_a = nn(acted, mod_ref[:, width : 2 * width])
    gate_a = nn(acted, mod_ref[:, 2 * width :])
    inner = (inner_normed * (1.0 + scale_a) + shift_a).astype(jnp.bfloat16)
    left_ref[2] = inner.T
    upper = nn(inner, expand_ref[...])
    upper_sigma = sigmoid(upper)
    lifted = (upper * upper_sigma).astype(jnp.bfloat16)
    left_ref[1] = lifted.T
    branch = nn(lifted, reduce_ref[...])
    shift_b = nn(acted, fin_ref[:, :width])
    scale_b = nn(acted, fin_ref[:, width:])
    last_normed, last_inverse = normalize(entry + gate_a * branch)
    last = (last_normed * (1.0 + scale_b) + shift_b).astype(jnp.bfloat16)
    live = live_ref[...]
    guess = nt(final_ref[...], last) * live
    guess_ref[0] = guess
    guess_grad = (2.0 / REPEATS * (guess - noise * live) * live).astype(jnp.bfloat16)
    final_grad_ref[...] += nn(guess_grad, last)
    last_grad = tn(guess_grad, final_ref[...])
    fin_grad = jnp.concatenate([last_grad, last_grad * last_normed], axis=1).astype(jnp.bfloat16)
    fin_grad_ref[...] = fin_grad
    after_grad = normalize_back(last_grad * (1.0 + scale_b), last_normed, last_inverse)
    branch_grad = (after_grad * gate_a).astype(jnp.bfloat16)
    branch_grad_ref[...] = branch_grad
    lifted_grad = nt(branch_grad, reduce_ref[...])
    upper_grad = (lifted_grad * silu_slope(upper, upper_sigma)).astype(jnp.bfloat16)
    upper_grad_ref[...] = upper_grad
    inner_grad = nt(upper_grad, expand_ref[...])
    entry_grad = (
        after_grad + normalize_back(inner_grad * (1.0 + scale_a), inner_normed, inner_inverse)
    ).astype(jnp.bfloat16)
    input_grad_ref[...] += nn(noisy, entry_grad)
    mod_grad = jnp.concatenate(
        [inner_grad, inner_grad * inner_normed, after_grad * branch], axis=1
    ).astype(jnp.bfloat16)
    mod_grad_ref[...] = mod_grad
    acted_grad = nt(mod_grad, mod_ref[...]) + nt(fin_grad, fin_ref[...])
    cond = embed_scratch[...] + timed_ref[...]
    cond_grad = acted_grad * silu_slope(cond, sigmoid(cond))
    timed_grad_ref[...] = cond_grad.astype(jnp.bfloat16)
    total_scratch[...] += cond_grad

    @pl.when(turn == REPEATS - 1)
    def _():
        embed_grad = total_scratch[...].astype(jnp.bfloat16)
        embed_grad_ref[...] = embed_grad
        rows_grad_ref[...] = nt(embed_grad, cond_ref[...]).astype(jnp.bfloat16)


def head_pass(dealt, timed, keep_sig, drop_sig, noise, live, weights):
    input_proj, cond_proj, block_mod, block_expand, block_reduce, final_mod, final_proj = weights
    slots = dealt.shape[0]
    width = cond_proj.shape[1]
    count = REPEATS * slots
    by_rows = lambda n: pl.BlockSpec((slots, n), lambda i: (i, 0))
    by_turn = lambda a: pl.BlockSpec((1,) + a, lambda i: (i, 0, 0))
    low = lambda *s: jax.ShapeDtypeStruct(s, jnp.bfloat16)
    full = lambda *s: jax.ShapeDtypeStruct(s, jnp.float32)
    operands = (
        dealt,
        timed,
        keep_sig,
        drop_sig,
        noise,
        live,
        input_proj,
        cond_proj,
        block_mod,
        block_expand,
        block_reduce,
        final_mod,
        final_proj,
    )
    return pl.pallas_call(
        head_kernel,
        grid=(REPEATS,),
        in_specs=[
            whole_block(dealt.shape),
            by_rows(width),
            whole_block(keep_sig.shape),
            whole_block(drop_sig.shape),
            by_turn((TOKEN_DIM, slots)),
        ]
        + [whole_block(a.shape) for a in operands[5:]],
        out_specs=[
            by_turn((TOKEN_DIM, slots)),
            pl.BlockSpec((3, width, slots), lambda i: (0, 0, i)),
            by_rows(2 * width),
            by_rows(width),
            by_rows(width),
            by_rows(3 * width),
            by_rows(width),
            whole_block((slots, width)),
            whole_block((slots, D)),
            whole_block((TOKEN_DIM, width)),
            whole_block((TOKEN_DIM, width)),
        ],
        out_shape=[
            full(REPEATS, TOKEN_DIM, slots),
            low(3, width, count),
            low(count, 2 * width),
            low(count, width),
            low(count, width),
            low(count, 3 * width),
            low(count, width),
            low(slots, width),
            low(slots, D),
            full(TOKEN_DIM, width),
            full(TOKEN_DIM, width),
        ],
        scratch_shapes=[pltpu.VMEM((slots, width), jnp.float32)] * 2,
        compiler_params=pltpu.CompilerParams(vmem_limit_bytes=VMEM),
        cost_estimate=OTHER,
        name="head_pass",
    )(*operands)


MARK = jax.ShapeDtypeStruct((8, 128), jnp.float32)


def head_grads_one_kernel(half_ref, left_ref, fin_ref, branch_ref, upper_ref, *refs):
    turn = pl.program_id(0)
    tile = head_one_tile(turn, half_ref)

    def put(grad):
        if len(refs) == 2:
            out_ref, mark_ref = refs
            out_ref[0] = grad.astype(jnp.bfloat16)
        else:
            got_ref, sent_ref, kept_ref, mark_ref = refs
            grad = (grad + got_ref[0].astype(jnp.float32)).astype(jnp.bfloat16)

            @pl.when(turn < 2)
            def _():
                sent_ref[0] = grad

            @pl.when(turn >= 2)
            def _():
                kept_ref[0] = grad

        mark_ref[...] = jnp.zeros_like(mark_ref)

    @pl.when(tile < 4)
    def _():
        put(nn(left_ref[0], fin_ref[...]))

    @pl.when((tile >= 4) & (tile < 6))
    def _():
        put(nn(left_ref[0], branch_ref[...]))

    @pl.when(tile >= 6)
    def _():
        put(nn(left_ref[0], upper_ref[...]))


def head_one_tile(turn, half):
    return half[0] * 4 + (turn ^ (2 - 2 * half[1]))


def head_grads_one(half, left, fin_grad, branch_grad, upper_grad, got=None):
    width, count = left.shape[1:]
    cols = width // 2

    def at(first, tiles):
        return lambda i, half: (0, jnp.clip(head_one_tile(i, half) - first, 0, tiles - 1))

    def which(i, half):
        tile = head_one_tile(i, half)
        return (jnp.where(tile < 4, 0, jnp.where(tile < 6, 1, 2)), 0, 0)

    tiles = lambda n: jax.ShapeDtypeStruct((n, width, cols), jnp.bfloat16)
    block = lambda where: pl.BlockSpec((1, width, cols), where)
    if got is None:
        more = ()
        outs = [(block(lambda i, half: (i ^ (2 - 2 * half[1]), 0, 0)), tiles(4))]
    else:
        more = (got,)
        outs = [
            (block(lambda i, half: (jnp.minimum(i, 1), 0, 0)), tiles(2)),
            (block(lambda i, half: (jnp.maximum(i - 2, 0), 0, 0)), tiles(2)),
        ]
    outs.append((whole_block((8, 128)), MARK))
    return pl.pallas_call(
        head_grads_one_kernel,
        grid_spec=pltpu.PrefetchScalarGridSpec(
            num_scalar_prefetch=1,
            grid=(4,),
            in_specs=[
                pl.BlockSpec((1, width, count), which),
                pl.BlockSpec((count, cols), at(0, 4)),
                pl.BlockSpec((count, cols), at(4, 2)),
                pl.BlockSpec((count, cols), at(6, 2)),
            ]
            + [block(lambda i, half: (i ^ (2 - 2 * half[1]), 0, 0))] * len(more),
            out_specs=[o[0] for o in outs],
        ),
        out_shape=[o[1] for o in outs],
        compiler_params=pltpu.CompilerParams(vmem_limit_bytes=VMEM),
        cost_estimate=OTHER if got is None else OWN,
        name="head_grads_one",
    )(half, left, fin_grad, branch_grad, upper_grad, *more)


def time_back_kernel(grad_ref, weight_ref, slope_ref, out_ref):
    grad = nt(grad_ref[...], weight_ref[...])
    out_ref[...] = (grad * slope_ref[...].astype(jnp.float32)).astype(jnp.bfloat16)


def time_back(timed_grad, weight, slope):
    count, width = timed_grad.shape
    by_rows = pl.BlockSpec((count // 4, width), lambda i: (i, 0))
    return pl.pallas_call(
        time_back_kernel,
        grid=(4,),
        in_specs=[by_rows, whole_block(weight.shape), by_rows],
        out_specs=by_rows,
        out_shape=jax.ShapeDtypeStruct((count, width), jnp.bfloat16),
        compiler_params=pltpu.CompilerParams(vmem_limit_bytes=VMEM),
        cost_estimate=OTHER,
        name="time_back",
    )(timed_grad, weight, slope)


def split_rows(grad, wide, y):
    grad = grad.reshape((wide // 2, 2, -1) + grad.shape[1:])
    own, other = jnp.where(y == 0, grad[:, 0], grad[:, 1]), jnp.where(y == 0, grad[:, 1], grad[:, 0])
    flat = lambda a: a.reshape((-1,) + a.shape[2:]).astype(jnp.bfloat16)
    return flat(other), flat(own)


def head_grads_two_kernel(
    wide, half_ref, acted_ref, low_ref, mod_ref, timed_ref, rows_ref, embed_ref, sinus_ref, first_ref, *refs
):
    turn = pl.program_id(0)
    tile = half_ref[0] * 10 + head_two_tile(turn, half_ref)

    def put(grad):
        refs[-1][...] = jnp.zeros_like(refs[-1])
        if len(refs) == 2:
            refs[0][0] = grad.astype(jnp.bfloat16)
            return
        got_ref, sent_one, kept_one, sent_two, kept_two, unused = refs
        grad = grad + got_ref[0].astype(jnp.float32)

        @pl.when(turn < 2)
        def _():
            sent_one[0] = grad.astype(jnp.bfloat16)

        @pl.when((turn >= 5) & (turn < 7))
        def _():
            kept_one[0] = grad.astype(jnp.bfloat16)

        @pl.when(turn % 5 >= 2)
        def _():
            sent_two[0], kept_two[0] = split_rows(grad, wide, half_ref[2])

    @pl.when(tile < 12)
    def _():
        put(nn(acted_ref[0], mod_ref[...]))

    @pl.when((tile >= 12) & (tile < 16))
    def _():
        put(nn(low_ref[...], timed_ref[...]))

    @pl.when(tile >= 16)
    def _():
        cond = tn(rows_ref[:, :D], embed_ref[...])
        time = tn(sinus_ref[...], first_ref[...])
        cols = cond.shape[1]
        both = jnp.concatenate(
            [cond.reshape(wide, -1, cols), time.reshape(wide, -1, cols)], axis=1
        )
        put(both.reshape(-1, cols))


def head_two_tile(turn, half):
    return (turn // 5 ^ (1 - half[1])) * 5 + turn % 5


def head_grads_two(half, left, low, mod_grad, timed_grad, dealt, embed_grad, sinus, first_grad, wide, got=None):
    width, count = left.shape[1:]
    slots = dealt.shape[0]
    cols = width // 4

    def at(first, tiles):
        return lambda i, half: (0, jnp.clip(half[0] * 10 + head_two_tile(i, half) - first, 0, tiles - 1))

    whole = pl.BlockSpec((1, width, cols), lambda i, half: (head_two_tile(i, half), 0, 0))
    like = lambda n, rows: jax.ShapeDtypeStruct((n, rows, cols), jnp.bfloat16)
    if got is None:
        more = ()
        outs = [(whole, like(10, width))]
    else:
        more = (got,)
        block = lambda rows, where: pl.BlockSpec((1, rows, cols), where)

        def second(i, half):
            return ((i // 5 ^ (1 - half[1])) * 3 + jnp.maximum(i % 5 - 2, 0), 0, 0)

        outs = [
            (block(width, lambda i, half: (jnp.minimum(i, 1), 0, 0)), like(2, width)),
            (block(width, lambda i, half: (jnp.clip(i - 5, 0, 1), 0, 0)), like(2, width)),
            (block(width // 2, second), like(6, width // 2)),
            (block(width // 2, second), like(6, width // 2)),
        ]
    outs.append((whole_block((8, 128)), MARK))
    return pl.pallas_call(
        partial(head_grads_two_kernel, wide),
        grid_spec=pltpu.PrefetchScalarGridSpec(
            num_scalar_prefetch=1,
            grid=(10,),
            in_specs=[
                whole_block((1, width, count)),
                whole_block((width, count)),
                pl.BlockSpec((count, cols), at(0, 12)),
                pl.BlockSpec((count, cols), at(12, 4)),
                whole_block(dealt.shape),
                pl.BlockSpec((slots, cols), at(16, 4)),
                whole_block(sinus.shape),
                pl.BlockSpec((count, cols), at(16, 4)),
            ]
            + [whole] * len(more),
            out_specs=[o[0] for o in outs],
        ),
        out_shape=[o[1] for o in outs],
        compiler_params=pltpu.CompilerParams(vmem_limit_bytes=VMEM),
        cost_estimate=OTHER if got is None else OWN,
        name="head_grads_two",
    )(half, left, low, mod_grad, timed_grad, dealt, embed_grad, sinus, first_grad, *more)


def attend_kernel(QB, at_ref, bucket_ref, q_ref, k_ref, v_ref, o_ref, lse_ref):
    length=BUFFER + bucket_ref[at_ref[0]]
    low=lax.broadcasted_iota(jnp.int32,(1,128),1)<64
    bias=jnp.where(lax.broadcasted_iota(jnp.int32,(1,SEQ),1)<length,0.0,-1e30).astype(jnp.float32)
    k=k_ref[...]; v=v_ref[...]
    one=jnp.ones((),v.dtype); zero=jnp.zeros((),v.dtype)
    vs=(jnp.where(low,v,one),jnp.where(low,one,v))
    for b in range(SEQ//QB):
        rows=pl.ds(b*QB,QB)
        q=q_ref[rows,:]
        outs=[];lses=[]
        for h in range(2):
            qh=jnp.where(low,q,zero) if h==0 else jnp.where(low,zero,q)
            s=nt(qh,k)+bias
            top=jnp.max(s,axis=1,keepdims=True)
            p=jnp.exp(s-top).astype(jnp.bfloat16)
            o=nn(p,vs[h])
            total=pltpu.roll(o,64,1)
            outs.append(o/total)
            lses.append(top+jnp.log(total))
        o_ref[rows,:]=jnp.where(low,outs[0],outs[1]).astype(jnp.bfloat16)
        lse_ref[rows,:]=jnp.where(low,lses[0],lses[1])

def attend(at,bucket,joint,QB=272):
    spec=lambda off: pl.BlockSpec((SEQ,128),lambda i,off=off:(0,i+off))
    return pl.pallas_call(partial(attend_kernel,QB),
        grid=(PAIRS,),
        in_specs=[smem(),smem(),spec(0),spec(6),spec(12)],
        out_specs=[spec(0),spec(0)],
        out_shape=[jax.ShapeDtypeStruct((SEQ,D),jnp.bfloat16),jax.ShapeDtypeStruct((SEQ,D),jnp.float32)],
        compiler_params=pltpu.CompilerParams(vmem_limit_bytes=VMEM),
        cost_estimate=OTHER,
        name='attend')(at,bucket,joint,joint,joint)

def attend_back_kernel(KB, at_ref, bucket_ref,q_ref,k_ref,v_ref,do_ref,o_ref,lse_ref,grads_ref,ds_ref):
    length=BUFFER + bucket_ref[at_ref[0]]
    low=lax.broadcasted_iota(jnp.int32,(1,128),1)<64
    q=q_ref[...]; do=do_ref[...]
    zero=jnp.zeros((),q.dtype)
    prod=do.astype(jnp.float32)*o_ref[...].astype(jnp.float32)
    prodT=prod.T
    lseT=lse_ref[...].T
    deltas=(jnp.sum(prodT[:64],axis=0,keepdims=True),jnp.sum(prodT[64:],axis=0,keepdims=True))
    lses=(lseT[0:1],lseT[64:65])
    for b in range(SEQ//KB):
        rows=pl.ds(b*KB,KB)
        k=k_ref[rows,:]; v=v_ref[rows,:]
        bias=jnp.where(lax.broadcasted_iota(jnp.int32,(KB,1),0)+b*KB<length,0.0,-1e30).astype(jnp.float32)
        dks=[];dvs=[]
        for h in range(2):
            pick=(lambda a: jnp.where(low,a,zero)) if h==0 else (lambda a: jnp.where(low,zero,a))
            s=nt(pick(k),q)+bias
            p=jnp.exp(s-lses[h])
            dp=nt(pick(v),do)
            ds=(p*(dp-deltas[h])).astype(jnp.bfloat16)
            dvs.append(nn(p.astype(jnp.bfloat16),do))
            dks.append(nn(ds,q))
            ds_ref[h,rows,:]=ds
        grads_ref[1,rows,:]=jnp.where(low,dks[0],dks[1]).astype(jnp.bfloat16)
        grads_ref[2,rows,:]=jnp.where(low,dvs[0],dvs[1]).astype(jnp.bfloat16)
    kT=k_ref[...].astype(jnp.float32).T.astype(jnp.bfloat16)
    dqT=jnp.concatenate([nn(kT[64*h:64*h+64],ds_ref[h]) for h in range(2)],axis=0)
    grads_ref[0]=(dqT.T*0.125).astype(jnp.bfloat16)

def attend_back(first,count,at,bucket,joint,do,o,lse,KB=544):
    spec=lambda off: pl.BlockSpec((SEQ,128),lambda i,off=off:(0,i+off))
    return pl.pallas_call(partial(attend_back_kernel,KB),
        grid=(count,),
        in_specs=[smem(),smem(),spec(first),spec(6+first),spec(12+first),spec(first),spec(first),spec(first)],
        out_specs=pl.BlockSpec((3,SEQ,128),lambda i:(0,0,i)),
        out_shape=jax.ShapeDtypeStruct((3,SEQ,count*128),jnp.bfloat16),
        scratch_shapes=[pltpu.VMEM((2,SEQ,SEQ),jnp.bfloat16)],
        compiler_params=pltpu.CompilerParams(vmem_limit_bytes=VMEM),
        cost_estimate=OWN,
        name="attend_back")(at,bucket,joint,joint,joint,do,o,lse)


def line(ref):
    return ref[...].reshape(1, ref.shape[0])


def smem():
    return pl.BlockSpec(memory_space=pltpu.SMEM)


def place_kernel(wide, at_ref, bucket_ref, start_ref, chosen_ref, latent_ref, spot_ref, live_ref, dealt_ref):
    image, place_wide, place_narrow, narrow = at_ref[0], at_ref[1], at_ref[2], at_ref[3]
    seq = chosen_ref.shape[1]
    slots = live_ref.shape[1]
    shift = wide.bit_length() - 1
    deep = slots // wide
    deep_shift = deep.bit_length() - 1
    row = lax.broadcasted_iota(jnp.int32, (seq, seq), 0)
    column = lax.broadcasted_iota(jnp.int32, (seq, seq), 1)
    lower = (column <= row).astype(jnp.float32).astype(jnp.bfloat16)
    chosen = jnp.broadcast_to(chosen_ref[...], (8, seq)).astype(jnp.float32).astype(jnp.bfloat16)
    counted = nt(lower, chosen)
    first_row = lax.broadcasted_iota(jnp.int32, counted.shape, 0) == 0
    before = jnp.where(first_row, 0.0, pltpu.roll(counted, 1, 0))
    is_chosen = (counted - before)[:, :1] > 0.5
    order = counted[:, :1].astype(jnp.int32) - 1
    target = ((start_ref[image] + order) & (wide - 1)) * deep + (order >> shift)
    target = jnp.where(is_chosen, target, -1)
    slot = lax.broadcasted_iota(jnp.int32, (seq, slots), 1)
    spot = (slot == target).astype(jnp.float32).astype(jnp.bfloat16)
    spot_ref[...] = spot
    dealt_ref[...] = nn(latent_ref[...], spot).T.astype(jnp.bfloat16)
    lane = lax.broadcasted_iota(jnp.int32, (1, slots), 1)
    live = jnp.zeros((1, slots), jnp.float32)
    for source in range(wide):
        other = source * narrow + place_narrow
        count = bucket_ref[other] * MASK_MAX // IMAGE_MAX
        rank = (place_wide - start_ref[other]) & (wide - 1)
        arrived = jnp.maximum((count - rank + wide - 1) >> shift, 0)
        inside = ((lane >> deep_shift) == source) & ((lane & (deep - 1)) < arrived)
        live = jnp.where(inside, 1.0, live)
    live_ref[...] = live


def places(at, bucket, deal_start, masked, latents, wide):
    seq = masked.shape[1]
    return pl.pallas_call(
        partial(place_kernel, wide),
        in_specs=[smem(), smem(), smem(), whole_block((1, seq)), whole_block((TOKEN_DIM, seq))],
        out_specs=[
            whole_block((seq, MASK_MAX)),
            whole_block((1, MASK_MAX)),
            whole_block((MASK_MAX, TOKEN_DIM)),
        ],
        grid=(1,),
        out_shape=[
            jax.ShapeDtypeStruct((seq, MASK_MAX), jnp.bfloat16),
            jax.ShapeDtypeStruct((1, MASK_MAX), jnp.float32),
            jax.ShapeDtypeStruct((MASK_MAX, TOKEN_DIM), jnp.bfloat16),
        ],
        compiler_params=pltpu.CompilerParams(vmem_limit_bytes=VMEM),
        cost_estimate=OTHER,
        name="places",
    )(at, bucket, deal_start, masked, latents)


def joint_kernel(tokens_ref, gain_ref, shift_ref, weight_ref, bias_ref, first_ref, joint_ref):
    normed, unused = normalize(tokens_ref[...].astype(jnp.float32))
    first = (normed * line(gain_ref) + line(shift_ref)).astype(jnp.bfloat16)
    first_ref[...] = first
    for part in range(3):
        cols = slice(part * D, (part + 1) * D)
        out = nn(first, weight_ref[:, cols])
        if part != 1:
            out = out + line(bias_ref)[:, part // 2 * D : part // 2 * D + D]
        out = out.astype(jnp.bfloat16)
        if part == 0:
            out = out * jnp.bfloat16(HEAD_DIM ** (-0.5))
        joint_ref[:, cols] = out


ROWS = 272


def by_block(columns):
    return pl.BlockSpec((ROWS, columns), lambda i: (i, 0))


def joint_pass(tokens, gain, shift, weight, bias):
    seq = tokens.shape[0]
    return pl.pallas_call(
        joint_kernel,
        grid=(seq // ROWS,),
        in_specs=[by_block(D)] + [whole_block(a.shape) for a in (gain, shift, weight, bias)],
        out_specs=[by_block(D), by_block(3 * D)],
        out_shape=[
            jax.ShapeDtypeStruct((seq, D), jnp.bfloat16),
            jax.ShapeDtypeStruct((seq, 3 * D), jnp.bfloat16),
        ],
        compiler_params=pltpu.CompilerParams(vmem_limit_bytes=VMEM),
        cost_estimate=OTHER,
        name="joint_pass",
    )(tokens, gain, shift, weight, bias)


def gelu_parts(value):
    size = jnp.abs(value)
    bell = jnp.exp(-0.5 * value * value)
    step = 1.0 / (1.0 + (0.3275911 * math.sqrt(0.5)) * size)
    tail = 0.5 * 1.061405429 * step - 0.5 * 1.453152027
    tail = tail * step + 0.5 * 1.421413741
    tail = tail * step - 0.5 * 0.284496736
    tail = tail * step + 0.5 * 0.254829592
    tail = tail * step * bell
    return jnp.where(value < 0.0, tail, 1.0 - tail), bell * (1.0 / math.sqrt(2.0 * math.pi))


def keep_column(at_ref, bucket_ref, rows):
    position = lax.broadcasted_iota(jnp.int32, (rows, 1), 0) + pl.program_id(0) * rows
    return (position < BUFFER + bucket_ref[at_ref[0]]).astype(jnp.float32)


def feed_kernel(
    at_ref,
    bucket_ref,
    mixed_ref,
    tokens_ref,
    latent_ref,
    spot_ref,
    out_w_ref,
    out_b_ref,
    gain_ref,
    shift_ref,
    expand_ref,
    expand_b_ref,
    reduce_ref,
    reduce_b_ref,
    output_ref,
    middle_ref,
    second_ref,
    active_ref,
    slope_ref,
    dealt_ref,
    spread_ref,
    dealt_scratch,
    spread_scratch,
):
    step = pl.program_id(0)

    @pl.when(step == 0)
    def _():
        dealt_scratch[...] = jnp.zeros_like(dealt_scratch)
        spread_scratch[...] = jnp.zeros_like(spread_scratch)

    keep = keep_column(at_ref, bucket_ref, mixed_ref.shape[0])
    branch = nn(mixed_ref[...], out_w_ref[...]) + line(out_b_ref)
    middle = tokens_ref[...].astype(jnp.float32) + branch
    middle_ref[...] = middle
    normed, unused = normalize(middle)
    second = (normed * line(gain_ref) + line(shift_ref)).astype(jnp.bfloat16)
    second_ref[...] = second
    hidden_width = expand_ref.shape[1]
    expand_b = line(expand_b_ref)
    feed = line(reduce_b_ref)
    for part in range(hidden_width // D):
        cols = slice(part * D, (part + 1) * D)
        hidden = nn(second, expand_ref[:, cols]) + expand_b[:, cols]
        phi, density = gelu_parts(hidden)
        active = (hidden * phi).astype(jnp.bfloat16)
        active_ref[:, cols] = active
        slope_ref[:, cols] = (phi + hidden * density).astype(jnp.bfloat16)
        feed = feed + nn(active, reduce_ref[cols, :])
    output = ((middle + feed) * keep).astype(jnp.bfloat16)
    output_ref[...] = output
    spread_scratch[0:1, :] += jnp.sum(keep * branch * branch, axis=0, keepdims=True)
    spread_scratch[1:2, :] += jnp.sum(keep * feed * feed, axis=0, keepdims=True)
    spot = spot_ref[...]
    dealt_scratch[:, :D] += tn(spot, output)

    @pl.when(step == pl.num_programs(0) - 1)
    def _():
        dealt_scratch[:, D : D + TOKEN_DIM] = latent_ref[...].astype(jnp.float32)
        dealt_ref[...] = dealt_scratch[...].astype(jnp.bfloat16)
        count = (BUFFER + bucket_ref[at_ref[0]]).astype(jnp.float32) * D
        total = jnp.sum(spread_scratch[...], axis=1, keepdims=True)
        spread_ref[...] = jnp.sqrt(jnp.broadcast_to(total, spread_ref.shape) / count)


def feed_pass(at, bucket, mixed, tokens, latents, spot, weights):
    seq = tokens.shape[0]
    slots = spot.shape[1]
    hidden = weights[4].shape[1]
    low = lambda *s: jax.ShapeDtypeStruct(s, jnp.bfloat16)
    full = lambda *s: jax.ShapeDtypeStruct(s, jnp.float32)
    return pl.pallas_call(
        feed_kernel,
        grid=(seq // ROWS,),
        in_specs=[smem(), smem(), by_block(D), by_block(D), whole_block((slots, TOKEN_DIM)), by_block(slots)]
        + [whole_block(a.shape) for a in weights],
        out_specs=[
            by_block(D),
            by_block(D),
            by_block(D),
            by_block(hidden),
            by_block(hidden),
            whole_block((slots, D + 128)),
            whole_block((8, 128)),
        ],
        out_shape=[
            low(seq, D),
            full(seq, D),
            low(seq, D),
            low(seq, hidden),
            low(seq, hidden),
            low(slots, D + 128),
            full(8, 128),
        ],
        scratch_shapes=[pltpu.VMEM((slots, D + 128), jnp.float32), pltpu.VMEM((8, D), jnp.float32)],
        compiler_params=pltpu.CompilerParams(vmem_limit_bytes=VMEM),
        cost_estimate=OTHER,
        name="feed_pass",
    )(at, bucket, mixed, tokens, latents, spot, *weights)


def feed_back_kernel(
    at_ref,
    bucket_ref,
    cot_ref,
    spot_ref,
    middle_ref,
    slope_ref,
    returned_ref,
    out_w_ref,
    gain_ref,
    expand_ref,
    reduce_ref,
    feed_grad_ref,
    hidden_grad_ref,
    middle_grad_ref,
    branch_grad_ref,
    mixed_grad_ref,
    sums_ref,
    wide_sum_ref,
):
    @pl.when(pl.program_id(0) == 0)
    def _():
        sums_ref[...] = jnp.zeros_like(sums_ref)
        wide_sum_ref[...] = jnp.zeros_like(wide_sum_ref)

    def add_sum(row, value):
        sums_ref[row : row + 1, :] += jnp.sum(value, axis=0, keepdims=True)

    keep = keep_column(at_ref, bucket_ref, cot_ref.shape[0])
    grad = (cot_ref[...].astype(jnp.float32) + nn(spot_ref[...], returned_ref[...])) * keep
    feed_grad = grad.astype(jnp.bfloat16)
    feed_grad_ref[...] = feed_grad
    add_sum(0, feed_grad.astype(jnp.float32))
    second_grad = jnp.zeros(grad.shape, jnp.float32)
    for part in range(expand_ref.shape[1] // D):
        cols = slice(part * D, (part + 1) * D)
        active_grad = nt(feed_grad, reduce_ref[cols, :])
        hidden_grad = (active_grad * slope_ref[:, cols].astype(jnp.float32)).astype(jnp.bfloat16)
        hidden_grad_ref[:, cols] = hidden_grad
        wide_sum_ref[:, cols] += jnp.sum(hidden_grad.astype(jnp.float32), axis=0, keepdims=True)
        second_grad = second_grad + nt(hidden_grad, expand_ref[:, cols])
    normed, inverse = normalize(middle_ref[...])
    add_sum(1, second_grad * normed)
    add_sum(2, second_grad)
    middle_grad = grad + normalize_back(second_grad * line(gain_ref), normed, inverse)
    middle_grad_ref[...] = middle_grad
    branch_grad = middle_grad.astype(jnp.bfloat16)
    branch_grad_ref[...] = branch_grad
    add_sum(3, branch_grad.astype(jnp.float32))
    mixed_grad_ref[...] = nt(branch_grad, out_w_ref[...]).astype(jnp.bfloat16)


def feed_back(at, bucket, cotangent, spot, middle, slope, returned, weights):
    seq = cotangent.shape[0]
    slots = spot.shape[1]
    hidden = slope.shape[1]
    low = lambda *s: jax.ShapeDtypeStruct(s, jnp.bfloat16)
    full = lambda *s: jax.ShapeDtypeStruct(s, jnp.float32)
    return pl.pallas_call(
        feed_back_kernel,
        grid=(seq // ROWS,),
        in_specs=[smem(), smem(), by_block(D), by_block(slots), by_block(D), by_block(hidden)]
        + [whole_block(a.shape) for a in (returned,) + weights],
        out_specs=[
            by_block(D),
            by_block(hidden),
            by_block(D),
            by_block(D),
            by_block(D),
            whole_block((8, D)),
            whole_block((1, hidden)),
        ],
        out_shape=[
            low(seq, D),
            low(seq, hidden),
            full(seq, D),
            low(seq, D),
            low(seq, D),
            full(8, D),
            full(1, hidden),
        ],
        compiler_params=pltpu.CompilerParams(vmem_limit_bytes=VMEM),
        cost_estimate=OTHER,
        name="feed_back",
    )(at, bucket, cotangent, spot, middle, slope, returned, *weights)


def feed_grads_kernel(wide, half_ref, second_ref, hidden_ref, active_ref, grad_ref, *refs):
    step = pl.program_id(0)
    refs[-1][...] = jnp.zeros_like(refs[-1])

    @pl.when(step < 2)
    def _():
        grad = tn(second_ref[...], hidden_ref[...])
        if len(refs) == 3:
            refs[0][0] = grad.astype(jnp.bfloat16)
        else:
            grad = (grad + refs[0][0].astype(jnp.float32)).astype(jnp.bfloat16)

            @pl.when(step == 0)
            def _():
                refs[2][...] = grad[None]

            @pl.when(step == 1)
            def _():
                refs[3][...] = grad[None]

    @pl.when(step >= 2)
    def _():
        whole = tn(active_ref[...], grad_ref[...])
        pieces = 4
        rows = D // wide
        places = whole.shape[0] // (pieces * rows)
        whole = whole.reshape(places, pieces, rows, D // 2)
        for piece in range(pieces):
            at = (piece // 2, slice(None), slice(piece % 2 * (D // 2), (piece % 2 + 1) * (D // 2)))
            part = whole[:, piece].reshape(places * rows, D // 2)
            if len(refs) == 3:
                refs[1][at] = part.astype(jnp.bfloat16)
            else:
                part = part + refs[1][at].astype(jnp.float32)
                refs[4][at], refs[5][at] = split_rows(part, places, half_ref[2])


def feed_grads(half, second, hidden_grad, active, feed_grad, wide, got=None):
    seq, hidden = active.shape
    chunk = lambda i: jnp.maximum(i - 2, 0)
    turned = lambda i, half: jnp.minimum(i, 1) ^ (1 - half[1])
    low = lambda *s: jax.ShapeDtypeStruct(s, jnp.bfloat16)
    expand_tile = pl.BlockSpec((1, D, D), lambda i, half: (turned(i, half), 0, 0))
    rows_of = lambda rows: pl.BlockSpec((2, rows, D), lambda i, half: (0, chunk(i), 0))
    if got is None:
        more = ()
        outs = [(expand_tile, low(2, D, D)), (rows_of(D // 4), low(2, D, D))]
    else:
        more = tuple(got)
        outs = [(whole_block((1, D, D)), low(1, D, D))] * 2
        outs += [(rows_of(D // 8), low(2, D // 2, D))] * 2
    outs.append((whole_block((8, 128)), MARK))
    return pl.pallas_call(
        partial(feed_grads_kernel, wide),
        grid_spec=pltpu.PrefetchScalarGridSpec(
            num_scalar_prefetch=1,
            grid=(6,),
            in_specs=[
                whole_block((seq, D)),
                pl.BlockSpec((seq, D), lambda i, half: (0, half[0] * 2 + turned(i, half))),
                pl.BlockSpec((seq, D), lambda i, half: (0, chunk(i))),
                pl.BlockSpec((seq, D // 2), lambda i, half: (0, half[0])),
            ]
            + [expand_tile, rows_of(D // 4)][: len(more)],
            out_specs=[o[0] for o in outs],
        ),
        out_shape=[o[1] for o in outs],
        compiler_params=pltpu.CompilerParams(vmem_limit_bytes=VMEM),
        cost_estimate=OTHER if got is None else OWN,
        name="feed_grads",
    )(half, second, hidden_grad, active, feed_grad, *more)


def last_kind(turn, half):
    return (turn // 2 ^ (1 - half[0])) * 2 + turn % 2


def last_grads_kernel(
    half_ref, first_ref, mixed_ref, a_ref, b_ref, c_ref, branch_ref, sent_ref, kept_ref, mark_ref
):
    turn = pl.program_id(0)
    kind = last_kind(turn, half_ref)
    mark_ref[...] = jnp.zeros_like(mark_ref)

    def put(whole):
        whole = whole.astype(jnp.bfloat16)

        @pl.when(turn < 2)
        def _():
            for i in range(6):
                sent_ref[i] = whole[:, i * 128 : (i + 1) * 128]

        @pl.when(turn >= 2)
        def _():
            for i in range(6):
                kept_ref[i] = whole[:, i * 128 : (i + 1) * 128]

    @pl.when(kind < 3)
    def _():
        put(tn(first_ref[...], jnp.concatenate([a_ref[0], b_ref[0], c_ref[0]], axis=1)))

    @pl.when(kind == 3)
    def _():
        put(tn(mixed_ref[...], branch_ref[...]))


def last_grads(half, first_in, mixed, parts, branch_grad):
    seq = mixed.shape[0]
    part = lambda a: pl.BlockSpec(
        (1,) + a.shape[1:], lambda i, half: (jnp.minimum(last_kind(i, half), 2), 0, 0)
    )
    tiles = jax.ShapeDtypeStruct((12, D, 128), jnp.bfloat16)
    return pl.pallas_call(
        last_grads_kernel,
        grid_spec=pltpu.PrefetchScalarGridSpec(
            num_scalar_prefetch=1,
            grid=(4,),
            in_specs=[whole_block((seq, D)), whole_block((seq, D))]
            + [part(a) for a in parts]
            + [whole_block((seq, D))],
            out_specs=[
                pl.BlockSpec((6, D, 128), lambda i, half: (jnp.minimum(i, 1), 0, 0)),
                pl.BlockSpec((6, D, 128), lambda i, half: (jnp.maximum(i - 2, 0), 0, 0)),
                whole_block((8, 128)),
            ],
        ),
        out_shape=[tiles, tiles, MARK],
        compiler_params=pltpu.CompilerParams(vmem_limit_bytes=VMEM),
        cost_estimate=OTHER,
        name="last_grads",
    )(half, first_in, mixed, *parts, branch_grad)


def tokens_back_kernel(
    tokens_ref, a_ref, b_ref, c_ref, middle_ref, gain_ref, weight_ref, out_ref, packed_ref, sums_ref
):
    @pl.when(pl.program_id(0) == 0)
    def _():
        sums_ref[...] = jnp.zeros_like(sums_ref)

    def add_sum(row, value):
        sums_ref[row : row + 1, :] += jnp.sum(value, axis=0, keepdims=True)

    query, keys, value = [
        jnp.concatenate([a_ref[i], b_ref[i], c_ref[i]], axis=1) for i in range(3)
    ]
    grad = nt(query, weight_ref[:, :D])
    grad = grad + nt(keys, weight_ref[:, D : 2 * D])
    grad = grad + nt(value, weight_ref[:, 2 * D :])
    normed, inverse = normalize(tokens_ref[...].astype(jnp.float32))
    add_sum(0, grad * normed)
    add_sum(1, grad)
    add_sum(2, query.astype(jnp.float32))
    add_sum(3, value.astype(jnp.float32))
    out_ref[...] = middle_ref[...] + normalize_back(grad * line(gain_ref), normed, inverse)

    @pl.when(pl.program_id(0) == pl.num_programs(0) - 1)
    def _():
        wide = packed_ref.shape[0]
        part = D // wide
        for w in range(wide):
            packed_ref[w : w + 1, :part] = sums_ref[0:1, w * part : (w + 1) * part]
            packed_ref[w : w + 1, part : 2 * part] = sums_ref[1:2, w * part : (w + 1) * part]
            bias_row = 2 + w * 2 // wide
            at = w % (wide // 2) * 2 * part
            packed_ref[w : w + 1, 2 * part :] = sums_ref[bias_row : bias_row + 1, at : at + 2 * part]


def tokens_back(tokens, parts, middle_grad, gain, weight, wide):
    seq = tokens.shape[0]
    return pl.pallas_call(
        tokens_back_kernel,
        grid=(seq // ROWS,),
        in_specs=[by_block(D)]
        + [pl.BlockSpec((3, ROWS, a.shape[2]), lambda i: (0, i, 0)) for a in parts]
        + [by_block(D)] + [whole_block(gain.shape), whole_block(weight.shape)],
        out_specs=[by_block(D), whole_block((wide, 4 * D // wide))],
        out_shape=[
            jax.ShapeDtypeStruct((seq, D), jnp.float32),
            jax.ShapeDtypeStruct((wide, 4 * D // wide), jnp.float32),
        ],
        scratch_shapes=[pltpu.VMEM((8, D), jnp.float32)],
        compiler_params=pltpu.CompilerParams(vmem_limit_bytes=VMEM),
        cost_estimate=OTHER,
        name="tokens_back",
    )(tokens, *parts, middle_grad, gain, weight)


def pack_kernel(feed_ref, hidden_ref, input_ref, final_ref, token_ref, *refs):
    low_ref, out_ref = refs[-2:]
    out_ref[...] = jnp.zeros_like(out_ref)
    wide, rows, cols = out_ref.shape
    part = D // wide
    block = input_ref.shape[1] // wide
    for w in range(wide):
        out_ref[w, :TOKEN_DIM, :block] = input_ref[:, w * block : (w + 1) * block]
        out_ref[w, :TOKEN_DIM, block : 2 * block] = final_ref[:, w * block : (w + 1) * block]
        out_ref[w, TOKEN_DIM : TOKEN_DIM + 1, :] = hidden_ref[:, w * cols : (w + 1) * cols]
        out_ref[w, TOKEN_DIM + 2 : TOKEN_DIM + 3, :] = token_ref[w : w + 1, :]
        for i in range(4):
            out_ref[w, TOKEN_DIM + 1 : TOKEN_DIM + 2, i * part : (i + 1) * part] = feed_ref[
                i : i + 1, w * part : (w + 1) * part
            ]
    low_ref[...] = out_ref[...].astype(jnp.bfloat16)


def pack(feed_sums, hidden_sum, input_grad, final_grad, token_packed, marks):
    operands = (feed_sums, hidden_sum, input_grad, final_grad, token_packed)
    wide = token_packed.shape[0]
    shape = (wide, TOKEN_DIM + 16, hidden_sum.shape[1] // wide)
    return pl.pallas_call(
        pack_kernel,
        grid=(1,),
        in_specs=[whole_block(a.shape) for a in operands] + [pl.BlockSpec(memory_space=pl.ANY)] * len(marks),
        out_specs=whole_block(shape),
        out_shape=jax.ShapeDtypeStruct(shape, jnp.bfloat16),
        scratch_shapes=[pltpu.VMEM(shape, jnp.float32)],
        cost_estimate=OTHER,
        name="pack",
    )(*operands, *marks)


def add_up(terms):
    total = terms[0].astype(jnp.float32)
    for term in terms[1:]:
        total = total + term.astype(jnp.float32)
    return total


def swap(array, axis, mask):
    count = lax.axis_size(axis)
    return lax.ppermute(array, axis, [(i, i ^ mask) for i in range(count)])


def bit(axis, mask):
    return lax.axis_index(axis) // mask % 2


def pick(array, index, axis):
    return lax.dynamic_index_in_dim(array, index, axis, keepdims=False)


class Order:
    def __init__(self):
        self.mark = ()
        self.marks = ()

    def __call__(self, *values):
        out = lax.optimization_barrier(values + self.mark)[: len(values)]
        return out if len(values) > 1 else out[0]

    def at(self, *values):
        self.mark = values


def bits():
    return jnp.stack([bit("narrow", 1), bit("narrow", 2), bit("wide", 1)]).astype(jnp.int32)


class Flow:
    AXES = {"x": ("narrow", 2), "y": ("wide", 1)}

    def __init__(self, order, lanes, sends=None):
        self.order = order
        self.wide = lax.axis_size("wide").bit_length() - 1
        self.lanes = [[list(terms), tuple(left)] for terms, left in lanes]
        self.steps = self.run(sends)

    def step(self):
        next(self.steps)

    def take(self):
        got = self.order(*self.got)
        return got if isinstance(got, (tuple, list)) else (got,)

    def send(self, *sends):
        self.got = tuple(swap(*s) for s in sends)
        self.order.at(*[s[0] for s in sends])

    def shaped(self, array, left):
        dims = (2,) * (self.wide - ("y" not in left))
        if "x" in left:
            return array.reshape((2, array.shape[0] // 2) + dims + (-1, array.shape[2]))
        return array.reshape((array.shape[0],) + dims + (-1, array.shape[2]))

    def exchange(self, lane, goal):
        terms, left = lane
        dim = 0 if goal == "x" else self.wide + ("x" in left)
        mine = bit(*self.AXES[goal])
        sent = add_up([pick(t, 1 - mine, dim) for t in terms]).astype(jnp.bfloat16)
        lane[0] = [pick(t, mine, dim) for t in terms]
        lane[1] = tuple(n for n in left if n != goal)
        return (sent,) + self.AXES[goal]

    def run(self, sends):
        if sends is not None:
            shapes = [lane[0][0].shape for lane in self.lanes]
            self.send(*sends)
            yield
            got = self.take()
            for lane, g, shape in zip(self.lanes, got, shapes):
                lane[0].append(g.reshape(shape))
        while any(lane[1] for lane in self.lanes):
            self.send(*[self.exchange(lane, lane[1][0]) for lane in self.lanes])
            yield
            for lane, got in zip(self.lanes, self.take()):
                lane[0].append(got)
        parts = [lane[0] for lane in self.lanes]
        both = []
        for b in reversed(range(1, self.wide)):
            mask = 1 << b
            mine = bit("wide", mask)
            sent = [add_up([pick(t, 1 - mine, 1) for t in terms]) for terms in parts]
            sent = [jnp.concatenate(sent, axis=0)] + [pick(t, 1 - mine, 1) for t in both]
            parts = [[pick(t, mine, 1) for t in terms] for terms in parts]
            both = [pick(t, mine, 1) for t in both]
            self.send((add_up(sent).astype(jnp.bfloat16), "wide", mask))
            yield
            both.append(self.take()[0])
        own = jnp.concatenate([add_up(terms) for terms in parts], axis=0)
        share = add_up([own] + both).astype(jnp.bfloat16)
        self.send((share, "narrow", 2))
        yield
        (other,) = self.take()
        share = self.order(share)
        self.send((share, "narrow", 1), (other, "narrow", 1))
        yield
        self.result = (share, other) + tuple(self.take())
        yield

    def finish(self):
        for unused in self.steps:
            pass
        return self.result


class Halves:
    def __init__(self, order, sent):
        *sent, mark = sent
        self.order = order
        self.flight = tuple(swap(a, "narrow", 1) for a in sent)
        order.at(mark)
        order.marks += (mark,)

    def got(self):
        got = self.order(*self.flight)
        return tuple(got) if isinstance(got, (tuple, list)) else (got,)


def unpack_kernel(put, bits_ref, *refs):
    shares, outs = refs[:4], refs[4:]
    core, x = bits_ref[0], bits_ref[1]
    for c in range(2):
        for k in range(2):
            same_x, same_core = x == k, core == c
            for t in range(shares[0].shape[0]):
                one, two, three, four = [s[t].astype(jnp.float32) for s in shares]
                near = jnp.where(same_x, one, two)
                far = jnp.where(same_x, three, four)
                put(outs, c, k, t, jnp.where(same_core, near, far))


def unpack(put, shares, shapes):
    return pl.pallas_call(
        partial(unpack_kernel, put),
        grid=(1,),
        in_specs=[smem()] + [whole_block(a.shape) for a in shares],
        out_specs=[whole_block(s) for s in shapes],
        out_shape=[jax.ShapeDtypeStruct(s, jnp.float32) for s in shapes],
        compiler_params=pltpu.CompilerParams(vmem_limit_bytes=VMEM),
        cost_estimate=OTHER,
        name="unpack",
    )(bits(), *shares)


def put_columns(spans, tiles):
    def put(outs, c, x, t, value):
        column = (c * 2 + x) * tiles + t
        for out_ref, (first, stop) in zip(outs, spans):
            if first <= column < stop:
                at = (column - first) * value.shape[1]
                out_ref[:, at : at + value.shape[1]] = value

    return put


def small_steps(order, rows):
    def send(*sends):
        order.at(*[s[0] for s in sends])
        return [swap(*s) for s in sends]

    wide = lax.axis_size("wide")
    low = rows.astype(jnp.bfloat16)
    for mask in (1, 2):
        (got,) = send((low, "narrow", mask))
        yield
        low = add_up([low, order(got)]).astype(jnp.bfloat16)
    low = low.reshape((wide // 2, 2) + low.shape[1:])
    mine = bit("wide", 1)
    (got,) = send((pick(low, 1 - mine, 1), "wide", 1))
    yield
    low = add_up([pick(low, mine, 1), order(got)]).astype(jnp.bfloat16)
    place = lax.axis_index("wide") // 2
    got = send(*[(pick(low, place ^ (m // 2), 0), "wide", m) for m in range(2, wide, 2)])
    yield
    yield add_up([pick(low, place, 0)] + list(order(*got)))


def shards(
    tokens,
    cotangent,
    latents,
    added_noise,
    timesteps,
    bucket,
    masked,
    deal_start,
    first_gain,
    first_shift,
    joint_weight,
    query_value_bias,
    output_weight,
    output_bias,
    second_gain,
    second_shift,
    expand_weight,
    expand_bias,
    reduce_weight,
    reduce_bias,
    input_proj,
    cond_proj,
    time_first,
    time_second,
    block_mod,
    block_expand,
    block_reduce,
    final_mod,
    final_proj,
):
    wide = lax.axis_size("wide")
    narrow = lax.axis_size("narrow")
    place_wide = lax.axis_index("wide")
    place_narrow = lax.axis_index("narrow")
    mine = bits()
    other = mine.at[0].set(1 - mine[0])
    image_index = place_wide * narrow + place_narrow
    at = jnp.stack([image_index, place_wide, place_narrow, jnp.int32(narrow)]).astype(jnp.int32)

    spot, live, dealt_latents = places(at, bucket, deal_start, masked, latents.T, wide)
    slots = spot.shape[1]
    steps = timesteps.astype(jnp.float32)
    half = time_first.shape[0] // 2
    freqs = jnp.exp(-math.log(10000.0) * jnp.arange(half).astype(jnp.float32) / half)
    angles = steps.reshape(-1, 1) * freqs
    sinus = jnp.concatenate([jnp.cos(angles), jnp.sin(angles)], axis=-1).astype(jnp.bfloat16)
    offset = steps * STEP_ANGLE
    keep_sig = jnp.cos(offset + SHIFT_ANGLE) / math.cos(SHIFT_ANGLE)
    drop_sig = jnp.sqrt(jnp.sin(offset) * jnp.sin(offset + 2.0 * SHIFT_ANGLE)) / math.cos(SHIFT_ANGLE)
    input_turned = input_proj.T
    final_turned = final_proj.T

    first_in, joint = joint_pass(
        tokens, first_gain, first_shift, joint_weight, query_value_bias
    )
    mixed, logsum = attend(at, bucket, joint)
    block_output, middle, second_in, active, slope, dealt, spread = feed_pass(
        at,
        bucket,
        mixed,
        tokens,
        dealt_latents,
        spot,
        (
            output_weight,
            output_bias,
            second_gain,
            second_shift,
            expand_weight,
            expand_bias,
            reduce_weight,
            reduce_bias,
        ),
    )

    def deal(array):
        shape = array.shape
        return lax.all_to_all(
            array.reshape(wide, -1, shape[1]), "wide", split_axis=0, concat_axis=0, tiled=True
        ).reshape(shape)

    dealt = deal(dealt)
    low_turned, time_slope, timed = time_embedding(sinus, time_first, time_second)
    (
        guess,
        left,
        fin_grad,
        branch_grad,
        upper_grad,
        mod_grad,
        timed_grad,
        embed_grad,
        rows_grad,
        input_grad,
        final_grad,
    ) = head_pass(
        dealt,
        timed,
        keep_sig,
        drop_sig,
        added_noise,
        live,
        (input_turned, cond_proj, block_mod, block_expand, block_reduce, final_mod, final_turned),
    )
    order = Order()
    order.at(rows_grad)
    returned = deal(rows_grad)
    first_grad = time_back(order(timed_grad), time_second, time_slope)
    order.at(first_grad)
    one_args = (fin_grad, branch_grad, upper_grad)
    halves_one = Halves(order, head_grads_one(other, order(left), *one_args))
    two_args = (mod_grad, timed_grad, dealt, embed_grad, sinus, first_grad, wide)
    halves_two = Halves(order, head_grads_two(other, left, order(low_turned), *two_args))
    returned = order(returned)
    order.at(returned, *order.mark)

    def note(mark):
        order.marks += (mark,)
        order.at(mark)

    sent, kept, mark = head_grads_one(mine, order(left), *one_args, *halves_one.got())
    note(mark)
    shape = lambda a: a.reshape((a.shape[0],) + (2,) * (wide.bit_length() - 1) + (-1, a.shape[2]))
    half_shape = lambda a: a.reshape(
        (2, a.shape[0] // 2) + (2,) * (wide.bit_length() - 2) + (-1, a.shape[2])
    )
    one = Flow(order, [([shape(kept)], ("y",))], [(sent, "narrow", 2)])
    one.step()
    order.at(mark)
    sent_a, kept_a, sent_b, kept_b, mark = head_grads_two(
        mine, left, order(low_turned), *two_args, *halves_two.got()
    )
    note(mark)
    two = Flow(
        order,
        [([shape(kept_a)], ("y",)), ([half_shape(kept_b)], ("x",))],
        [(sent_a, "narrow", 2), (sent_b, "wide", 1)],
    )
    two.step()
    order.at(mark)
    feed_grad, hidden_grad, middle_grad, out_grad, mixed_grad, feed_sums, hidden_sum = feed_back(
        at,
        bucket,
        order(cotangent),
        spot,
        middle,
        slope,
        returned,
        (output_weight, second_gain, expand_weight, reduce_weight),
    )
    order.at(mixed_grad)
    feed_args = (hidden_grad, active, feed_grad, wide)
    halves_feed = Halves(order, feed_grads(other, order(second_in), *feed_args))
    one.step()
    parts = []

    def attend_back_part(i):
        grads = attend_back(2 * i, 2, at, bucket, joint, order(mixed_grad), mixed, logsum)
        order.at(grads)
        parts.append(grads)

    attend_back_part(0)
    two.step()
    sent_e, kept_e, sent_r, kept_r, mark = feed_grads(
        mine, order(second_in), *feed_args, halves_feed.got()
    )
    note(mark)
    feed = Flow(
        order,
        [([shape(kept_e)], ("y",)), ([half_shape(kept_r)], ("x",))],
        [(sent_e, "narrow", 2), (sent_r, "wide", 1)],
    )
    feed.step()
    order.at(mark)
    one.step()
    attend_back_part(1)
    two.step()
    one.step()
    feed.step()
    attend_back_part(2)
    feed.step()
    two.step()
    one.step()
    sent, own, mark = last_grads(mine, order(first_in), mixed, parts, out_grad)
    halves_last = Halves(order, (sent, mark))
    terms = [
        a.reshape((2, 6) + (2,) * (wide.bit_length() - 1) + (-1, 128)) for a in (own,) + halves_last.got()
    ]
    last = Flow(
        order, [([a[:, :3] for a in terms], ("x", "y")), ([a[:, 3:] for a in terms], ("y", "x"))]
    )
    last.step()
    tokens_gradient, token_packed = tokens_back(
        order(tokens), parts, middle_grad, first_gain, joint_weight, wide
    )
    order.at(token_packed)
    width = cond_proj.shape[1]
    rows = width // wide
    cut = cond_proj.shape[0] // wide

    def hold(outs):
        order.at(*outs)
        return outs

    last.step()
    two.step()
    feed.step()
    one.step()
    packed = pack(feed_sums, hidden_sum, input_grad, final_grad, order(token_packed), order.marks)
    order.at(packed)
    small = small_steps(order, packed)
    next(small)
    last.step()
    next(small)
    one = one.finish()
    final_mod_out, block_reduce_out, block_expand_out = hold(
        unpack(
            put_columns(((0, 4), (4, 6), (6, 8)), 2),
            (order(one[0]),) + one[1:],
            ((rows, 2 * width), (rows, width), (rows, width)),
        )
    )
    two.step()
    feed.step()
    two = two.finish()

    def put_two(outs, c, x, t, value):
        column = (c * 2 + x) * 5 + t
        if column < 16:
            put_columns(((0, 12), (12, 16)), 5)(outs, c, x, t, value)
        else:
            cols = slice((column - 16) * 256, (column - 15) * 256)
            outs[2][:, cols] = value[:cut]
            outs[3][:, cols] = value[cut:]

    block_mod_out, time_second_out, cond_out, time_first_out = hold(
        unpack(
            put_two,
            (order(two[0]),) + two[1:],
            ((rows, 3 * width), (rows, width), (cut, width), (rows - cut, width)),
        )
    )
    last.step()
    next(small)
    feed.step()
    feed = feed.finish()

    def put_feed(outs, c, x, t, value):
        if t == 0:
            at = (c * 2 + x) * D
            outs[0][:, at : at + D] = value
        else:
            for i in range(2):
                piece = x * 2 + i
                outs[1][piece * cut : (piece + 1) * cut, c * (D // 2) : (c + 1) * (D // 2)] = value[
                    :, i * (D // 2) : (i + 1) * (D // 2)
                ]

    last.step()
    next(small)
    expand_out, reduce_out = hold(
        unpack(put_feed, (order(feed[0]),) + feed[1:], ((cut, 4 * D), (4 * cut, D)))
    )
    last.step()
    small = next(small)
    last = last.finish()
    joint_out, output_out = unpack(
        put_columns(((0, 18), (18, 24)), 6), last, ((cut, 3 * D), (cut, D))
    )
    part = D // wide
    block = input_grad.shape[1] // wide
    vectors = [small[TOKEN_DIM + 1, i * part : (i + 1) * part] for i in range(4)]
    input_out = small[:TOKEN_DIM, :block].T
    final_out = small[:TOKEN_DIM, block : 2 * block].T
    late = small[TOKEN_DIM + 2]
    outs = [
        late[:part],
        late[part : 2 * part],
        late[2 * part :],
        vectors[3],
        vectors[1],
        vectors[2],
        small[TOKEN_DIM],
        vectors[0],
        input_out,
        final_out,
    ]
    return (
        block_output,
        guess,
        spread[:2, 0].reshape(1, 2),
        tokens_gradient,
        outs[0],
        outs[1],
        joint_out,
        outs[2],
        output_out,
        outs[3],
        outs[4],
        outs[5],
        expand_out,
        outs[6],
        reduce_out,
        outs[7],
        outs[8],
        cond_out,
        time_first_out,
        time_second_out,
        block_mod_out,
        block_expand_out,
        block_reduce_out,
        final_mod_out,
        outs[9],
    )


def solution(mesh):
    in_specs = (
        P(("wide", "narrow"), None),
        P(("wide", "narrow"), None),
        P(("wide", "narrow"), None),
        P(None, None, ("wide", "narrow")),
        P(None, ("wide", "narrow")),
        P(),
        P(("wide", "narrow"), None),
        P(),
        P(),
        P(),
        P(),
        P(),
        P(),
        P(),
        P(),
        P(),
        P(),
        P(),
        P(),
        P(),
        P(),
        P(),
        P(),
        P(),
        P(),
        P(),
        P(),
        P(),
        P(),
    )
    out_specs = (
        P(("wide", "narrow"), None),
        P(None, None, ("wide", "narrow")),
        P(("wide", "narrow"), None),
        P(("wide", "narrow"), None),
        P("wide"),
        P("wide"),
        P("wide", None),
        P("wide"),
        P("wide", None),
        P("wide"),
        P("wide"),
        P("wide"),
        P("wide", None),
        P("wide"),
        P("wide", None),
        P("wide"),
        P("wide", None),
        P("wide", None),
        P("wide", None),
        P("wide", None),
        P("wide", None),
        P("wide", None),
        P("wide", None),
        P("wide", None),
        P("wide", None),
    )
    return jax.shard_map(shards, mesh=mesh, in_specs=in_specs, out_specs=out_specs, check_vma=False)
```
